256 devices in a mesh: gx: 16 (over z, core), gy: 16 (over y, x).
Axes of the slice: x: 4, y: 4, z: 8, core: 2. Of those that a mesh axis runs over, the one named last changes fastest.
Arguments:
- right_side: float32 [2, 4096, 8192], P(None, 'gy', 'gx'), may hold values from -16 to 16
- coefficient: float32 [2, 4096, 8192], P(None, 'gy', 'gx'), may hold values from 0.2 to 5
- strength_table: float32 [35], replicated, may hold values from 0.3 to 3
- layer_entry: int32 [2], replicated, may hold values from 0 to 34
- shifts: int32 [6, 2, 2], replicated, may hold values from -32 to 32, as said below
Outputs:
- solution_field: float32 [2, 4096, 8192], P(None, 'gy', 'gx')
- residual: float32 [2, 4096, 8192], P(None, 'gy', 'gx')
The draws below stay inside these ranges and needn't reach their ends.
Inputs may be any that keep to these rules, and one draw needn't show every extreme that they name: `shifts`: every entry lies in -32 to 32; both ends are reached.
All inputs are finite; a program needn't handle non-finite values.
Results may differ from the reference program's by a relative error of at most 0.0003.
Values sent between devices are 32-bit elements; how exact they have to be, the bound alone decides.
No kernel may reach another device: no remote copies, remote signals or barrier semaphores. Data moves between devices by JAX's collectives and lax.ppermute only.
A program may use at most 64 MiB of HBM per device.

```python
import math
import jax
import jax.numpy as jnp
from jax import lax

L = 2
DIRS = 6
SMAX = 32
TABLE = 35
ITERS = 2
NR = 4096
NC = 8192


def draw_right_side(key, part):
    key = jax.random.fold_in(key, 11)
    rows = jnp.arange(NR, dtype=jnp.float32) / NR
    scale = (1.0 + 2.0 * rows)[None, :, None]
    base = jnp.clip(jax.random.normal(key, (L, NR, NC), jnp.float32), -5.0, 5.0)
    values = base * scale
    return values.astype(jnp.float32)


def draw_shifts(key, part):
    key = jax.random.fold_in(key, 7)
    values = jax.random.randint(key, (DIRS, L, 2), -SMAX, SMAX + 1, jnp.int32)
    values = values.at[0, L - 1, 0].set(-SMAX)
    values = values.at[0, L - 1, 1].set(SMAX)
    return values


def steps_of(stream_key, dims, cuts, low, largest):
    level, own = 1.0, jax.random.fold_in(stream_key, 6)
    for axis_at, parts in cuts:
        draws = jnp.exp(jax.random.uniform(jax.random.fold_in(own, axis_at), (parts,), jnp.float32, low / len(cuts), largest / len(cuts)))
        level = level * jnp.repeat(draws, dims[axis_at] // parts).reshape([-1 if axis == axis_at else 1 for axis in range(len(dims))])
    return level


def setup_inputs(seed: int = 0) -> dict:
    seeds = jax.random.split(jax.random.key(seed), 6)
    right_side = draw_right_side(jax.random.fold_in(seeds[5], 71), 0)
    coefficient = jnp.clip(jnp.exp(math.log(5.0) - 3.218876 * jax.random.uniform(seeds[1], (L, NR, NC), jnp.float32) ** steps_of(seeds[1], (L, NR, NC), ((1, 16), (2, 16)), -0.2, 0.2)), 0.2, 5.0)
    strength_table = jnp.clip(jnp.exp(jax.random.uniform(seeds[2], (TABLE,), jnp.float32, math.log(0.3), math.log(3.0))), 0.3, 3.0)
    layer_entry = jax.random.randint(seeds[3], (L,), 0, TABLE).astype(jnp.int32)
    shifts = draw_shifts(jax.random.fold_in(seeds[5], 71), 0)
    return {"right_side": right_side, "coefficient": coefficient, "strength_table": strength_table, "layer_entry": layer_entry, "shifts": shifts}


def shift_field(field, rows, cols):
    padded = jnp.pad(field, SMAX)
    start_rows = (SMAX + rows).astype(jnp.int32)
    start_cols = (SMAX + cols).astype(jnp.int32)
    return lax.dynamic_slice(padded, (start_rows, start_cols), field.shape)


def prior_term(field, coefficient, weights):
    padded = jnp.pad(field, ((0, 0), (1, 1), (1, 1)))
    coeff_pad = jnp.pad(coefficient, ((0, 0), (1, 1), (1, 1)))
    return prior_from_pads(padded, coeff_pad, weights)


def prior_from_pads(padded, coeff_pad, weights):
    rows = padded.shape[1] - 2
    cols = padded.shape[2] - 2
    centre = padded[:, 1:1 + rows, 1:1 + cols]
    coeff_centre = coeff_pad[:, 1:1 + rows, 1:1 + cols]
    total = jnp.zeros_like(centre)
    for step_r, step_c in ((1, 0), (-1, 0), (0, 1), (0, -1)):
        other = padded[:, 1 + step_r:1 + step_r + rows, 1 + step_c:1 + step_c + cols]
        coeff_other = coeff_pad[:, 1 + step_r:1 + step_r + rows, 1 + step_c:1 + step_c + cols]
        total = total + 0.5 * (coeff_centre + coeff_other) * (centre - other)
    return weights[:, None, None] * total


def operate(field, coefficient, weights, shifts):
    layers = field.shape[0]
    back = [jnp.zeros(field.shape[1:], jnp.float32) for layer in range(layers)]
    for direction in range(DIRS):
        image = jnp.zeros(field.shape[1:], jnp.float32)
        for layer in range(layers):
            image = image + shift_field(field[layer], shifts[direction, layer, 0], shifts[direction, layer, 1])
        for layer in range(layers):
            back[layer] = back[layer] + shift_field(image, -shifts[direction, layer, 0], -shifts[direction, layer, 1])
    return jnp.stack(back) + prior_term(field, coefficient, weights)


def reference(right_side, coefficient, strength_table, layer_entry, shifts):
    entries = jnp.arange(TABLE, dtype=jnp.int32)
    weights = jnp.sum(jnp.where(layer_entry[:, None] == entries[None, :], strength_table[None, :], 0.0), axis=1)
    solution_field = jnp.zeros_like(right_side)
    residual = right_side
    w_vec = operate(residual, coefficient, weights, shifts)
    z_vec = jnp.zeros_like(right_side)
    s_vec = jnp.zeros_like(right_side)
    p_vec = jnp.zeros_like(right_side)
    gamma_prev = jnp.float32(1.0)
    alpha_prev = jnp.float32(1.0)
    for step in range(ITERS):
        gamma = jnp.sum(residual * residual)
        delta = jnp.sum(w_vec * residual)
        n_vec = operate(w_vec, coefficient, weights, shifts)
        if step == 0:
            beta = jnp.float32(0.0)
            alpha = gamma / delta
        else:
            beta = gamma / gamma_prev
            alpha = gamma / (delta - beta * gamma / alpha_prev)
        z_vec = n_vec + beta * z_vec
        s_vec = w_vec + beta * s_vec
        p_vec = residual + beta * p_vec
        solution_field = solution_field + alpha * p_vec
        residual = residual - alpha * s_vec
        w_vec = w_vec - alpha * z_vec
        gamma_prev = gamma
        alpha_prev = alpha
    return solution_field, residual
```

```python
import jax
import jax.numpy as jnp
from jax import lax
from jax.experimental import pallas as pl
from jax.experimental.pallas import tpu as pltpu
from jax.sharding import PartitionSpec as P

REACH = 64
LANES = 128
HALF = 64
CHUNK = 16
VMEM_BYTES = 32 * 1024 * 1024


def even_swap(count):
    return [(i, i ^ 1) for i in range(count)]


def odd_swap(count):
    return [(i, i + 1 if i % 2 else i - 1) for i in range(1, count - 1)]


def is_odd(axis):
    return lax.rem(lax.axis_index(axis), 2) == 1


def swap(even, odd, axis):
    count = lax.axis_size(axis)
    return (
        lax.ppermute(even, axis, even_swap(count)),
        lax.ppermute(odd, axis, odd_swap(count)),
    )


def lane_of(shape):
    return lax.broadcasted_iota(jnp.int32, shape, 1)


def pack_columns(first, second, high):
    low_lanes = lane_of(first.shape) < HALF
    turned = pltpu.roll(second, HALF, 1)
    if high:
        return jnp.where(low_lanes, turned, first)
    return jnp.where(low_lanes, first, turned)


def store_packed(even_ref, odd_ref, odd, start, low, high):
    rows = low.shape[0]
    even_ref[start : start + rows, :] = jnp.where(odd, low, high)
    odd_ref[start : start + rows, :] = jnp.where(odd, high, low)


def pack_kernel(with_coeff, *refs):
    if with_coeff:
        field, coeff, even_rows, odd_rows, even_out, odd_out = refs
    else:
        field, even_rows, odd_rows, even_out, odd_out = refs
    rows, cols = field.shape[1:]
    odd_x, odd_y = is_odd("gx"), is_odd("gy")
    edges = (slice(0, LANES), slice(cols - LANES, cols))

    def halo(layer, edge, before):
        even = even_rows[layer, 0:REACH, edge]
        other = odd_rows[layer, 0:REACH, edge]
        return jnp.where(odd_y == before, even, other)

    for start, part in ((0, "above"), (REACH, "own"), (REACH + rows, "below")):
        packed = []
        for high, edge in enumerate(edges):
            if part == "own":
                pair = [field[layer, :, edge] for layer in range(2)]
            else:
                pair = [halo(layer, edge, part == "above") for layer in range(2)]
            packed.append(pack_columns(pair[0], pair[1], high))
        store_packed(even_out, odd_out, odd_x, start, packed[0], packed[1])
    if with_coeff:
        packed = [
            pack_columns(coeff[0, :, edge], coeff[1, :, edge], high)
            for high, edge in enumerate(edges)
        ]
        store_packed(even_out, odd_out, odd_x, 2 * REACH + rows, packed[0], packed[1])


def pack(field, coeff, even_rows, odd_rows):
    rows = field.shape[1]
    total = rows + 2 * REACH + (0 if coeff is None else rows)
    out = jax.ShapeDtypeStruct((total, LANES), jnp.float32)
    operands = [field] + ([] if coeff is None else [coeff]) + [even_rows, odd_rows]

    def kernel(*refs):
        pack_kernel(coeff is not None, *refs)

    return pl.pallas_call(
        kernel,
        out_shape=(out, out),
        in_specs=[pl.BlockSpec(memory_space=pltpu.VMEM)] * len(operands),
        out_specs=(pl.BlockSpec(memory_space=pltpu.VMEM),) * 2,
        compiler_params=pltpu.CompilerParams(vmem_limit_bytes=VMEM_BYTES),
        name="pack_columns",
    )(*operands)


def fill_field(pad, field, even_rows, odd_rows, even_cols, odd_cols):
    rows, cols = field.shape[1:]
    odd_x, odd_y = is_odd("gx"), is_odd("gy")
    tiles = cols // LANES
    for layer in range(2):
        for tile in range(tiles):
            lanes = slice(tile * LANES, (tile + 1) * LANES)
            pad[layer, 1 + tile, REACH : REACH + rows, :] = field[layer, :, lanes]
            even = even_rows[layer, 0:REACH, lanes]
            other = odd_rows[layer, 0:REACH, lanes]
            pad[layer, 1 + tile, 0:REACH, :] = jnp.where(odd_y, even, other)
            pad[layer, 1 + tile, REACH + rows :, :] = jnp.where(odd_y, other, even)
    even = even_cols[0 : rows + 2 * REACH, :]
    other = odd_cols[0 : rows + 2 * REACH, :]
    for tile, packed in (
        (0, jnp.where(odd_x, even, other)),
        (1 + tiles, jnp.where(odd_x, other, even)),
    ):
        pad[0, tile] = packed
        pad[1, tile] = pltpu.roll(packed, HALF, 1)


def fill_coeff(pad, coeff, even_rows, odd_rows, even_cols, odd_cols):
    rows, cols = coeff.shape[1:]
    odd_x, odd_y = is_odd("gx"), is_odd("gy")
    tiles = cols // LANES
    for layer in range(2):
        for tile in range(tiles):
            lanes = slice(tile * LANES, (tile + 1) * LANES)
            pad[layer, 1 + tile, 8 : 8 + rows, :] = coeff[layer, :, lanes]
            even = even_rows[layer, REACH : REACH + 8, lanes]
            other = odd_rows[layer, REACH : REACH + 8, lanes]
            pad[layer, 1 + tile, 0:8, :] = jnp.where(odd_y, even, other)
            pad[layer, 1 + tile, 8 + rows :, :] = jnp.where(odd_y, other, even)
    start = rows + 2 * REACH
    even = even_cols[start : start + rows, :]
    other = odd_cols[start : start + rows, :]
    for tile, packed in (
        (0, jnp.where(odd_x, even, other)),
        (1 + tiles, jnp.where(odd_x, other, even)),
    ):
        pad[0, tile, 8 : 8 + rows, :] = packed
        pad[1, tile, 8 : 8 + rows, :] = pltpu.roll(packed, HALF, 1)


def neighbours_across(load, tiles):
    lane = lane_of((CHUNK, LANES))
    values = [load(tile) for tile in range(tiles + 2)]
    back = [pltpu.roll(value, 1, 1) for value in values[:-1]]
    ahead = [pltpu.roll(value, LANES - 1, 1) for value in values[1:]]
    left = [jnp.where(lane == 0, back[i], back[i + 1]) for i in range(tiles)]
    right = [jnp.where(lane == LANES - 1, ahead[i + 1], ahead[i]) for i in range(tiles)]
    return values[1:-1], left, right


def apply_chunk(layer, row, pad, coeff_pad, shifts, weight, field_rows, grid_shape, tile_shape):
    dirs = shifts.shape[0]
    rows, cols = tile_shape
    tiles = cols // LANES
    other = 1 - layer
    lane = lane_of((CHUNK, LANES))
    row_at = lax.broadcasted_iota(jnp.int32, (CHUNK, LANES), 0)
    first_row = lax.axis_index("gy") * rows + row
    first_col = lax.axis_index("gx") * cols

    def field_at(tile):
        return pad[layer, tile, pl.ds(REACH + row, CHUNK), :]

    def coeff_at(tile):
        return coeff_pad[layer, tile, pl.ds(8 + row, CHUNK), :]

    own, left, right = neighbours_across(field_at, tiles)
    own_c, left_c, right_c = neighbours_across(coeff_at, tiles)
    result = []
    for tile in range(tiles):
        value, coeff = own[tile], own_c[tile]
        above = pad[layer, 1 + tile, pl.ds(REACH - 1 + row, CHUNK), :]
        below = pad[layer, 1 + tile, pl.ds(REACH + 1 + row, CHUNK), :]
        above_c = coeff_pad[layer, 1 + tile, pl.ds(7 + row, CHUNK), :]
        below_c = coeff_pad[layer, 1 + tile, pl.ds(9 + row, CHUNK), :]
        total = (coeff + above_c) * (value - above) + (coeff + below_c) * (value - below)
        total += (coeff + left_c[tile]) * (value - left[tile])
        total += (coeff + right_c[tile]) * (value - right[tile])
        result.append(weight * total)
    for direction in range(dirs):
        shift_r, shift_c = shifts[direction, layer, 0], shifts[direction, layer, 1]
        start_r = REACH + row + shifts[direction, other, 0] - shift_r
        start_c = LANES + shifts[direction, other, 1] - shift_c
        skip = lax.shift_right_logical(start_c, 7)
        turn = jnp.bitwise_and(start_c, LANES - 1)
        back = jnp.bitwise_and(LANES - turn, LANES - 1)
        moved = [
            pltpu.roll(pad[other, skip + tile, pl.ds(start_r, CHUNK), :], back, 1)
            for tile in range(tiles + 1)
        ]
        here = lane < LANES - turn
        image_row = row_at + (first_row - shift_r)
        inside = (image_row >= 0) & (image_row < grid_shape[0])
        for tile in range(tiles):
            mask = inside
            if tile == 0:
                mask = mask & (lane >= shift_c - first_col)
            if tile == tiles - 1:
                mask = mask & (lane < grid_shape[1] + shift_c - first_col - tile * LANES)
            value = own[tile] + jnp.where(here, moved[tile], moved[tile + 1])
            result[tile] = result[tile] + jnp.where(mask, value, 0.0)
    return own, result


def fold(parts):
    total = sum(parts[1:], parts[0])
    pieces = [total[8 * i : 8 * i + 8] for i in range(CHUNK // 8)]
    return sum(pieces[1:], pieces[0])


def dot_of(first, second):
    return fold([a * b for a, b in zip(first, second, strict=True)])


def weight_of(table, entry, layer):
    return 0.5 * table[entry[layer]]


def first_kernel(
    grid_shape, field, coeff, even_rows, odd_rows, even_cols, odd_cols, shifts, table, entry,
    out, sums, even_out, odd_out, pad, coeff_pad,
):
    rows, cols = field.shape[1:]
    fill_field(pad, field, even_rows, odd_rows, even_cols, odd_cols)
    fill_coeff(coeff_pad, coeff, even_rows, odd_rows, even_cols, odd_cols)
    carry = (jnp.zeros((8, LANES), jnp.float32),) * 3
    for layer in range(2):
        weight = weight_of(table, entry, layer)

        def step(i, carry, layer=layer, weight=weight):
            row = pl.multiple_of(i * CHUNK, CHUNK)
            own, result = apply_chunk(
                layer, row, pad, coeff_pad, shifts, weight, field, grid_shape, (rows, cols)
            )
            for tile, value in enumerate(result):
                out[layer, pl.ds(row, CHUNK), tile * LANES : (tile + 1) * LANES] = value
            pairs = ((own, own), (own, result), (result, result))
            return tuple(c + dot_of(*p) for c, p in zip(carry, pairs, strict=True))

        carry = lax.fori_loop(0, rows // CHUNK, step, carry)
    for index, value in enumerate(carry):
        sums[index] = value
    odd_y = is_odd("gy")
    low, high = out[:, 0:REACH, :], out[:, rows - REACH :, :]
    even_out[...] = jnp.where(odd_y, low, high)
    odd_out[...] = jnp.where(odd_y, high, low)


def second_kernel(
    grid_shape, base, field, coeff, even_rows, odd_rows, even_cols, odd_cols, even_edge, odd_edge,
    even_side, odd_side, sums, shifts, table, entry, out, parts, pad, coeff_pad,
):
    rows, cols = field.shape[1:]
    fill_field(pad, field, even_rows, odd_rows, even_cols, odd_cols)
    fill_coeff(coeff_pad, coeff, even_edge, odd_edge, even_side, odd_side)
    gamma, delta, omega = (jnp.sum(sums[index], keepdims=True) for index in range(3))
    fit = jnp.where(omega > 0.0, delta / jnp.where(omega > 0.0, omega, 1.0), 0.0)
    fit = jnp.clip(fit, -1.0, 1.0)
    carry = (jnp.zeros((8, LANES), jnp.float32),) * 6
    for layer in range(2):
        weight = weight_of(table, entry, layer)

        def step(i, carry, layer=layer, weight=weight):
            row = pl.multiple_of(i * CHUNK, CHUNK)
            own, result = apply_chunk(
                layer, row, pad, coeff_pad, shifts, weight, field, grid_shape, (rows, cols)
            )
            rest, slope = [], []
            for tile, value in enumerate(result):
                lanes = slice(tile * LANES, (tile + 1) * LANES)
                out[layer, pl.ds(row, CHUNK), lanes] = value
                rest.append(base[layer, pl.ds(row, CHUNK), lanes] - fit * own[tile])
                slope.append(own[tile] - fit * value)
            pairs = (
                (rest, rest), (rest, own), (slope, rest), (result, rest), (slope, own), (result, own),
            )
            return tuple(c + dot_of(*p) for c, p in zip(carry, pairs, strict=True))

        carry = lax.fori_loop(0, rows // CHUNK, step, carry)
    rest2, rest_w, slope_rest, n_rest, slope_w, n_w = (
        jnp.sum(value, keepdims=True) for value in carry
    )
    lane = lane_of((8, LANES))
    row = jnp.zeros((8, LANES), jnp.float32)
    for at, value in (
        (0, rest2), (1, slope_rest), (8, 2.0 * rest_w), (9, n_rest + slope_w),
        (16, omega), (17, n_w), (24, fit), (25, fit), (32, gamma), (33, delta),
    ):
        row = jnp.where(lane == at, value, row)
    for start in range(0, parts.shape[0], 8):
        parts[start : start + 8, :] = row


def pick(row, lane, at):
    return jnp.sum(jnp.where(lane == at, row, 0.0), keepdims=True)


def last_kernel(parts, base, w_vec, n_vec, solution_out, residual_out):
    gathered = parts[...]
    count = gathered.shape[0]
    lane = lane_of((8, LANES))
    total = sum(gathered[8 * i : 8 * i + 8] for i in range(count // 8))
    gamma, delta = pick(total, lane, 32), pick(total, lane, 33)
    alpha = gamma / delta
    gap = alpha - pltpu.roll(gathered, LANES - 24, 1)
    moved = gathered - gap * pltpu.roll(gathered, LANES - 8, 1)
    moved = moved + gap * gap * pltpu.roll(gathered, LANES - 16, 1)
    total = sum(moved[8 * i : 8 * i + 8] for i in range(count // 8))
    gamma_next, delta_next = pick(total, lane, 0), pick(total, lane, 1)
    beta = gamma_next / gamma
    alpha_next = gamma_next / (delta_next - beta * gamma_next / alpha)
    for layer in range(base.shape[0]):
        start, w_start = base[layer], w_vec[layer]
        residual = start - alpha * w_start
        w_next = w_start - alpha * n_vec[layer]
        solution_out[layer] = alpha * start + alpha_next * (residual + beta * start)
        residual_out[layer] = residual - alpha_next * (w_next + beta * w_start)


VMEM_SPEC = pl.BlockSpec(memory_space=pltpu.VMEM)
SMEM_SPEC = pl.BlockSpec(memory_space=pltpu.SMEM)


def pads(rows, cols):
    tiles = cols // LANES + 2
    return [
        pltpu.VMEM((2, tiles, rows + 2 * REACH, LANES), jnp.float32),
        pltpu.VMEM((2, tiles, rows + 16, LANES), jnp.float32),
    ]


def on_device(right_side, coefficient, strength_table, layer_entry, shifts):
    layers, rows, cols = right_side.shape
    count_y, count_x = lax.axis_size("gy"), lax.axis_size("gx")
    devices = count_x * count_y
    grid_shape = (rows * count_y, cols * count_x)
    params = pltpu.CompilerParams(vmem_limit_bytes=VMEM_BYTES)
    full = jax.ShapeDtypeStruct((layers, rows, cols), jnp.float32)
    edge = jax.ShapeDtypeStruct((layers, REACH, cols), jnp.float32)
    odd_y = is_odd("gy")
    low = jnp.concatenate([right_side[:, :REACH], coefficient[:, :8]], axis=1)
    high = jnp.concatenate([right_side[:, rows - REACH :], coefficient[:, rows - 8 :]], axis=1)
    rows0 = swap(jnp.where(odd_y, low, high), jnp.where(odd_y, high, low), "gy")
    cols0 = swap(*pack(right_side, coefficient, *rows0), "gx")
    scalars = (shifts, strength_table, layer_entry)

    def first(*refs):
        first_kernel(grid_shape, *refs)

    w_vec, sums, even, odd = pl.pallas_call(
        first,
        out_shape=(full, jax.ShapeDtypeStruct((3, 8, LANES), jnp.float32), edge, edge),
        in_specs=[VMEM_SPEC] * 6 + [SMEM_SPEC] * 3,
        out_specs=(VMEM_SPEC,) * 4,
        scratch_shapes=pads(rows, cols),
        compiler_params=params,
        name="first_apply",
    )(right_side, coefficient, *rows0, *cols0, *scalars)
    rows1 = swap(even, odd, "gy")
    cols1 = swap(*pack(w_vec, None, *rows1), "gx")

    def second(*refs):
        second_kernel(grid_shape, *refs)

    n_vec, parts = pl.pallas_call(
        second,
        out_shape=(full, jax.ShapeDtypeStruct((devices, LANES), jnp.float32)),
        in_specs=[VMEM_SPEC] * 12 + [SMEM_SPEC] * 3,
        out_specs=(VMEM_SPEC,) * 2,
        scratch_shapes=pads(rows, cols),
        compiler_params=params,
        name="second_apply",
    )(right_side, w_vec, coefficient, *rows1, *cols1, *rows0, *cols0, sums, *scalars)
    gathered = lax.all_to_all(parts, ("gx", "gy"), 0, 0, tiled=True)
    steps = 4
    block = pl.BlockSpec((layers, rows // steps, cols), lambda i: (0, i, 0))
    return pl.pallas_call(
        last_kernel,
        grid=(steps,),
        out_shape=(full, full),
        in_specs=[pl.BlockSpec((devices, LANES), lambda i: (0, 0))] + [block] * 3,
        out_specs=(block, block),
        compiler_params=params,
        name="last_update",
    )(gathered, right_side, w_vec, n_vec)


def solution(mesh):
    placed = (P(None, "gy", "gx"), P(None, "gy", "gx"), P(), P(), P())
    return jax.shard_map(
        on_device,
        mesh=mesh,
        in_specs=placed,
        out_specs=(P(None, "gy", "gx"), P(None, "gy", "gx")),
        check_vma=False,
    )
```

```python
import jax
import jax.numpy as jnp
from jax import lax
from jax.experimental import pallas as pl
from jax.experimental.pallas import tpu as pltpu
from jax.sharding import PartitionSpec as P

REACH = 64
LANES = 128
HALF = 64
CHUNK = 32
VMEM_BYTES = 32 * 1024 * 1024


def even_swap(count):
    return [(i, i ^ 1) for i in range(count)]


def odd_swap(count):
    return [(i, i + 1 if i % 2 else i - 1) for i in range(1, count - 1)]


def is_odd(axis):
    return lax.rem(lax.axis_index(axis), 2) == 1


def swap(even, odd, axis):
    count = lax.axis_size(axis)
    return (
        lax.ppermute(even, axis, even_swap(count)),
        lax.ppermute(odd, axis, odd_swap(count)),
    )


def lane_of(shape):
    return lax.broadcasted_iota(jnp.int32, shape, 1)


def pack_columns(first, second, high):
    low_lanes = lane_of(first.shape) < HALF
    turned = pltpu.roll(second, HALF, 1)
    if high:
        return jnp.where(low_lanes, turned, first)
    return jnp.where(low_lanes, first, turned)


def store_packed(even_ref, odd_ref, odd, start, low, high):
    rows = low.shape[0]
    even_ref[start : start + rows, :] = jnp.where(odd, low, high)
    odd_ref[start : start + rows, :] = jnp.where(odd, high, low)


def pack_kernel(with_coeff, *refs):
    if with_coeff:
        field, coeff, even_rows, odd_rows, even_out, odd_out = refs
    else:
        field, even_rows, odd_rows, even_out, odd_out = refs
    rows, cols = field.shape[1:]
    odd_x, odd_y = is_odd("gx"), is_odd("gy")
    edges = (slice(0, LANES), slice(cols - LANES, cols))

    def halo(layer, edge, before):
        even = even_rows[layer, 0:REACH, edge]
        other = odd_rows[layer, 0:REACH, edge]
        return jnp.where(odd_y == before, even, other)

    for start, part in ((0, "above"), (REACH, "own"), (REACH + rows, "below")):
        packed = []
        for high, edge in enumerate(edges):
            if part == "own":
                pair = [field[layer, :, edge] for layer in range(2)]
            else:
                pair = [halo(layer, edge, part == "above") for layer in range(2)]
            packed.append(pack_columns(pair[0], pair[1], high))
        store_packed(even_out, odd_out, odd_x, start, packed[0], packed[1])
    if with_coeff:
        packed = [
            pack_columns(coeff[0, :, edge], coeff[1, :, edge], high)
            for high, edge in enumerate(edges)
        ]
        store_packed(even_out, odd_out, odd_x, 2 * REACH + rows, packed[0], packed[1])


def pack(field, coeff, even_rows, odd_rows, after):
    rows = field.shape[1]
    total = rows + 2 * REACH + (0 if coeff is None else rows)
    out = jax.ShapeDtypeStruct((total, LANES), jnp.float32)
    operands = [after, field] + ([] if coeff is None else [coeff]) + [even_rows, odd_rows]

    def kernel(unused, *refs):
        del unused
        pack_kernel(coeff is not None, *refs)

    return pl.pallas_call(
        kernel,
        out_shape=(out, out),
        in_specs=[pl.BlockSpec(memory_space=pltpu.VMEM)] * len(operands),
        out_specs=(pl.BlockSpec(memory_space=pltpu.VMEM),) * 2,
        compiler_params=pltpu.CompilerParams(vmem_limit_bytes=VMEM_BYTES),
        name="pack_columns",
    )(*operands)


def zero_rim(pad, depth, rows):
    tiles = pad.shape[1]
    for layer in range(2):
        for tile in range(tiles):
            if tile in (0, tiles - 1):
                pad[layer, tile] = jnp.zeros(pad.shape[2:], jnp.float32)
            else:
                pad[layer, tile, 0:depth, :] = jnp.zeros((depth, LANES), jnp.float32)
                pad[layer, tile, depth + rows :, :] = jnp.zeros((depth, LANES), jnp.float32)


def fill_own(pad, depth, field):
    rows, cols = field.shape[1:]
    for layer in range(2):
        for tile in range(cols // LANES):
            lanes = slice(tile * LANES, (tile + 1) * LANES)
            pad[layer, 1 + tile, depth : depth + rows, :] = field[layer, :, lanes]


def neighbours_across(load, tiles):
    lane = lane_of((CHUNK, LANES))
    values = [load(tile) for tile in range(tiles + 2)]
    back = [pltpu.roll(value, 1, 1) for value in values[:-1]]
    ahead = [pltpu.roll(value, LANES - 1, 1) for value in values[1:]]
    left = [jnp.where(lane == 0, back[i], back[i + 1]) for i in range(tiles)]
    right = [jnp.where(lane == LANES - 1, ahead[i + 1], ahead[i]) for i in range(tiles)]
    return values[1:-1], left, right


def apply_chunk(layer, row, pad, coeff_pad, shifts, weight, grid_shape, tile_shape):
    dirs = shifts.shape[0]
    rows, cols = tile_shape
    tiles = cols // LANES
    other = 1 - layer
    lane = lane_of((CHUNK, LANES))
    row_at = lax.broadcasted_iota(jnp.int32, (CHUNK, LANES), 0)
    first_row = lax.axis_index("gy") * rows + row
    first_col = lax.axis_index("gx") * cols

    def field_at(tile):
        return pad[layer, tile, pl.ds(REACH + row, CHUNK), :]

    def coeff_at(tile):
        return coeff_pad[layer, tile, pl.ds(8 + row, CHUNK), :]

    own, left, right = neighbours_across(field_at, tiles)
    own_c, left_c, right_c = neighbours_across(coeff_at, tiles)
    result = []
    for tile in range(tiles):
        value, coeff = own[tile], own_c[tile]
        above = pad[layer, 1 + tile, pl.ds(REACH - 1 + row, CHUNK), :]
        below = pad[layer, 1 + tile, pl.ds(REACH + 1 + row, CHUNK), :]
        above_c = coeff_pad[layer, 1 + tile, pl.ds(7 + row, CHUNK), :]
        below_c = coeff_pad[layer, 1 + tile, pl.ds(9 + row, CHUNK), :]
        total = (coeff + above_c) * (value - above) + (coeff + below_c) * (value - below)
        total += (coeff + left_c[tile]) * (value - left[tile])
        total += (coeff + right_c[tile]) * (value - right[tile])
        result.append(weight * total)
    for direction in range(dirs):
        shift_r, shift_c = shifts[direction, layer, 0], shifts[direction, layer, 1]
        start_r = REACH + row + shifts[direction, other, 0] - shift_r
        start_c = LANES + shifts[direction, other, 1] - shift_c
        skip = lax.shift_right_logical(start_c, 7)
        turn = jnp.bitwise_and(start_c, LANES - 1)
        back = jnp.bitwise_and(LANES - turn, LANES - 1)
        moved = [
            pltpu.roll(pad[other, skip + tile, pl.ds(start_r, CHUNK), :], back, 1)
            for tile in range(tiles + 1)
        ]
        here = lane < LANES - turn
        image_row = row_at + (first_row - shift_r)
        inside = (image_row >= 0) & (image_row < grid_shape[0])
        for tile in range(tiles):
            mask = inside
            if tile == 0:
                mask = mask & (lane >= shift_c - first_col)
            if tile == tiles - 1:
                mask = mask & (lane < grid_shape[1] + shift_c - first_col - tile * LANES)
            value = own[tile] + jnp.where(here, moved[tile], moved[tile + 1])
            result[tile] = result[tile] + jnp.where(mask, value, 0.0)
    return result


def fold(parts):
    total = sum(parts[1:], parts[0])
    pieces = [total[8 * i : 8 * i + 8] for i in range(total.shape[0] // 8)]
    return sum(pieces[1:], pieces[0])


def dot_of(first, second):
    return fold([a * b for a, b in zip(first, second, strict=True)])


def weight_of(table, entry, layer):
    return 0.5 * table[entry[layer]]


def own_kernel(grid_shape, field, coeff, shifts, table, entry, out, pad, coeff_pad):
    rows, cols = field.shape[1:]
    zero_rim(pad, REACH, rows)
    zero_rim(coeff_pad, 8, rows)
    fill_own(pad, REACH, field)
    fill_own(coeff_pad, 8, coeff)
    for layer in range(2):
        weight = weight_of(table, entry, layer)

        def step(i, carry, layer=layer, weight=weight):
            row = pl.multiple_of(i * CHUNK, CHUNK)
            result = apply_chunk(
                layer, row, pad, coeff_pad, shifts, weight, grid_shape, (rows, cols)
            )
            for tile, value in enumerate(result):
                out[layer, pl.ds(row, CHUNK), tile * LANES : (tile + 1) * LANES] = value
            return carry

        lax.fori_loop(0, rows // CHUNK, step, 0)


def rows_kernel(
    grid_shape, before, field, coeff, even_rows, odd_rows, even_edge, odd_edge, packed, shifts,
    table, entry, out, pad,
):
    del packed
    rows, cols = field.shape[1:]
    tiles = cols // LANES
    odd_y = is_odd("gy")
    first_row = lax.axis_index("gy") * rows
    first_col = lax.axis_index("gx") * cols
    zeros = jnp.zeros((REACH, LANES), jnp.float32)
    for layer in range(2):
        for side in range(2):
            for tile in (0, tiles + 1):
                pad[layer, side, tile, 0:REACH, :] = zeros
                pad[layer, side, tile, REACH:, :] = zeros
        for tile in range(tiles):
            lanes = slice(tile * LANES, (tile + 1) * LANES)
            even = even_rows[layer, 0:REACH, lanes]
            other = odd_rows[layer, 0:REACH, lanes]
            pad[layer, 0, 1 + tile, 0:REACH, :] = jnp.where(odd_y, even, other)
            pad[layer, 0, 1 + tile, REACH:, :] = zeros
            pad[layer, 1, 1 + tile, 0:REACH, :] = zeros
            pad[layer, 1, 1 + tile, REACH:, :] = jnp.where(odd_y, other, even)
    out[...] = before[...]
    lane = lane_of((CHUNK, LANES))
    row_at = lax.broadcasted_iota(jnp.int32, (CHUNK, LANES), 0)
    for layer in range(2):
        other_layer = 1 - layer

        def step(i, carry, layer=layer, other_layer=other_layer):
            part = pl.multiple_of(i * CHUNK, CHUNK)
            totals = [[jnp.zeros((CHUNK, LANES), jnp.float32)] * tiles for _ in range(2)]
            for direction in range(shifts.shape[0]):
                shift_r, shift_c = shifts[direction, layer, 0], shifts[direction, layer, 1]
                step_r = shifts[direction, other_layer, 0] - shift_r
                start_c = LANES + shifts[direction, other_layer, 1] - shift_c
                side = jnp.where(step_r < 0, 0, 1)
                start_r = part + step_r + jnp.where(step_r < 0, REACH, 0)
                row = part + jnp.where(step_r < 0, 0, rows - REACH)
                skip = lax.shift_right_logical(start_c, 7)
                turn = jnp.bitwise_and(start_c, LANES - 1)
                back = jnp.bitwise_and(LANES - turn, LANES - 1)
                moved = [
                    pltpu.roll(
                        pad[other_layer, side, skip + tile, pl.ds(start_r, CHUNK), :], back, 1
                    )
                    for tile in range(tiles + 1)
                ]
                here = lane < LANES - turn
                image_row = row_at + (first_row + row - shift_r)
                inside = (image_row >= 0) & (image_row < grid_shape[0])
                upper = inside & (jnp.full((CHUNK, LANES), side, jnp.int32) == 0)
                lower = inside & (jnp.full((CHUNK, LANES), side, jnp.int32) == 1)
                for tile in range(tiles):
                    value = jnp.where(here, moved[tile], moved[tile + 1])
                    if tile == 0:
                        value = jnp.where(lane >= shift_c - first_col, value, 0.0)
                    if tile == tiles - 1:
                        last = grid_shape[1] + shift_c - first_col - tile * LANES
                        value = jnp.where(lane < last, value, 0.0)
                    totals[0][tile] = totals[0][tile] + jnp.where(upper, value, 0.0)
                    totals[1][tile] = totals[1][tile] + jnp.where(lower, value, 0.0)
            for side, base in enumerate((0, rows - REACH)):
                for tile in range(tiles):
                    lanes = slice(tile * LANES, (tile + 1) * LANES)
                    out[layer, pl.ds(base + part, CHUNK), lanes] += totals[side][tile]
            return carry

        lax.fori_loop(0, REACH // CHUNK, step, 0)
        weight = weight_of(table, entry, layer)
        at = lax.broadcasted_iota(jnp.int32, (8, cols), 0)
        even = even_edge[layer, REACH : REACH + 8, :]
        other = odd_edge[layer, REACH : REACH + 8, :]
        even_v = [even_rows[layer, start : start + 8, :] for start in (0, REACH - 8)]
        other_v = [odd_rows[layer, start : start + 8, :] for start in (0, REACH - 8)]
        for start, edge_c, edge_v, spot, source in (
            (0, jnp.where(odd_y, even, other), jnp.where(odd_y, even_v[1], other_v[1]), 0, 1),
            (
                rows - 8, jnp.where(odd_y, other, even), jnp.where(odd_y, other_v[0], even_v[0]),
                7, 7,
            ),
        ):
            edge_c = pltpu.roll(edge_c, source, 0)
            edge_v = pltpu.roll(edge_v, source, 0)
            value = field[layer, start : start + 8, :]
            own_c = coeff[layer, start : start + 8, :]
            extra = weight * (edge_c * value - (own_c + edge_c) * edge_v)
            out[layer, start : start + 8, :] += jnp.where(at == spot, extra, 0.0)


def finish_chunk(
    grid_shape, layer, row, before, field, coeff, pad, coeff_pad, shifts, weight, odd_x,
):
    rows, cols = field.shape[1:]
    tiles = cols // LANES
    first_row = lax.axis_index("gy") * rows + row
    first_col = lax.axis_index("gx") * cols
    lane = lane_of((CHUNK, LANES))
    row_at = lax.broadcasted_iota(jnp.int32, (CHUNK, LANES), 0)
    cut = [slice(tile * LANES, (tile + 1) * LANES) for tile in range(tiles)]
    own = [field[layer, pl.ds(row, CHUNK), lanes] for lanes in cut]
    result = [before[layer, pl.ds(row, CHUNK), lanes] for lanes in cut]
    ends = []
    for tile, side, turn, spot in ((0, 0, 1, 0), (tiles - 1, 1, LANES - 1, LANES - 1)):
        edge_v = pltpu.roll(pad[layer, side, pl.ds(REACH + row, CHUNK), :], turn, 1)
        edge_c = pltpu.roll(coeff_pad[layer, side, pl.ds(row, CHUNK), :], turn, 1)
        own_c = coeff[layer, pl.ds(row, CHUNK), cut[tile]]
        extra = weight * (edge_c * own[tile] - (own_c + edge_c) * edge_v)
        ends.append(result[tile] + jnp.where(lane == spot, extra, 0.0))
    for direction in range(shifts.shape[0]):
        shift_r, shift_c = shifts[direction, layer, 0], shifts[direction, layer, 1]
        start_r = REACH + row + shifts[direction, 1 - layer, 0] - shift_r
        step_c = shifts[direction, 1 - layer, 1] - shift_c
        side = jnp.where(step_c < 0, 0, 1)
        back = jnp.bitwise_and(LANES - step_c, LANES - 1)
        moved = pltpu.roll(pad[1 - layer, side, pl.ds(start_r, CHUNK), :], back, 1)
        image_row = row_at + (first_row - shift_r)
        moved = jnp.where((image_row >= 0) & (image_row < grid_shape[0]), moved, 0.0)
        low, low_end = shift_c - first_col, jnp.where(step_c < 0, -step_c, 0)
        high = jnp.where(step_c < 0, LANES, LANES - step_c)
        high_end = grid_shape[1] + shift_c - first_col - (tiles - 1) * LANES
        ends[0] = ends[0] + jnp.where((lane >= low) & (lane < low_end), moved, 0.0)
        ends[1] = ends[1] + jnp.where((lane >= high) & (lane < high_end), moved, 0.0)
    return own, [ends[0]] + result[1:-1] + [ends[1]]


def fill_sides(pad, coeff_pad, rows, even_cols, odd_cols, even_side, odd_side):
    odd_x = is_odd("gx")
    depth = rows + 2 * REACH
    for target, even, other in (
        (pad, even_cols[0:depth, :], odd_cols[0:depth, :]),
        (coeff_pad, even_side[depth : depth + rows, :], odd_side[depth : depth + rows, :]),
    ):
        for side, packed in ((0, jnp.where(odd_x, even, other)), (1, jnp.where(odd_x, other, even))):
            target[0, side] = packed
            target[1, side] = pltpu.roll(packed, HALF, 1)


def first_kernel(
    grid_shape, before, field, coeff, even_cols, odd_cols, shifts, table, entry,
    out, sums, even_out, odd_out, pad, coeff_pad,
):
    rows, cols = field.shape[1:]
    fill_sides(pad, coeff_pad, rows, even_cols, odd_cols, even_cols, odd_cols)
    odd_x = is_odd("gx")
    carry = (jnp.zeros((8, LANES), jnp.float32),) * 3
    for layer in range(2):
        weight = weight_of(table, entry, layer)

        def step(i, carry, layer=layer, weight=weight):
            row = pl.multiple_of(i * CHUNK, CHUNK)
            own, result = finish_chunk(
                grid_shape, layer, row, before, field, coeff, pad, coeff_pad, shifts, weight, odd_x,
            )
            for tile, value in enumerate(result):
                out[layer, pl.ds(row, CHUNK), tile * LANES : (tile + 1) * LANES] = value
            pairs = ((own, own), (own, result), (result, result))
            return tuple(c + dot_of(*p) for c, p in zip(carry, pairs, strict=True))

        carry = lax.fori_loop(0, rows // CHUNK, step, carry)
    for index, value in enumerate(carry):
        sums[index] = value
    odd_y = is_odd("gy")
    low, high = out[:, 0:REACH, :], out[:, rows - REACH :, :]
    even_out[...] = jnp.where(odd_y, low, high)
    odd_out[...] = jnp.where(odd_y, high, low)


def second_kernel(
    grid_shape, base, before, field, coeff, even_cols, odd_cols, even_side, odd_side, sums, shifts,
    table, entry, out, parts, pad, coeff_pad,
):
    rows, cols = field.shape[1:]
    fill_sides(pad, coeff_pad, rows, even_cols, odd_cols, even_side, odd_side)
    odd_x = is_odd("gx")
    gamma, delta, omega = (jnp.sum(sums[index], keepdims=True) for index in range(3))
    fit = jnp.where(omega > 0.0, delta / jnp.where(omega > 0.0, omega, 1.0), 0.0)
    fit = jnp.clip(fit, -1.0, 1.0)
    carry = (jnp.zeros((8, LANES), jnp.float32),) * 6
    for layer in range(2):
        weight = weight_of(table, entry, layer)

        def step(i, carry, layer=layer, weight=weight):
            row = pl.multiple_of(i * CHUNK, CHUNK)
            own, result = finish_chunk(
                grid_shape, layer, row, before, field, coeff, pad, coeff_pad, shifts, weight, odd_x,
            )
            rest, slope = [], []
            for tile, value in enumerate(result):
                lanes = slice(tile * LANES, (tile + 1) * LANES)
                out[layer, pl.ds(row, CHUNK), lanes] = value
                rest.append(base[layer, pl.ds(row, CHUNK), lanes] - fit * own[tile])
                slope.append(own[tile] - fit * value)
            pairs = (
                (rest, rest), (rest, own), (slope, rest), (result, rest), (slope, own), (result, own),
            )
            return tuple(c + dot_of(*p) for c, p in zip(carry, pairs, strict=True))

        carry = lax.fori_loop(0, rows // CHUNK, step, carry)
    rest2, rest_w, slope_rest, n_rest, slope_w, n_w = (
        jnp.sum(value, keepdims=True) for value in carry
    )
    lane = lane_of((8, LANES))
    row = jnp.zeros((8, LANES), jnp.float32)
    for at, value in (
        (0, rest2), (1, slope_rest), (8, 2.0 * rest_w), (9, n_rest + slope_w),
        (16, omega), (17, n_w), (24, fit), (25, fit), (32, gamma), (33, delta),
    ):
        row = jnp.where(lane == at, value, row)
    for start in range(0, parts.shape[0], 8):
        parts[start : start + 8, :] = row


def pick(row, lane, at):
    return jnp.sum(jnp.where(lane == at, row, 0.0), keepdims=True)


def last_kernel(parts, base, w_vec, n_vec, solution_out, residual_out):
    gathered = parts[...]
    count = gathered.shape[0]
    lane = lane_of((8, LANES))
    total = sum(gathered[8 * i : 8 * i + 8] for i in range(count // 8))
    gamma, delta = pick(total, lane, 32), pick(total, lane, 33)
    alpha = gamma / delta
    gap = alpha - pltpu.roll(gathered, LANES - 24, 1)
    moved = gathered - gap * pltpu.roll(gathered, LANES - 8, 1)
    moved = moved + gap * gap * pltpu.roll(gathered, LANES - 16, 1)
    total = sum(moved[8 * i : 8 * i + 8] for i in range(count // 8))
    gamma_next, delta_next = pick(total, lane, 0), pick(total, lane, 1)
    beta = gamma_next / gamma
    alpha_next = gamma_next / (delta_next - beta * gamma_next / alpha)
    for layer in range(base.shape[0]):
        start, w_start = base[layer], w_vec[layer]
        residual = start - alpha * w_start
        w_next = w_start - alpha * n_vec[layer]
        solution_out[layer] = alpha * start + alpha_next * (residual + beta * start)
        residual_out[layer] = residual - alpha_next * (w_next + beta * w_start)


VMEM_SPEC = pl.BlockSpec(memory_space=pltpu.VMEM)
SMEM_SPEC = pl.BlockSpec(memory_space=pltpu.SMEM)


def on_tensor_core(kernel, name, operands, scalars, out_shape, scratch, microseconds):
    many = isinstance(out_shape, tuple)
    return pl.pallas_call(
        kernel,
        out_shape=out_shape,
        in_specs=[VMEM_SPEC] * len(operands) + [SMEM_SPEC] * len(scalars),
        out_specs=(VMEM_SPEC,) * len(out_shape) if many else VMEM_SPEC,
        scratch_shapes=[pltpu.VMEM(shape, jnp.float32) for shape in scratch],
        compiler_params=pltpu.CompilerParams(vmem_limit_bytes=VMEM_BYTES),
        cost_estimate=pl.CostEstimate(
            flops=0, bytes_accessed=3_000_000 * microseconds, transcendentals=0
        ),
        name=name,
    )(*operands, *scalars)


def on_device(right_side, coefficient, strength_table, layer_entry, shifts):
    layers, rows, cols = right_side.shape
    count_y, count_x = lax.axis_size("gy"), lax.axis_size("gx")
    devices = count_x * count_y
    tiles = cols // LANES
    grid_shape = (rows * count_y, cols * count_x)
    params = pltpu.CompilerParams(vmem_limit_bytes=VMEM_BYTES)
    full = jax.ShapeDtypeStruct((layers, rows, cols), jnp.float32)
    edge = jax.ShapeDtypeStruct((layers, REACH, cols), jnp.float32)
    scalars = (shifts, strength_table, layer_entry)
    sides = [(2, 2, rows + 2 * REACH, LANES), (2, 2, rows, LANES)]

    def bind(kernel):
        def bound(*refs):
            kernel(grid_shape, *refs)

        return bound

    def own_part(field):
        return on_tensor_core(
            bind(own_kernel), "own_part", (field, coefficient), scalars, full,
            [(2, tiles + 2, rows + 2 * REACH, LANES), (2, tiles + 2, rows + 16, LANES)], 6,
        )

    def rows_part(before, field, around, edges, packed):
        return on_tensor_core(
            bind(rows_kernel), "rows_part", (before, field, coefficient, *around, *edges, packed),
            scalars, full, [(2, 2, tiles + 2, 2 * REACH, LANES)], 3,
        )

    odd_y = is_odd("gy")
    low = jnp.concatenate([right_side[:, :REACH], coefficient[:, :8]], axis=1)
    high = jnp.concatenate([right_side[:, rows - REACH :], coefficient[:, rows - 8 :]], axis=1)
    rows0 = swap(jnp.where(odd_y, low, high), jnp.where(odd_y, high, low), "gy")
    w_own = own_part(right_side)
    packed = pack(right_side, coefficient, *rows0, w_own)
    cols0 = swap(*packed, "gx")
    w_rows = rows_part(w_own, right_side, rows0, rows0, packed[0])
    w_vec, sums, even, odd = on_tensor_core(
        bind(first_kernel), "first_apply", (w_rows, right_side, coefficient, *cols0), scalars,
        (full, jax.ShapeDtypeStruct((3, 8, LANES), jnp.float32), edge, edge), sides, 3,
    )
    rows1 = swap(even, odd, "gy")
    n_own = own_part(w_vec)
    packed = pack(w_vec, None, *rows1, n_own)
    cols1 = swap(*packed, "gx")
    n_rows = rows_part(n_own, w_vec, rows1, rows0, packed[0])
    n_vec, parts = on_tensor_core(
        bind(second_kernel), "second_apply",
        (right_side, n_rows, w_vec, coefficient, *cols1, *cols0, sums), scalars,
        (full, jax.ShapeDtypeStruct((devices, LANES), jnp.float32)), sides, 3,
    )
    gathered = lax.all_to_all(parts, ("gx", "gy"), 0, 0, tiled=True)
    steps = 4
    block = pl.BlockSpec((layers, rows // steps, cols), lambda i: (0, i, 0))
    return pl.pallas_call(
        last_kernel,
        grid=(steps,),
        out_shape=(full, full),
        in_specs=[pl.BlockSpec((devices, LANES), lambda i: (0, 0))] + [block] * 3,
        out_specs=(block, block),
        compiler_params=params,
        name="last_update",
    )(gathered, right_side, w_vec, n_vec)


def solution(mesh):
    placed = (P(None, "gy", "gx"), P(None, "gy", "gx"), P(), P(), P())
    return jax.shard_map(
        on_device,
        mesh=mesh,
        in_specs=placed,
        out_specs=(P(None, "gy", "gx"), P(None, "gy", "gx")),
        check_vma=False,
    )
```

```python
import jax
import jax.numpy as jnp
from jax import lax
from jax.experimental import pallas as pl
from jax.experimental.pallas import tpu as pltpu
from jax.sharding import PartitionSpec as P

REACH = 64
LANES = 128
HALF = 64
CHUNK = 32
PIECES = 4
VMEM_BYTES = 32 * 1024 * 1024
EDGE_BYTES = 62 * 1024 * 1024
VMEM_SPEC = pl.BlockSpec(memory_space=pltpu.VMEM)
SMEM_SPEC = pl.BlockSpec(memory_space=pltpu.SMEM)


def even_swap(count):
    return [(i, i ^ 1) for i in range(count)]


def odd_swap(count):
    return [(i, i + 1 if i % 2 else i - 1) for i in range(1, count - 1)]


def is_odd(axis):
    return lax.rem(lax.axis_index(axis), 2) == 1


def swap(even, odd, axis):
    count = lax.axis_size(axis)
    return (
        lax.ppermute(even, axis, even_swap(count)),
        lax.ppermute(odd, axis, odd_swap(count)),
    )


def lane_of(shape):
    return lax.broadcasted_iota(jnp.int32, shape, 1)


def pack_columns(first, second, high):
    low_lanes = lane_of(first.shape) < HALF
    turned = pltpu.roll(second, HALF, 1)
    if high:
        return jnp.where(low_lanes, turned, first)
    return jnp.where(low_lanes, first, turned)


def store_packed(even_ref, odd_ref, odd, start, low, high):
    rows = low.shape[0]
    even_ref[start : start + rows, :] = jnp.where(odd, low, high)
    odd_ref[start : start + rows, :] = jnp.where(odd, high, low)


def pack_kernel(field, even_rows, odd_rows, ends, even_out, odd_out):
    rows, cols = field.shape[1:]
    odd_x, odd_y = is_odd("gx"), is_odd("gy")
    edges = (slice(0, LANES), slice(cols - LANES, cols))

    def halo(layer, edge, before):
        even = even_rows[layer, 0:REACH, edge]
        other = odd_rows[layer, 0:REACH, edge]
        return jnp.where(odd_y == before, even, other)

    for start, part in ((0, "above"), (REACH, "own"), (REACH + rows, "below")):
        packed = []
        for high, edge in enumerate(edges):
            if part == "own":
                pair = [field[layer, :, edge] for layer in range(2)]
            else:
                pair = [halo(layer, edge, part == "above") for layer in range(2)]
            packed.append(pack_columns(pair[0], pair[1], high))
        store_packed(even_out, odd_out, odd_x, start, packed[0], packed[1])
    if ends is not None:
        store_packed(even_out, odd_out, odd_x, 2 * REACH + rows, ends[0], ends[1])


def pack(field, even_rows, odd_rows, after, with_ends):
    rows = field.shape[1]
    out = jax.ShapeDtypeStruct((rows + 2 * REACH + (8 if with_ends else 0), LANES), jnp.float32)

    def kernel(field, even_rows, odd_rows, after, even_out, odd_out):
        pack_kernel(field, even_rows, odd_rows, after if with_ends else None, even_out, odd_out)

    return pl.pallas_call(
        kernel,
        out_shape=(out, out),
        in_specs=[VMEM_SPEC] * 4,
        out_specs=(VMEM_SPEC,) * 2,
        compiler_params=pltpu.CompilerParams(vmem_limit_bytes=VMEM_BYTES),
        name="pack_columns",
    )(field, even_rows, odd_rows, after)


def edge_kernel(field, coeff, even_out, odd_out, sems):
    rows = field.shape[1]
    odd_y = is_odd("gy")
    copies = []
    for index, (out, at_top) in enumerate(((even_out, odd_y), (odd_out, jnp.logical_not(odd_y)))):
        for part, (source, place, depth) in enumerate(((field, 0, REACH), (coeff, REACH, 8))):
            start = pl.multiple_of(jnp.where(at_top, 0, rows - depth), 8)
            copies.append(
                pltpu.make_async_copy(
                    source.at[:, pl.ds(start, depth), :],
                    out.at[:, pl.ds(place, depth), :],
                    sems.at[index, part],
                )
            )
    for copy in copies:
        copy.start()
    for copy in copies:
        copy.wait()


def edge_rows(field, coeff):
    layers, _, cols = field.shape
    out = jax.ShapeDtypeStruct((layers, REACH + 8, cols), jnp.float32)
    return pl.pallas_call(
        edge_kernel,
        out_shape=(out, out),
        in_specs=[pl.BlockSpec(memory_space=pltpu.HBM)] * 2,
        out_specs=(pl.BlockSpec(memory_space=pltpu.HBM),) * 2,
        scratch_shapes=[pltpu.SemaphoreType.DMA((2, 2))],
        compiler_params=pltpu.CompilerParams(vmem_limit_bytes=EDGE_BYTES),
        name="edge_rows",
    )(field, coeff)


def zero_rim(pad, depth, rows):
    tiles = pad.shape[1]
    for layer in range(2):
        for tile in range(tiles):
            if tile in (0, tiles - 1):
                pad[layer, tile] = jnp.zeros(pad.shape[2:], jnp.float32)
            else:
                pad[layer, tile, 0:depth, :] = jnp.zeros((depth, LANES), jnp.float32)
                pad[layer, tile, depth + rows :, :] = jnp.zeros((depth, LANES), jnp.float32)


def fill_own(pad, depth, field):
    rows, cols = field.shape[1:]
    for layer in range(2):
        for tile in range(cols // LANES):
            lanes = slice(tile * LANES, (tile + 1) * LANES)
            pad[layer, 1 + tile, depth : depth + rows, :] = field[layer, :, lanes]


def neighbours_across(load, tiles):
    lane = lane_of((CHUNK, LANES))
    values = [load(tile) for tile in range(tiles + 2)]
    back = [pltpu.roll(value, 1, 1) for value in values[:-1]]
    ahead = [pltpu.roll(value, LANES - 1, 1) for value in values[1:]]
    left = [jnp.where(lane == 0, back[i], back[i + 1]) for i in range(tiles)]
    right = [jnp.where(lane == LANES - 1, ahead[i + 1], ahead[i]) for i in range(tiles)]
    return values[1:-1], left, right


def apply_chunk(layer, row, pad, coeff_pad, shifts, weight, grid_shape, tile_shape):
    dirs = shifts.shape[0]
    rows, cols = tile_shape
    tiles = cols // LANES
    other = 1 - layer
    lane = lane_of((CHUNK, LANES))
    row_at = lax.broadcasted_iota(jnp.int32, (CHUNK, LANES), 0)
    first_row = lax.axis_index("gy") * rows + row
    first_col = lax.axis_index("gx") * cols

    def field_at(tile):
        return pad[layer, tile, pl.ds(REACH + row, CHUNK), :]

    def coeff_at(tile):
        return coeff_pad[layer, tile, pl.ds(8 + row, CHUNK), :]

    own, left, right = neighbours_across(field_at, tiles)
    own_c, left_c, right_c = neighbours_across(coeff_at, tiles)
    result = []
    for tile in range(tiles):
        value, coeff = own[tile], own_c[tile]
        above = pad[layer, 1 + tile, pl.ds(REACH - 1 + row, CHUNK), :]
        below = pad[layer, 1 + tile, pl.ds(REACH + 1 + row, CHUNK), :]
        above_c = coeff_pad[layer, 1 + tile, pl.ds(7 + row, CHUNK), :]
        below_c = coeff_pad[layer, 1 + tile, pl.ds(9 + row, CHUNK), :]
        total = (coeff + above_c) * (value - above) + (coeff + below_c) * (value - below)
        total += (coeff + left_c[tile]) * (value - left[tile])
        total += (coeff + right_c[tile]) * (value - right[tile])
        result.append(weight * total)
    for direction in range(dirs):
        shift_r, shift_c = shifts[direction, layer, 0], shifts[direction, layer, 1]
        start_r = REACH + row + shifts[direction, other, 0] - shift_r
        start_c = LANES + shifts[direction, other, 1] - shift_c
        skip = lax.shift_right_logical(start_c, 7)
        turn = jnp.bitwise_and(start_c, LANES - 1)
        back = jnp.bitwise_and(LANES - turn, LANES - 1)
        moved = [
            pltpu.roll(pad[other, skip + tile, pl.ds(start_r, CHUNK), :], back, 1)
            for tile in range(tiles + 1)
        ]
        here = lane < LANES - turn
        image_row = row_at + (first_row - shift_r)
        inside = (image_row >= 0) & (image_row < grid_shape[0])
        for tile in range(tiles):
            mask = inside
            if tile == 0:
                mask = mask & (lane >= shift_c - first_col)
            if tile == tiles - 1:
                mask = mask & (lane < grid_shape[1] + shift_c - first_col - tile * LANES)
            value = own[tile] + jnp.where(here, moved[tile], moved[tile + 1])
            result[tile] = result[tile] + jnp.where(mask, value, 0.0)
    return result


def fold(parts):
    total = sum(parts[1:], parts[0])
    pieces = [total[8 * i : 8 * i + 8] for i in range(total.shape[0] // 8)]
    return sum(pieces[1:], pieces[0])


def dot_of(first, second):
    return fold([a * b for a, b in zip(first, second, strict=True)])


def weight_of(table, entry, layer):
    return 0.5 * table[entry[layer]]


def pack_ends(coeff, ends):
    rows, cols = coeff.shape[1:]
    lane = lane_of((8, LANES))
    for high, edge in enumerate((slice(0, LANES), slice(cols - LANES, cols))):
        packed = jnp.zeros((8, LANES), jnp.float32)
        for layer in range(2):
            for group in range(rows // 8):
                at = layer * (rows // 8) + group
                turn = (at + high) % LANES
                value = coeff[layer, 8 * group : 8 * group + 8, edge]
                value = pltpu.roll(value, turn, 1) if turn else value
                packed = jnp.where(lane == at, value, packed)
        ends[high] = packed


def own_kernel(grid_shape, field, coeff, shifts, table, entry, out, ends, pad, coeff_pad):
    rows, cols = field.shape[1:]
    zero_rim(pad, REACH, rows)
    zero_rim(coeff_pad, 8, rows)
    fill_own(pad, REACH, field)
    fill_own(coeff_pad, 8, coeff)
    if ends is not None:
        pack_ends(coeff, ends)
    for layer in range(2):
        weight = weight_of(table, entry, layer)

        def step(i, carry, layer=layer, weight=weight):
            row = pl.multiple_of(i * CHUNK, CHUNK)
            result = apply_chunk(
                layer, row, pad, coeff_pad, shifts, weight, grid_shape, (rows, cols)
            )
            for tile, value in enumerate(result):
                out[layer, pl.ds(row, CHUNK), tile * LANES : (tile + 1) * LANES] = value
            return carry

        lax.fori_loop(0, rows // CHUNK, step, 0)


def products_of(own, result, base, fit):
    if base is None:
        pairs = ((own, own), (own, result), (result, result))
    else:
        rest = [a - fit * b for a, b in zip(base, own, strict=True)]
        slope = [a - fit * b for a, b in zip(own, result, strict=True)]
        pairs = (
            (rest, rest), (rest, own), (slope, rest), (result, rest), (slope, own), (result, own),
        )
    return tuple(dot_of(*pair) for pair in pairs)


def fit_of(sums):
    gamma, delta, omega = (jnp.sum(sums[index], keepdims=True) for index in range(3))
    fit = jnp.where(omega > 0.0, delta / jnp.where(omega > 0.0, omega, 1.0), 0.0)
    return gamma, delta, omega, jnp.clip(fit, -1.0, 1.0)


def rows_kernel(
    grid_shape, field, coeff, even_rows, odd_rows, even_edge, odd_edge, base, sums, shifts,
    table, entry, out, products, pad,
):
    rows, cols = field.shape[1:]
    tiles = cols // LANES
    odd_y = is_odd("gy")
    first_row = lax.axis_index("gy") * rows
    first_col = lax.axis_index("gx") * cols
    zeros = jnp.zeros((REACH, LANES), jnp.float32)
    for layer in range(2):
        for side in range(2):
            for tile in (0, tiles + 1):
                pad[layer, side, tile, 0:REACH, :] = zeros
                pad[layer, side, tile, REACH:, :] = zeros
        for tile in range(tiles):
            lanes = slice(tile * LANES, (tile + 1) * LANES)
            even = even_rows[layer, 0:REACH, lanes]
            other = odd_rows[layer, 0:REACH, lanes]
            pad[layer, 0, 1 + tile, 0:REACH, :] = jnp.where(odd_y, even, other)
            pad[layer, 0, 1 + tile, REACH:, :] = zeros
            pad[layer, 1, 1 + tile, 0:REACH, :] = zeros
            pad[layer, 1, 1 + tile, REACH:, :] = jnp.where(odd_y, other, even)
    lane = lane_of((CHUNK, LANES))
    row_at = lax.broadcasted_iota(jnp.int32, (CHUNK, LANES), 0)
    for layer in range(2):
        other_layer = 1 - layer

        def step(i, carry, layer=layer, other_layer=other_layer):
            part = pl.multiple_of(i * CHUNK, CHUNK)
            totals = [[jnp.zeros((CHUNK, LANES), jnp.float32)] * tiles for _ in range(2)]
            for direction in range(shifts.shape[0]):
                shift_r, shift_c = shifts[direction, layer, 0], shifts[direction, layer, 1]
                step_r = shifts[direction, other_layer, 0] - shift_r
                start_c = LANES + shifts[direction, other_layer, 1] - shift_c
                side = jnp.where(step_r < 0, 0, 1)
                start_r = part + step_r + jnp.where(step_r < 0, REACH, 0)
                row = part + jnp.where(step_r < 0, 0, rows - REACH)
                skip = lax.shift_right_logical(start_c, 7)
                turn = jnp.bitwise_and(start_c, LANES - 1)
                back = jnp.bitwise_and(LANES - turn, LANES - 1)
                moved = [
                    pltpu.roll(
                        pad[other_layer, side, skip + tile, pl.ds(start_r, CHUNK), :], back, 1
                    )
                    for tile in range(tiles + 1)
                ]
                here = lane < LANES - turn
                image_row = row_at + (first_row + row - shift_r)
                inside = (image_row >= 0) & (image_row < grid_shape[0])
                upper = inside & (jnp.full((CHUNK, LANES), side, jnp.int32) == 0)
                lower = inside & (jnp.full((CHUNK, LANES), side, jnp.int32) == 1)
                for tile in range(tiles):
                    value = jnp.where(here, moved[tile], moved[tile + 1])
                    if tile == 0:
                        value = jnp.where(lane >= shift_c - first_col, value, 0.0)
                    if tile == tiles - 1:
                        last = grid_shape[1] + shift_c - first_col - tile * LANES
                        value = jnp.where(lane < last, value, 0.0)
                    totals[0][tile] = totals[0][tile] + jnp.where(upper, value, 0.0)
                    totals[1][tile] = totals[1][tile] + jnp.where(lower, value, 0.0)
            for side, base in enumerate((0, rows - REACH)):
                for tile in range(tiles):
                    lanes = slice(tile * LANES, (tile + 1) * LANES)
                    out[layer, pl.ds(base + part, CHUNK), lanes] += totals[side][tile]
            return carry

        lax.fori_loop(0, REACH // CHUNK, step, 0)
        weight = weight_of(table, entry, layer)
        at = lax.broadcasted_iota(jnp.int32, (8, cols), 0)
        even = even_edge[layer, REACH : REACH + 8, :]
        other = odd_edge[layer, REACH : REACH + 8, :]
        even_v = [even_rows[layer, start : start + 8, :] for start in (0, REACH - 8)]
        other_v = [odd_rows[layer, start : start + 8, :] for start in (0, REACH - 8)]
        for start, edge_c, edge_v, spot, source in (
            (0, jnp.where(odd_y, even, other), jnp.where(odd_y, even_v[1], other_v[1]), 0, 1),
            (
                rows - 8, jnp.where(odd_y, other, even), jnp.where(odd_y, other_v[0], even_v[0]),
                7, 7,
            ),
        ):
            edge_c = pltpu.roll(edge_c, source, 0)
            edge_v = pltpu.roll(edge_v, source, 0)
            value = field[layer, start : start + 8, :]
            own_c = coeff[layer, start : start + 8, :]
            extra = weight * (edge_c * value - (own_c + edge_c) * edge_v)
            out[layer, start : start + 8, :] += jnp.where(at == spot, extra, 0.0)
    fit = None if base is None else fit_of(sums)[3]
    carry = (jnp.zeros((8, LANES), jnp.float32),) * products.shape[0]
    inner = [slice(tile * LANES, (tile + 1) * LANES) for tile in range(1, tiles - 1)]
    for layer in range(2):

        def add(i, carry, layer=layer):
            chunk = pl.ds(pl.multiple_of(i * CHUNK, CHUNK), CHUNK)
            start, own, result = (
                None if ref is None else [ref[layer, chunk, lanes] for lanes in inner]
                for ref in (base, field, out)
            )
            more = products_of(own, result, start, fit)
            return tuple(a + b for a, b in zip(carry, more, strict=True))

        carry = lax.fori_loop(0, rows // CHUNK, add, carry)
    for index, value in enumerate(carry):
        products[index] = value


def finish_chunk(grid_shape, layer, row, field, coeff, out, pad, ends, shifts, weight):
    rows, cols = field.shape[1:]
    tiles = cols // LANES
    first_row = lax.axis_index("gy") * rows + row
    first_col = lax.axis_index("gx") * cols
    lane = lane_of((CHUNK, LANES))
    row_at = lax.broadcasted_iota(jnp.int32, (CHUNK, LANES), 0)
    cut = (slice(0, LANES), slice(cols - LANES, cols))
    own = [field[layer, pl.ds(row, CHUNK), lanes] for lanes in cut]
    result = []
    for side, spot in ((0, 0), (1, LANES - 1)):
        at = layer * (rows // 8) + lax.shift_right_logical(row, 3)
        edge_c = jnp.concatenate(
            [
                pltpu.roll(ends[side], jnp.bitwise_and(LANES + spot - at - i, LANES - 1), 1)
                for i in range(CHUNK // 8)
            ]
        )
        edge_v = pad[layer, side, pl.ds(REACH + row, CHUNK), :]
        edge_v = pltpu.roll(edge_v, LANES - 1 if side else 1, 1)
        own_c = coeff[layer, pl.ds(row, CHUNK), cut[side]]
        extra = weight * (edge_c * own[side] - (own_c + edge_c) * edge_v)
        extra = jnp.where(lane == spot, extra, 0.0)
        result.append(out[layer, pl.ds(row, CHUNK), cut[side]] + extra)
    for direction in range(shifts.shape[0]):
        shift_r, shift_c = shifts[direction, layer, 0], shifts[direction, layer, 1]
        start_r = REACH + row + shifts[direction, 1 - layer, 0] - shift_r
        step_c = shifts[direction, 1 - layer, 1] - shift_c
        side = jnp.where(step_c < 0, 0, 1)
        back = jnp.bitwise_and(LANES - step_c, LANES - 1)
        moved = pltpu.roll(pad[1 - layer, side, pl.ds(start_r, CHUNK), :], back, 1)
        image_row = row_at + (first_row - shift_r)
        moved = jnp.where((image_row >= 0) & (image_row < grid_shape[0]), moved, 0.0)
        low, low_end = shift_c - first_col, jnp.where(step_c < 0, -step_c, 0)
        high = jnp.where(step_c < 0, LANES, LANES - step_c)
        high_end = grid_shape[1] + shift_c - first_col - (tiles - 1) * LANES
        result[0] = result[0] + jnp.where((lane >= low) & (lane < low_end), moved, 0.0)
        result[1] = result[1] + jnp.where((lane >= high) & (lane < high_end), moved, 0.0)
    for side in range(2):
        out[layer, pl.ds(row, CHUNK), cut[side]] = result[side]
    return own, result


def finish(
    grid_shape, base, fit, field, coeff, even_cols, odd_cols, even_ends, odd_ends, products, shifts,
    table, entry, out, pad,
):
    rows, cols = field.shape[1:]
    depth = rows + 2 * REACH
    odd_x = is_odd("gx")
    even, other = even_cols[0:depth, :], odd_cols[0:depth, :]
    for side, packed in ((0, jnp.where(odd_x, even, other)), (1, jnp.where(odd_x, other, even))):
        pad[0, side] = packed
        pad[1, side] = pltpu.roll(packed, HALF, 1)
    even, other = even_ends[depth : depth + 8, :], odd_ends[depth : depth + 8, :]
    ends = (jnp.where(odd_x, even, other), jnp.where(odd_x, other, even))
    cut = (slice(0, LANES), slice(cols - LANES, cols))
    carry = tuple(products[index] for index in range(products.shape[0]))
    for layer in range(2):
        weight = weight_of(table, entry, layer)

        def step(i, carry, layer=layer, weight=weight):
            row = pl.multiple_of(i * CHUNK, CHUNK)
            own, result = finish_chunk(
                grid_shape, layer, row, field, coeff, out, pad, ends, shifts, weight
            )
            chunk = pl.ds(row, CHUNK)
            start = None if base is None else [base[layer, chunk, lanes] for lanes in cut]
            more = products_of(own, result, start, fit)
            return tuple(a + b for a, b in zip(carry, more, strict=True))

        carry = lax.fori_loop(0, rows // CHUNK, step, carry)
    return carry


def first_kernel(
    grid_shape, before, field, coeff, even_cols, odd_cols, products, shifts, table, entry,
    out, sums, even_out, odd_out, pad,
):
    del before
    rows = field.shape[1]
    carry = finish(
        grid_shape, None, None, field, coeff, even_cols, odd_cols, even_cols, odd_cols, products,
        shifts, table, entry, out, pad,
    )
    for index, value in enumerate(carry):
        sums[index] = value
    odd_y = is_odd("gy")
    low, high = out[:, 0:REACH, :], out[:, rows - REACH :, :]
    even_out[...] = jnp.where(odd_y, low, high)
    odd_out[...] = jnp.where(odd_y, high, low)


def second_kernel(
    grid_shape, before, base, field, coeff, even_cols, odd_cols, even_ends, odd_ends, products,
    sums, shifts, table, entry, out, parts, pad,
):
    del before
    gamma, delta, omega, fit = fit_of(sums)
    carry = finish(
        grid_shape, base, fit, field, coeff, even_cols, odd_cols, even_ends, odd_ends, products,
        shifts, table, entry, out, pad,
    )
    rest2, rest_w, slope_rest, n_rest, slope_w, n_w = (
        jnp.sum(value, keepdims=True) for value in carry
    )
    lane = lane_of((8, LANES))
    row = jnp.zeros((8, LANES), jnp.float32)
    for at, value in (
        (0, rest2), (1, slope_rest), (8, 2.0 * rest_w), (9, n_rest + slope_w),
        (16, omega), (17, n_w), (24, fit), (25, fit), (32, gamma), (33, delta),
    ):
        row = jnp.where(lane == at, value, row)
    for start in range(0, parts.shape[0], 8):
        parts[start : start + 8, :] = row


def pick(row, lane, at):
    return jnp.sum(jnp.where(lane == at, row, 0.0), keepdims=True)


def last_kernel(
    parts, base, w_vec, n_vec, solution_out, residual_out, solution_part, residual_part, sems
):
    gathered = parts[...]
    count = gathered.shape[0]
    lane = lane_of((8, LANES))
    total = sum(gathered[8 * i : 8 * i + 8] for i in range(count // 8))
    gamma, delta = pick(total, lane, 32), pick(total, lane, 33)
    alpha = gamma / delta
    gap = alpha - pltpu.roll(gathered, LANES - 24, 1)
    moved = gathered - gap * pltpu.roll(gathered, LANES - 8, 1)
    moved = moved + gap * gap * pltpu.roll(gathered, LANES - 16, 1)
    total = sum(moved[8 * i : 8 * i + 8] for i in range(count // 8))
    gamma_next, delta_next = pick(total, lane, 0), pick(total, lane, 1)
    beta = gamma_next / gamma
    alpha_next = gamma_next / (delta_next - beta * gamma_next / alpha)
    layers, rows = base.shape[:2]
    depth = rows // PIECES
    copies = []
    for layer in range(layers):
        for piece in range(PIECES):
            part = pl.ds(piece * depth, depth)
            start, w_start = base[layer, part, :], w_vec[layer, part, :]
            residual = start - alpha * w_start
            w_next = w_start - alpha * n_vec[layer, part, :]
            solution_part[layer, part, :] = alpha * start + alpha_next * (residual + beta * start)
            residual_part[layer, part, :] = residual - alpha_next * (w_next + beta * w_start)
            for which, (source, target) in enumerate(
                ((solution_part, solution_out), (residual_part, residual_out))
            ):
                copy = pltpu.make_async_copy(
                    source.at[layer, part, :],
                    target.at[layer, part, :],
                    sems.at[which, layer, piece],
                )
                copy.start()
                copies.append(copy)
    for copy in copies:
        copy.wait()


def on_tensor_core(kernel, name, operands, scalars, out_shape, scratch, microseconds, in_place=False):
    return pl.pallas_call(
        kernel,
        out_shape=out_shape,
        in_specs=[VMEM_SPEC] * len(operands) + [SMEM_SPEC] * len(scalars),
        out_specs=(VMEM_SPEC,) * len(out_shape),
        scratch_shapes=[pltpu.VMEM(shape, jnp.float32) for shape in scratch],
        input_output_aliases={0: 0} if in_place else {},
        compiler_params=pltpu.CompilerParams(vmem_limit_bytes=VMEM_BYTES),
        cost_estimate=pl.CostEstimate(
            flops=0, bytes_accessed=3_000_000 * microseconds, transcendentals=0
        ),
        name=name,
    )(*operands, *scalars)


def on_device(right_side, coefficient, strength_table, layer_entry, shifts):
    layers, rows, cols = right_side.shape
    count_y, count_x = lax.axis_size("gy"), lax.axis_size("gx")
    devices = count_x * count_y
    tiles = cols // LANES
    grid_shape = (rows * count_y, cols * count_x)
    full = jax.ShapeDtypeStruct((layers, rows, cols), jnp.float32)
    edge = jax.ShapeDtypeStruct((layers, REACH, cols), jnp.float32)
    scalars = (shifts, strength_table, layer_entry)
    own_pads = [(2, tiles + 2, rows + 2 * REACH, LANES), (2, tiles + 2, rows + 16, LANES)]
    row_pads = [(2, 2, tiles + 2, 2 * REACH, LANES)]
    side_pads = [(2, 2, rows + 2 * REACH, LANES)]

    def sums_of(count):
        return jax.ShapeDtypeStruct((count, 8, LANES), jnp.float32)

    def bind(kernel):
        def bound(*refs):
            kernel(grid_shape, *refs)

        return bound

    def rows_first(before, field, coeff, even, odd, packed, *refs):
        del before, packed
        rows_kernel(grid_shape, field, coeff, even, odd, even, odd, None, None, *refs)

    def rows_second(before, field, coeff, even, odd, even_edge, odd_edge, packed, *refs):
        del before, packed
        rows_kernel(grid_shape, field, coeff, even, odd, even_edge, odd_edge, *refs)

    def own_first(field, coeff, shifts, table, entry, out, ends, *pads):
        own_kernel(grid_shape, field, coeff, shifts, table, entry, out, ends, *pads)

    def own_second(field, coeff, shifts, table, entry, out, *pads):
        own_kernel(grid_shape, field, coeff, shifts, table, entry, out, None, *pads)

    rows0 = swap(*edge_rows(right_side, coefficient), "gy")
    w_own, ends = on_tensor_core(
        own_first, "own_first", (right_side, coefficient), scalars, (full, sums_of(2)), own_pads, 6
    )
    packed = pack(right_side, *rows0, ends, True)
    cols0 = swap(*packed, "gx")
    w_rows, products = on_tensor_core(
        rows_first, "rows_first", (w_own, right_side, coefficient, *rows0, packed[0]), scalars,
        (full, sums_of(3)), row_pads, 3, True,
    )
    w_vec, sums, even, odd = on_tensor_core(
        bind(first_kernel), "first_apply", (w_rows, right_side, coefficient, *cols0, products),
        scalars, (full, sums_of(3), edge, edge), side_pads, 3, True,
    )
    rows1 = swap(even, odd, "gy")
    (n_own,) = on_tensor_core(
        own_second, "own_second", (w_vec, coefficient), scalars, (full,), own_pads, 6
    )
    packed = pack(w_vec, *rows1, n_own, False)
    cols1 = swap(*packed, "gx")
    n_rows, products = on_tensor_core(
        rows_second, "rows_second",
        (n_own, w_vec, coefficient, *rows1, *rows0, packed[0], right_side, sums), scalars,
        (full, sums_of(6)), row_pads, 3, True,
    )
    n_vec, parts = on_tensor_core(
        bind(second_kernel), "second_apply",
        (n_rows, right_side, w_vec, coefficient, *cols1, *cols0, products, sums), scalars,
        (full, jax.ShapeDtypeStruct((devices, LANES), jnp.float32)), side_pads, 3, True,
    )
    gathered = lax.all_to_all(parts, ("gx", "gy"), 0, 0, tiled=True)
    return pl.pallas_call(
        last_kernel,
        out_shape=(full, full),
        in_specs=[VMEM_SPEC] * 4,
        out_specs=(pl.BlockSpec(memory_space=pltpu.HBM),) * 2,
        scratch_shapes=[
            pltpu.VMEM((layers, rows, cols), jnp.float32),
            pltpu.VMEM((layers, rows, cols), jnp.float32),
            pltpu.SemaphoreType.DMA((2, layers, PIECES)),
        ],
        compiler_params=pltpu.CompilerParams(vmem_limit_bytes=VMEM_BYTES),
        name="last_update",
    )(gathered, right_side, w_vec, n_vec)


def solution(mesh):
    placed = (P(None, "gy", "gx"), P(None, "gy", "gx"), P(), P(), P())
    return jax.shard_map(
        on_device,
        mesh=mesh,
        in_specs=placed,
        out_specs=(P(None, "gy", "gx"), P(None, "gy", "gx")),
        check_vma=False,
    )
```

```python
import jax
import jax.numpy as jnp
from jax import lax
from jax.experimental import pallas as pl
from jax.experimental.pallas import tpu as pltpu
from jax.sharding import PartitionSpec as P

REACH = 64
LANES = 128
HALF = 64
CHUNK = 32
UNROLL = 8
PIECES = 4
VMEM_BYTES = 32 * 1024 * 1024
EDGE_BYTES = 60 * 1024 * 1024
VMEM_SPEC = pl.BlockSpec(memory_space=pltpu.VMEM)
SMEM_SPEC = pl.BlockSpec(memory_space=pltpu.SMEM)


def even_swap(count):
    return [(i, i ^ 1) for i in range(count)]


def odd_swap(count):
    return [(i, i + 1 if i % 2 else i - 1) for i in range(1, count - 1)]


def is_odd(axis):
    return lax.rem(lax.axis_index(axis), 2) == 1


def swap(even, odd, axis):
    count = lax.axis_size(axis)
    return (
        lax.ppermute(even, axis, even_swap(count)),
        lax.ppermute(odd, axis, odd_swap(count)),
    )


def lane_of(shape):
    return lax.broadcasted_iota(jnp.int32, shape, 1)


def pack_columns(first, second, high):
    low_lanes = lane_of(first.shape) < HALF
    turned = pltpu.roll(second, HALF, 1)
    if high:
        return jnp.where(low_lanes, turned, first)
    return jnp.where(low_lanes, first, turned)


def store_packed(even_ref, odd_ref, odd, start, low, high):
    rows = low.shape[0]
    even_ref[start : start + rows, :] = jnp.where(odd, low, high)
    odd_ref[start : start + rows, :] = jnp.where(odd, high, low)


def pack_kernel(field, even_rows, odd_rows, ends, even_out, odd_out):
    rows, cols = field.shape[1:]
    odd_x, odd_y = is_odd("gx"), is_odd("gy")
    edges = (slice(0, LANES), slice(cols - LANES, cols))

    def halo(layer, edge, before):
        even = even_rows[layer, 0:REACH, edge]
        other = odd_rows[layer, 0:REACH, edge]
        return jnp.where(odd_y == before, even, other)

    for start, part in ((0, "above"), (REACH, "own"), (REACH + rows, "below")):
        packed = []
        for high, edge in enumerate(edges):
            if part == "own":
                pair = [field[layer, :, edge] for layer in range(2)]
            else:
                pair = [halo(layer, edge, part == "above") for layer in range(2)]
            packed.append(pack_columns(pair[0], pair[1], high))
        store_packed(even_out, odd_out, odd_x, start, packed[0], packed[1])
    if ends is not None:
        store_packed(even_out, odd_out, odd_x, 2 * REACH + rows, ends[0], ends[1])


def pack(field, even_rows, odd_rows, after, with_ends):
    rows = field.shape[1]
    out = jax.ShapeDtypeStruct((rows + 2 * REACH + (8 if with_ends else 0), LANES), jnp.float32)

    def kernel(field, even_rows, odd_rows, after, even_out, odd_out):
        pack_kernel(field, even_rows, odd_rows, after if with_ends else None, even_out, odd_out)

    return pl.pallas_call(
        kernel,
        out_shape=(out, out),
        in_specs=[VMEM_SPEC] * 4,
        out_specs=(VMEM_SPEC,) * 2,
        compiler_params=pltpu.CompilerParams(vmem_limit_bytes=VMEM_BYTES),
        name="pack_columns",
    )(field, even_rows, odd_rows, after)


def edge_kernel(field, coeff, even_out, odd_out, sems):
    rows = field.shape[1]
    odd_y = is_odd("gy")
    copies = []
    for index, (out, at_top) in enumerate(((even_out, odd_y), (odd_out, jnp.logical_not(odd_y)))):
        for part, (source, place, depth) in enumerate(((field, 0, REACH), (coeff, REACH, 8))):
            start = pl.multiple_of(jnp.where(at_top, 0, rows - depth), 8)
            copies.append(
                pltpu.make_async_copy(
                    source.at[:, pl.ds(start, depth), :],
                    out.at[:, pl.ds(place, depth), :],
                    sems.at[index, part],
                )
            )
    for copy in copies:
        copy.start()
    for copy in copies:
        copy.wait()


def edge_rows(field, coeff):
    layers, _, cols = field.shape
    out = jax.ShapeDtypeStruct((layers, REACH + 8, cols), jnp.float32)
    return pl.pallas_call(
        edge_kernel,
        out_shape=(out, out),
        in_specs=[pl.BlockSpec(memory_space=pltpu.HBM)] * 2,
        out_specs=(VMEM_SPEC,) * 2,
        scratch_shapes=[pltpu.SemaphoreType.DMA((2, 2))],
        compiler_params=pltpu.CompilerParams(vmem_limit_bytes=EDGE_BYTES),
        name="edge_rows",
    )(field, coeff)


def zero_rim(pad, depth, rows):
    tiles = pad.shape[1]
    for layer in range(2):
        for tile in range(tiles):
            if tile in (0, tiles - 1):
                pad[layer, tile] = jnp.zeros(pad.shape[2:], jnp.float32)
            else:
                pad[layer, tile, 0:depth, :] = jnp.zeros((depth, LANES), jnp.float32)
                pad[layer, tile, depth + rows :, :] = jnp.zeros((depth, LANES), jnp.float32)


def fill_own(pad, depth, field):
    rows, cols = field.shape[1:]
    for layer in range(2):
        for tile in range(cols // LANES):
            lanes = slice(tile * LANES, (tile + 1) * LANES)
            pad[layer, 1 + tile, depth : depth + rows, :] = field[layer, :, lanes]


def neighbours_across(load, tiles):
    lane = lane_of((CHUNK, LANES))
    values = [load(tile) for tile in range(tiles + 2)]
    back = [pltpu.roll(value, 1, 1) for value in values[:-1]]
    ahead = [pltpu.roll(value, LANES - 1, 1) for value in values[1:]]
    left = [jnp.where(lane == 0, back[i], back[i + 1]) for i in range(tiles)]
    right = [jnp.where(lane == LANES - 1, ahead[i + 1], ahead[i]) for i in range(tiles)]
    return values[1:-1], left, right


def apply_chunk(layer, row, pad, coeff_pad, shifts, weight, grid_shape, tile_shape):
    dirs = shifts.shape[0]
    rows, cols = tile_shape
    tiles = cols // LANES
    other = 1 - layer
    lane = lane_of((CHUNK, LANES))
    row_at = lax.broadcasted_iota(jnp.int32, (CHUNK, LANES), 0)
    first_row = lax.axis_index("gy") * rows + row
    first_col = lax.axis_index("gx") * cols

    def field_at(tile):
        return pad[layer, tile, pl.ds(REACH + row, CHUNK), :]

    def coeff_at(tile):
        return coeff_pad[layer, tile, pl.ds(8 + row, CHUNK), :]

    own, left, right = neighbours_across(field_at, tiles)
    own_c, left_c, right_c = neighbours_across(coeff_at, tiles)
    result = []
    for tile in range(tiles):
        value, coeff = own[tile], own_c[tile]
        above = pad[layer, 1 + tile, pl.ds(REACH - 1 + row, CHUNK), :]
        below = pad[layer, 1 + tile, pl.ds(REACH + 1 + row, CHUNK), :]
        above_c = coeff_pad[layer, 1 + tile, pl.ds(7 + row, CHUNK), :]
        below_c = coeff_pad[layer, 1 + tile, pl.ds(9 + row, CHUNK), :]
        total = (coeff + above_c) * (value - above) + (coeff + below_c) * (value - below)
        total += (coeff + left_c[tile]) * (value - left[tile])
        total += (coeff + right_c[tile]) * (value - right[tile])
        result.append(weight * total)
    for direction in range(dirs):
        shift_r, shift_c = shifts[direction, layer, 0], shifts[direction, layer, 1]
        start_r = REACH + row + shifts[direction, other, 0] - shift_r
        start_c = LANES + shifts[direction, other, 1] - shift_c
        skip = lax.shift_right_logical(start_c, 7)
        turn = jnp.bitwise_and(start_c, LANES - 1)
        back = jnp.bitwise_and(LANES - turn, LANES - 1)
        moved = [
            pltpu.roll(pad[other, skip + tile, pl.ds(start_r, CHUNK), :], back, 1)
            for tile in range(tiles + 1)
        ]
        here = lane < LANES - turn
        image_row = row_at + (first_row - shift_r)
        inside = (image_row >= 0) & (image_row < grid_shape[0])
        for tile in range(tiles):
            mask = inside
            if tile == 0:
                mask = mask & (lane >= shift_c - first_col)
            if tile == tiles - 1:
                mask = mask & (lane < grid_shape[1] + shift_c - first_col - tile * LANES)
            value = own[tile] + jnp.where(here, moved[tile], moved[tile + 1])
            result[tile] = result[tile] + jnp.where(mask, value, 0.0)
    return result


def fold(parts):
    total = sum(parts[1:], parts[0])
    pieces = [total[8 * i : 8 * i + 8] for i in range(total.shape[0] // 8)]
    return sum(pieces[1:], pieces[0])


def dot_of(first, second):
    return fold([a * b for a, b in zip(first, second, strict=True)])


def weight_of(table, entry, layer):
    return 0.5 * table[entry[layer]]


def pack_ends(coeff, ends):
    rows, cols = coeff.shape[1:]
    lane = lane_of((8, LANES))
    for high, edge in enumerate((slice(0, LANES), slice(cols - LANES, cols))):
        packed = jnp.zeros((8, LANES), jnp.float32)
        for layer in range(2):
            for group in range(rows // 8):
                at = layer * (rows // 8) + group
                turn = (at + high) % LANES
                value = coeff[layer, 8 * group : 8 * group + 8, edge]
                value = pltpu.roll(value, turn, 1) if turn else value
                packed = jnp.where(lane == at, value, packed)
        ends[high] = packed


def own_kernel(grid_shape, field, coeff, shifts, table, entry, out, ends, pad, coeff_pad):
    rows, cols = field.shape[1:]
    zero_rim(pad, REACH, rows)
    zero_rim(coeff_pad, 8, rows)
    fill_own(pad, REACH, field)
    fill_own(coeff_pad, 8, coeff)
    if ends is not None:
        pack_ends(coeff, ends)
    for layer in range(2):
        weight = weight_of(table, entry, layer)

        def step(i, carry, layer=layer, weight=weight):
            row = pl.multiple_of(i * CHUNK, CHUNK)
            result = apply_chunk(
                layer, row, pad, coeff_pad, shifts, weight, grid_shape, (rows, cols)
            )
            for tile, value in enumerate(result):
                out[layer, pl.ds(row, CHUNK), tile * LANES : (tile + 1) * LANES] = value
            return carry

        lax.fori_loop(0, rows // CHUNK, step, 0, unroll=UNROLL)


def products_of(own, result, base, fit):
    if base is None:
        pairs = ((own, own), (own, result), (result, result))
    else:
        rest = [a - fit * b for a, b in zip(base, own, strict=True)]
        slope = [a - fit * b for a, b in zip(own, result, strict=True)]
        pairs = (
            (rest, rest), (rest, own), (slope, rest), (result, rest), (slope, own), (result, own),
        )
    return tuple(dot_of(*pair) for pair in pairs)


def fit_of(sums):
    gamma, delta, omega = (jnp.sum(sums[index], keepdims=True) for index in range(3))
    fit = jnp.where(omega > 0.0, delta / jnp.where(omega > 0.0, omega, 1.0), 0.0)
    return gamma, delta, omega, jnp.clip(fit, -1.0, 1.0)


def rows_kernel(
    grid_shape, field, coeff, even_rows, odd_rows, even_edge, odd_edge, base, sums, shifts,
    table, entry, out, products, pad,
):
    rows, cols = field.shape[1:]
    tiles = cols // LANES
    odd_y = is_odd("gy")
    first_row = lax.axis_index("gy") * rows
    first_col = lax.axis_index("gx") * cols
    zeros = jnp.zeros((REACH, LANES), jnp.float32)
    for layer in range(2):
        for side in range(2):
            for tile in (0, tiles + 1):
                pad[layer, side, tile, 0:REACH, :] = zeros
                pad[layer, side, tile, REACH:, :] = zeros
        for tile in range(tiles):
            lanes = slice(tile * LANES, (tile + 1) * LANES)
            even = even_rows[layer, 0:REACH, lanes]
            other = odd_rows[layer, 0:REACH, lanes]
            pad[layer, 0, 1 + tile, 0:REACH, :] = jnp.where(odd_y, even, other)
            pad[layer, 0, 1 + tile, REACH:, :] = zeros
            pad[layer, 1, 1 + tile, 0:REACH, :] = zeros
            pad[layer, 1, 1 + tile, REACH:, :] = jnp.where(odd_y, other, even)
    lane = lane_of((CHUNK, LANES))
    row_at = lax.broadcasted_iota(jnp.int32, (CHUNK, LANES), 0)
    for layer in range(2):
        other_layer = 1 - layer

        def step(i, carry, layer=layer, other_layer=other_layer):
            part = pl.multiple_of(i * CHUNK, CHUNK)
            totals = [[jnp.zeros((CHUNK, LANES), jnp.float32)] * tiles for _ in range(2)]
            for direction in range(shifts.shape[0]):
                shift_r, shift_c = shifts[direction, layer, 0], shifts[direction, layer, 1]
                step_r = shifts[direction, other_layer, 0] - shift_r
                start_c = LANES + shifts[direction, other_layer, 1] - shift_c
                side = jnp.where(step_r < 0, 0, 1)
                start_r = part + step_r + jnp.where(step_r < 0, REACH, 0)
                row = part + jnp.where(step_r < 0, 0, rows - REACH)
                skip = lax.shift_right_logical(start_c, 7)
                turn = jnp.bitwise_and(start_c, LANES - 1)
                back = jnp.bitwise_and(LANES - turn, LANES - 1)
                moved = [
                    pltpu.roll(
                        pad[other_layer, side, skip + tile, pl.ds(start_r, CHUNK), :], back, 1
                    )
                    for tile in range(tiles + 1)
                ]
                here = lane < LANES - turn
                image_row = row_at + (first_row + row - shift_r)
                inside = (image_row >= 0) & (image_row < grid_shape[0])
                upper = inside & (jnp.full((CHUNK, LANES), side, jnp.int32) == 0)
                lower = inside & (jnp.full((CHUNK, LANES), side, jnp.int32) == 1)
                for tile in range(tiles):
                    value = jnp.where(here, moved[tile], moved[tile + 1])
                    if tile == 0:
                        value = jnp.where(lane >= shift_c - first_col, value, 0.0)
                    if tile == tiles - 1:
                        last = grid_shape[1] + shift_c - first_col - tile * LANES
                        value = jnp.where(lane < last, value, 0.0)
                    totals[0][tile] = totals[0][tile] + jnp.where(upper, value, 0.0)
                    totals[1][tile] = totals[1][tile] + jnp.where(lower, value, 0.0)
            for side, base in enumerate((0, rows - REACH)):
                for tile in range(tiles):
                    lanes = slice(tile * LANES, (tile + 1) * LANES)
                    out[layer, pl.ds(base + part, CHUNK), lanes] += totals[side][tile]
            return carry

        lax.fori_loop(0, REACH // CHUNK, step, 0)
        weight = weight_of(table, entry, layer)
        at = lax.broadcasted_iota(jnp.int32, (8, cols), 0)
        even = even_edge[layer, REACH : REACH + 8, :]
        other = odd_edge[layer, REACH : REACH + 8, :]
        even_v = [even_rows[layer, start : start + 8, :] for start in (0, REACH - 8)]
        other_v = [odd_rows[layer, start : start + 8, :] for start in (0, REACH - 8)]
        for start, edge_c, edge_v, spot, source in (
            (0, jnp.where(odd_y, even, other), jnp.where(odd_y, even_v[1], other_v[1]), 0, 1),
            (
                rows - 8, jnp.where(odd_y, other, even), jnp.where(odd_y, other_v[0], even_v[0]),
                7, 7,
            ),
        ):
            edge_c = pltpu.roll(edge_c, source, 0)
            edge_v = pltpu.roll(edge_v, source, 0)
            value = field[layer, start : start + 8, :]
            own_c = coeff[layer, start : start + 8, :]
            extra = weight * (edge_c * value - (own_c + edge_c) * edge_v)
            out[layer, start : start + 8, :] += jnp.where(at == spot, extra, 0.0)
    fit = None if base is None else fit_of(sums)[3]
    carry = (jnp.zeros((8, LANES), jnp.float32),) * products.shape[0]
    inner = [slice(tile * LANES, (tile + 1) * LANES) for tile in range(1, tiles - 1)]
    for layer in range(2):

        def add(i, carry, layer=layer):
            chunk = pl.ds(pl.multiple_of(i * CHUNK, CHUNK), CHUNK)
            start, own, result = (
                None if ref is None else [ref[layer, chunk, lanes] for lanes in inner]
                for ref in (base, field, out)
            )
            more = products_of(own, result, start, fit)
            return tuple(a + b for a, b in zip(carry, more, strict=True))

        carry = lax.fori_loop(0, rows // CHUNK, add, carry, unroll=UNROLL)
    for index, value in enumerate(carry):
        products[index] = value


def finish_chunk(grid_shape, layer, row, field, coeff, out, pad, ends, shifts, weight):
    rows, cols = field.shape[1:]
    tiles = cols // LANES
    first_row = lax.axis_index("gy") * rows + row
    first_col = lax.axis_index("gx") * cols
    lane = lane_of((CHUNK, LANES))
    row_at = lax.broadcasted_iota(jnp.int32, (CHUNK, LANES), 0)
    cut = (slice(0, LANES), slice(cols - LANES, cols))
    own = [field[layer, pl.ds(row, CHUNK), lanes] for lanes in cut]
    result = []
    for side, spot in ((0, 0), (1, LANES - 1)):
        at = layer * (rows // 8) + lax.shift_right_logical(row, 3)
        edge_c = jnp.concatenate(
            [
                pltpu.roll(ends[side], jnp.bitwise_and(LANES + spot - at - i, LANES - 1), 1)
                for i in range(CHUNK // 8)
            ]
        )
        edge_v = pad[layer, side, pl.ds(REACH + row, CHUNK), :]
        edge_v = pltpu.roll(edge_v, LANES - 1 if side else 1, 1)
        own_c = coeff[layer, pl.ds(row, CHUNK), cut[side]]
        extra = weight * (edge_c * own[side] - (own_c + edge_c) * edge_v)
        extra = jnp.where(lane == spot, extra, 0.0)
        result.append(out[layer, pl.ds(row, CHUNK), cut[side]] + extra)
    for direction in range(shifts.shape[0]):
        shift_r, shift_c = shifts[direction, layer, 0], shifts[direction, layer, 1]
        start_r = REACH + row + shifts[direction, 1 - layer, 0] - shift_r
        step_c = shifts[direction, 1 - layer, 1] - shift_c
        side = jnp.where(step_c < 0, 0, 1)
        back = jnp.bitwise_and(LANES - step_c, LANES - 1)
        moved = pltpu.roll(pad[1 - layer, side, pl.ds(start_r, CHUNK), :], back, 1)
        image_row = row_at + (first_row - shift_r)
        moved = jnp.where((image_row >= 0) & (image_row < grid_shape[0]), moved, 0.0)
        low, low_end = shift_c - first_col, jnp.where(step_c < 0, -step_c, 0)
        high = jnp.where(step_c < 0, LANES, LANES - step_c)
        high_end = grid_shape[1] + shift_c - first_col - (tiles - 1) * LANES
        result[0] = result[0] + jnp.where((lane >= low) & (lane < low_end), moved, 0.0)
        result[1] = result[1] + jnp.where((lane >= high) & (lane < high_end), moved, 0.0)
    for side in range(2):
        out[layer, pl.ds(row, CHUNK), cut[side]] = result[side]
    return own, result


def finish(
    grid_shape, base, fit, field, coeff, even_cols, odd_cols, even_ends, odd_ends, products, shifts,
    table, entry, out, pad,
):
    rows, cols = field.shape[1:]
    depth = rows + 2 * REACH
    odd_x = is_odd("gx")
    even, other = even_cols[0:depth, :], odd_cols[0:depth, :]
    for side, packed in ((0, jnp.where(odd_x, even, other)), (1, jnp.where(odd_x, other, even))):
        pad[0, side] = packed
        pad[1, side] = pltpu.roll(packed, HALF, 1)
    even, other = even_ends[depth : depth + 8, :], odd_ends[depth : depth + 8, :]
    ends = (jnp.where(odd_x, even, other), jnp.where(odd_x, other, even))
    cut = (slice(0, LANES), slice(cols - LANES, cols))
    carry = tuple(products[index] for index in range(products.shape[0]))
    for layer in range(2):
        weight = weight_of(table, entry, layer)

        def step(i, carry, layer=layer, weight=weight):
            row = pl.multiple_of(i * CHUNK, CHUNK)
            own, result = finish_chunk(
                grid_shape, layer, row, field, coeff, out, pad, ends, shifts, weight
            )
            chunk = pl.ds(row, CHUNK)
            start = None if base is None else [base[layer, chunk, lanes] for lanes in cut]
            more = products_of(own, result, start, fit)
            return tuple(a + b for a, b in zip(carry, more, strict=True))

        carry = lax.fori_loop(0, rows // CHUNK, step, carry, unroll=UNROLL)
    return carry


def first_kernel(
    grid_shape, before, field, coeff, even_cols, odd_cols, products, shifts, table, entry,
    out, sums, even_out, odd_out, pad,
):
    del before
    rows = field.shape[1]
    carry = finish(
        grid_shape, None, None, field, coeff, even_cols, odd_cols, even_cols, odd_cols, products,
        shifts, table, entry, out, pad,
    )
    for index, value in enumerate(carry):
        sums[index] = value
    odd_y = is_odd("gy")
    low, high = out[:, 0:REACH, :], out[:, rows - REACH :, :]
    even_out[...] = jnp.where(odd_y, low, high)
    odd_out[...] = jnp.where(odd_y, high, low)


def second_kernel(
    grid_shape, before, base, field, coeff, even_cols, odd_cols, even_ends, odd_ends, products,
    sums, shifts, table, entry, out, parts, pad,
):
    del before
    gamma, delta, omega, fit = fit_of(sums)
    carry = finish(
        grid_shape, base, fit, field, coeff, even_cols, odd_cols, even_ends, odd_ends, products,
        shifts, table, entry, out, pad,
    )
    rest2, rest_w, slope_rest, n_rest, slope_w, n_w = (
        jnp.sum(value, keepdims=True) for value in carry
    )
    lane = lane_of((8, LANES))
    row = jnp.zeros((8, LANES), jnp.float32)
    for at, value in (
        (0, rest2), (1, slope_rest), (8, 2.0 * rest_w), (9, n_rest + slope_w),
        (16, omega), (17, n_w), (24, fit), (25, fit), (32, gamma), (33, delta),
    ):
        row = jnp.where(lane == at, value, row)
    for start in range(0, parts.shape[0], 8):
        parts[start : start + 8, :] = row


def pick(row, lane, at):
    return jnp.sum(jnp.where(lane == at, row, 0.0), keepdims=True)


def last_kernel(
    parts, base, w_vec, n_vec, solution_out, residual_out, solution_part, residual_part, sems
):
    gathered = parts[...]
    count = gathered.shape[0]
    lane = lane_of((8, LANES))
    total = sum(gathered[8 * i : 8 * i + 8] for i in range(count // 8))
    gamma, delta = pick(total, lane, 32), pick(total, lane, 33)
    alpha = gamma / delta
    gap = alpha - pltpu.roll(gathered, LANES - 24, 1)
    moved = gathered - gap * pltpu.roll(gathered, LANES - 8, 1)
    moved = moved + gap * gap * pltpu.roll(gathered, LANES - 16, 1)
    total = sum(moved[8 * i : 8 * i + 8] for i in range(count // 8))
    gamma_next, delta_next = pick(total, lane, 0), pick(total, lane, 1)
    beta = gamma_next / gamma
    alpha_next = gamma_next / (delta_next - beta * gamma_next / alpha)
    layers, rows = base.shape[:2]
    depth = rows // PIECES
    copies = []
    for layer in range(layers):
        for piece in range(PIECES):
            part = pl.ds(piece * depth, depth)
            start, w_start = base[layer, part, :], w_vec[layer, part, :]
            residual = start - alpha * w_start
            w_next = w_start - alpha * n_vec[layer, part, :]
            solution_part[layer, part, :] = alpha * start + alpha_next * (residual + beta * start)
            residual_part[layer, part, :] = residual - alpha_next * (w_next + beta * w_start)
            for which, (source, target) in enumerate(
                ((solution_part, solution_out), (residual_part, residual_out))
            ):
                copy = pltpu.make_async_copy(
                    source.at[layer, part, :],
                    target.at[layer, part, :],
                    sems.at[which, layer, piece],
                )
                copy.start()
                copies.append(copy)
    for copy in copies:
        copy.wait()


def on_tensor_core(kernel, name, operands, scalars, out_shape, scratch, microseconds, in_place=False):
    return pl.pallas_call(
        kernel,
        out_shape=out_shape,
        in_specs=[VMEM_SPEC] * len(operands) + [SMEM_SPEC] * len(scalars),
        out_specs=(VMEM_SPEC,) * len(out_shape),
        scratch_shapes=[pltpu.VMEM(shape, jnp.float32) for shape in scratch],
        input_output_aliases={0: 0} if in_place else {},
        compiler_params=pltpu.CompilerParams(vmem_limit_bytes=VMEM_BYTES),
        cost_estimate=pl.CostEstimate(
            flops=0, bytes_accessed=3_000_000 * microseconds, transcendentals=0
        ),
        name=name,
    )(*operands, *scalars)


def on_device(right_side, coefficient, strength_table, layer_entry, shifts):
    layers, rows, cols = right_side.shape
    count_y, count_x = lax.axis_size("gy"), lax.axis_size("gx")
    devices = count_x * count_y
    tiles = cols // LANES
    grid_shape = (rows * count_y, cols * count_x)
    full = jax.ShapeDtypeStruct((layers, rows, cols), jnp.float32)
    edge = jax.ShapeDtypeStruct((layers, REACH, cols), jnp.float32)
    scalars = (shifts, strength_table, layer_entry)
    own_pads = [(2, tiles + 2, rows + 2 * REACH, LANES), (2, tiles + 2, rows + 16, LANES)]
    row_pads = [(2, 2, tiles + 2, 2 * REACH, LANES)]
    side_pads = [(2, 2, rows + 2 * REACH, LANES)]

    def sums_of(count):
        return jax.ShapeDtypeStruct((count, 8, LANES), jnp.float32)

    def bind(kernel):
        def bound(*refs):
            kernel(grid_shape, *refs)

        return bound

    def rows_first(before, field, coeff, even, odd, packed, *refs):
        del before, packed
        rows_kernel(grid_shape, field, coeff, even, odd, even, odd, None, None, *refs)

    def rows_second(before, field, coeff, even, odd, even_edge, odd_edge, packed, *refs):
        del before, packed
        rows_kernel(grid_shape, field, coeff, even, odd, even_edge, odd_edge, *refs)

    def own_first(field, coeff, shifts, table, entry, out, ends, *pads):
        own_kernel(grid_shape, field, coeff, shifts, table, entry, out, ends, *pads)

    def own_second(field, coeff, shifts, table, entry, out, *pads):
        own_kernel(grid_shape, field, coeff, shifts, table, entry, out, None, *pads)

    rows0 = swap(*edge_rows(right_side, coefficient), "gy")
    w_own, ends = on_tensor_core(
        own_first, "own_first", (right_side, coefficient), scalars, (full, sums_of(2)), own_pads, 6
    )
    packed = pack(right_side, *rows0, ends, True)
    cols0 = swap(*packed, "gx")
    w_rows, products = on_tensor_core(
        rows_first, "rows_first", (w_own, right_side, coefficient, *rows0, packed[0]), scalars,
        (full, sums_of(3)), row_pads, 3, True,
    )
    w_vec, sums, even, odd = on_tensor_core(
        bind(first_kernel), "first_apply", (w_rows, right_side, coefficient, *cols0, products),
        scalars, (full, sums_of(3), edge, edge), side_pads, 3, True,
    )
    rows1 = swap(even, odd, "gy")
    (n_own,) = on_tensor_core(
        own_second, "own_second", (w_vec, coefficient), scalars, (full,), own_pads, 6
    )
    packed = pack(w_vec, *rows1, n_own, False)
    cols1 = swap(*packed, "gx")
    n_rows, products = on_tensor_core(
        rows_second, "rows_second",
        (n_own, w_vec, coefficient, *rows1, *rows0, packed[0], right_side, sums), scalars,
        (full, sums_of(6)), row_pads, 3, True,
    )
    n_vec, parts = on_tensor_core(
        bind(second_kernel), "second_apply",
        (n_rows, right_side, w_vec, coefficient, *cols1, *cols0, products, sums), scalars,
        (full, jax.ShapeDtypeStruct((devices, LANES), jnp.float32)), side_pads, 3, True,
    )
    gathered = lax.all_to_all(parts, ("gx", "gy"), 0, 0, tiled=True)
    return pl.pallas_call(
        last_kernel,
        out_shape=(full, full),
        in_specs=[VMEM_SPEC] * 4,
        out_specs=(pl.BlockSpec(memory_space=pltpu.HBM),) * 2,
        scratch_shapes=[
            pltpu.VMEM((layers, rows, cols), jnp.float32),
            pltpu.VMEM((layers, rows, cols), jnp.float32),
            pltpu.SemaphoreType.DMA((2, layers, PIECES)),
        ],
        compiler_params=pltpu.CompilerParams(vmem_limit_bytes=VMEM_BYTES),
        name="last_update",
    )(gathered, right_side, w_vec, n_vec)


def solution(mesh):
    placed = (P(None, "gy", "gx"), P(None, "gy", "gx"), P(), P(), P())
    return jax.shard_map(
        on_device,
        mesh=mesh,
        in_specs=placed,
        out_specs=(P(None, "gy", "gx"), P(None, "gy", "gx")),
        check_vma=False,
    )
```

```python
import jax
import jax.numpy as jnp
from jax import lax
from jax.experimental import pallas as pl
from jax.experimental.pallas import tpu as pltpu
from jax.sharding import PartitionSpec as P

REACH = 64
LANES = 128
HALF = 64
CHUNK = 32
UNROLL = 8
PIECES = 4
VMEM_BYTES = 32 * 1024 * 1024
EDGE_BYTES = 60 * 1024 * 1024
VMEM_SPEC = pl.BlockSpec(memory_space=pltpu.VMEM)
SMEM_SPEC = pl.BlockSpec(memory_space=pltpu.SMEM)


def even_swap(count):
    return [(i, i ^ 1) for i in range(count)]


def odd_swap(count):
    return [(i, i + 1 if i % 2 else i - 1) for i in range(1, count - 1)]


def is_odd(axis):
    return lax.rem(lax.axis_index(axis), 2) == 1


def swap(even, odd, axis):
    count = lax.axis_size(axis)
    return (
        lax.ppermute(even, axis, even_swap(count)),
        lax.ppermute(odd, axis, odd_swap(count)),
    )


def lane_of(shape):
    return lax.broadcasted_iota(jnp.int32, shape, 1)


def pack_columns(first, second, high):
    low_lanes = lane_of(first.shape) < HALF
    turned = pltpu.roll(second, HALF, 1)
    if high:
        return jnp.where(low_lanes, turned, first)
    return jnp.where(low_lanes, first, turned)


def packed_edges(load, cols):
    edges = (slice(0, LANES), slice(cols - LANES, cols))
    return [pack_columns(load(0, edge), load(1, edge), high) for high, edge in enumerate(edges)]


def store_packed(even_ref, odd_ref, start, low, high):
    odd = is_odd("gx")
    rows = low.shape[0]
    even_ref[start : start + rows, :] = jnp.where(odd, low, high)
    odd_ref[start : start + rows, :] = jnp.where(odd, high, low)


def pack_sides_kernel(with_ends, field, after, even_out, odd_out):
    rows, cols = field.shape[1:]
    low, high = packed_edges(lambda layer, edge: field[layer, :, edge], cols)
    store_packed(even_out, odd_out, 0, low, high)
    if with_ends:
        store_packed(even_out, odd_out, rows, after[0], after[1])


def pack_corners_kernel(even_rows, odd_rows, even_out, odd_out):
    cols = even_rows.shape[2]
    odd_y = is_odd("gy")
    for start, above in ((0, True), (REACH, False)):

        def halo(layer, edge, above=above):
            even = even_rows[layer, 0:REACH, edge]
            other = odd_rows[layer, 0:REACH, edge]
            return jnp.where(odd_y == above, even, other)

        store_packed(even_out, odd_out, start, *packed_edges(halo, cols))


def pack(kernel, operands, rows, name):
    out = jax.ShapeDtypeStruct((rows, LANES), jnp.float32)
    return pl.pallas_call(
        kernel,
        out_shape=(out, out),
        in_specs=[VMEM_SPEC] * len(operands),
        out_specs=(VMEM_SPEC,) * 2,
        compiler_params=pltpu.CompilerParams(vmem_limit_bytes=VMEM_BYTES),
        name=name,
    )(*operands)


def pack_sides(field, after, with_ends):
    def kernel(*refs):
        pack_sides_kernel(with_ends, *refs)

    return pack(kernel, (field, after), field.shape[1] + (8 if with_ends else 0), "pack_sides")


def pack_corners(even_rows, odd_rows):
    return pack(pack_corners_kernel, (even_rows, odd_rows), 2 * REACH, "pack_corners")


def edge_kernel(field, coeff, even_out, odd_out, sems):
    rows = field.shape[1]
    odd_y = is_odd("gy")
    copies = []
    for index, (out, at_top) in enumerate(((even_out, odd_y), (odd_out, jnp.logical_not(odd_y)))):
        for part, (source, place, depth) in enumerate(((field, 0, REACH), (coeff, REACH, 8))):
            start = pl.multiple_of(jnp.where(at_top, 0, rows - depth), 8)
            copies.append(
                pltpu.make_async_copy(
                    source.at[:, pl.ds(start, depth), :],
                    out.at[:, pl.ds(place, depth), :],
                    sems.at[index, part],
                )
            )
    for copy in copies:
        copy.start()
    for copy in copies:
        copy.wait()


def edge_rows(field, coeff):
    layers, _, cols = field.shape
    out = jax.ShapeDtypeStruct((layers, REACH + 8, cols), jnp.float32)
    return pl.pallas_call(
        edge_kernel,
        out_shape=(out, out),
        in_specs=[pl.BlockSpec(memory_space=pltpu.HBM)] * 2,
        out_specs=(VMEM_SPEC,) * 2,
        scratch_shapes=[pltpu.SemaphoreType.DMA((2, 2))],
        compiler_params=pltpu.CompilerParams(vmem_limit_bytes=EDGE_BYTES),
        name="edge_rows",
    )(field, coeff)


def zero_rim(pad, depth, rows):
    tiles = pad.shape[1]
    for layer in range(2):
        for tile in range(tiles):
            if tile in (0, tiles - 1):
                pad[layer, tile] = jnp.zeros(pad.shape[2:], jnp.float32)
            else:
                pad[layer, tile, 0:depth, :] = jnp.zeros((depth, LANES), jnp.float32)
                pad[layer, tile, depth + rows :, :] = jnp.zeros((depth, LANES), jnp.float32)


def fill_own(pad, depth, field):
    rows, cols = field.shape[1:]
    for layer in range(2):
        for tile in range(cols // LANES):
            lanes = slice(tile * LANES, (tile + 1) * LANES)
            pad[layer, 1 + tile, depth : depth + rows, :] = field[layer, :, lanes]


def neighbours_across(load, tiles):
    lane = lane_of((CHUNK, LANES))
    values = [load(tile) for tile in range(tiles + 2)]
    back = [pltpu.roll(value, 1, 1) for value in values[:-1]]
    ahead = [pltpu.roll(value, LANES - 1, 1) for value in values[1:]]
    left = [jnp.where(lane == 0, back[i], back[i + 1]) for i in range(tiles)]
    right = [jnp.where(lane == LANES - 1, ahead[i + 1], ahead[i]) for i in range(tiles)]
    return values[1:-1], left, right


def apply_chunk(layer, row, pad, coeff_pad, shifts, weight, grid_shape, tile_shape):
    dirs = shifts.shape[0]
    rows, cols = tile_shape
    tiles = cols // LANES
    other = 1 - layer
    lane = lane_of((CHUNK, LANES))
    row_at = lax.broadcasted_iota(jnp.int32, (CHUNK, LANES), 0)
    first_row = lax.axis_index("gy") * rows + row
    first_col = lax.axis_index("gx") * cols

    def field_at(tile):
        return pad[layer, tile, pl.ds(REACH + row, CHUNK), :]

    def coeff_at(tile):
        return coeff_pad[layer, tile, pl.ds(8 + row, CHUNK), :]

    own, left, right = neighbours_across(field_at, tiles)
    own_c, left_c, right_c = neighbours_across(coeff_at, tiles)
    result = []
    for tile in range(tiles):
        value, coeff = own[tile], own_c[tile]
        above = pad[layer, 1 + tile, pl.ds(REACH - 1 + row, CHUNK), :]
        below = pad[layer, 1 + tile, pl.ds(REACH + 1 + row, CHUNK), :]
        above_c = coeff_pad[layer, 1 + tile, pl.ds(7 + row, CHUNK), :]
        below_c = coeff_pad[layer, 1 + tile, pl.ds(9 + row, CHUNK), :]
        total = (coeff + above_c) * (value - above) + (coeff + below_c) * (value - below)
        total += (coeff + left_c[tile]) * (value - left[tile])
        total += (coeff + right_c[tile]) * (value - right[tile])
        result.append(weight * total)
    for direction in range(dirs):
        shift_r, shift_c = shifts[direction, layer, 0], shifts[direction, layer, 1]
        start_r = REACH + row + shifts[direction, other, 0] - shift_r
        start_c = LANES + shifts[direction, other, 1] - shift_c
        skip = lax.shift_right_logical(start_c, 7)
        turn = jnp.bitwise_and(start_c, LANES - 1)
        back = jnp.bitwise_and(LANES - turn, LANES - 1)
        moved = [
            pltpu.roll(pad[other, skip + tile, pl.ds(start_r, CHUNK), :], back, 1)
            for tile in range(tiles + 1)
        ]
        here = lane < LANES - turn
        image_row = row_at + (first_row - shift_r)
        inside = (image_row >= 0) & (image_row < grid_shape[0])
        for tile in range(tiles):
            mask = inside
            if tile == 0:
                mask = mask & (lane >= shift_c - first_col)
            if tile == tiles - 1:
                mask = mask & (lane < grid_shape[1] + shift_c - first_col - tile * LANES)
            value = own[tile] + jnp.where(here, moved[tile], moved[tile + 1])
            result[tile] = result[tile] + jnp.where(mask, value, 0.0)
    return result


def fold(parts):
    total = sum(parts[1:], parts[0])
    pieces = [total[8 * i : 8 * i + 8] for i in range(total.shape[0] // 8)]
    return sum(pieces[1:], pieces[0])


def dot_of(first, second):
    return fold([a * b for a, b in zip(first, second, strict=True)])


def weight_of(table, entry, layer):
    return 0.5 * table[entry[layer]]


def pack_ends(coeff, ends):
    rows, cols = coeff.shape[1:]
    lane = lane_of((8, LANES))
    for high, edge in enumerate((slice(0, LANES), slice(cols - LANES, cols))):
        packed = jnp.zeros((8, LANES), jnp.float32)
        for layer in range(2):
            for group in range(rows // 8):
                at = layer * (rows // 8) + group
                turn = (at + high) % LANES
                value = coeff[layer, 8 * group : 8 * group + 8, edge]
                value = pltpu.roll(value, turn, 1) if turn else value
                packed = jnp.where(lane == at, value, packed)
        ends[high] = packed


def own_kernel(grid_shape, field, coeff, shifts, table, entry, out, ends, pad, coeff_pad):
    rows, cols = field.shape[1:]
    zero_rim(pad, REACH, rows)
    zero_rim(coeff_pad, 8, rows)
    fill_own(pad, REACH, field)
    fill_own(coeff_pad, 8, coeff)
    if ends is not None:
        pack_ends(coeff, ends)
    for layer in range(2):
        weight = weight_of(table, entry, layer)

        def step(i, carry, layer=layer, weight=weight):
            row = pl.multiple_of(i * CHUNK, CHUNK)
            result = apply_chunk(
                layer, row, pad, coeff_pad, shifts, weight, grid_shape, (rows, cols)
            )
            for tile, value in enumerate(result):
                out[layer, pl.ds(row, CHUNK), tile * LANES : (tile + 1) * LANES] = value
            return carry

        lax.fori_loop(0, rows // CHUNK, step, 0, unroll=UNROLL)


def products_of(own, result, base, fit):
    if base is None:
        pairs = ((own, own), (own, result), (result, result))
    else:
        rest = [a - fit * b for a, b in zip(base, own, strict=True)]
        slope = [a - fit * b for a, b in zip(own, result, strict=True)]
        pairs = (
            (rest, rest), (rest, own), (slope, rest), (result, rest), (slope, own), (result, own),
        )
    return tuple(dot_of(*pair) for pair in pairs)


def fit_of(sums):
    gamma, delta, omega = (jnp.sum(sums[index], keepdims=True) for index in range(3))
    fit = jnp.where(omega > 0.0, delta / jnp.where(omega > 0.0, omega, 1.0), 0.0)
    return gamma, delta, omega, jnp.clip(fit, -1.0, 1.0)


def rows_kernel(
    grid_shape, field, coeff, even_rows, odd_rows, even_edge, odd_edge, base, sums, shifts,
    table, entry, out, products, pad,
):
    rows, cols = field.shape[1:]
    tiles = cols // LANES
    odd_y = is_odd("gy")
    first_row = lax.axis_index("gy") * rows
    first_col = lax.axis_index("gx") * cols
    zeros = jnp.zeros((REACH, LANES), jnp.float32)
    for layer in range(2):
        for side in range(2):
            for tile in (0, tiles + 1):
                pad[layer, side, tile, 0:REACH, :] = zeros
                pad[layer, side, tile, REACH:, :] = zeros
        for tile in range(tiles):
            lanes = slice(tile * LANES, (tile + 1) * LANES)
            even = even_rows[layer, 0:REACH, lanes]
            other = odd_rows[layer, 0:REACH, lanes]
            pad[layer, 0, 1 + tile, 0:REACH, :] = jnp.where(odd_y, even, other)
            pad[layer, 0, 1 + tile, REACH:, :] = zeros
            pad[layer, 1, 1 + tile, 0:REACH, :] = zeros
            pad[layer, 1, 1 + tile, REACH:, :] = jnp.where(odd_y, other, even)
    lane = lane_of((CHUNK, LANES))
    row_at = lax.broadcasted_iota(jnp.int32, (CHUNK, LANES), 0)
    for layer in range(2):
        other_layer = 1 - layer

        def step(i, carry, layer=layer, other_layer=other_layer):
            part = pl.multiple_of(i * CHUNK, CHUNK)
            totals = [[jnp.zeros((CHUNK, LANES), jnp.float32)] * tiles for _ in range(2)]
            for direction in range(shifts.shape[0]):
                shift_r, shift_c = shifts[direction, layer, 0], shifts[direction, layer, 1]
                step_r = shifts[direction, other_layer, 0] - shift_r
                start_c = LANES + shifts[direction, other_layer, 1] - shift_c
                side = jnp.where(step_r < 0, 0, 1)
                start_r = part + step_r + jnp.where(step_r < 0, REACH, 0)
                row = part + jnp.where(step_r < 0, 0, rows - REACH)
                skip = lax.shift_right_logical(start_c, 7)
                turn = jnp.bitwise_and(start_c, LANES - 1)
                back = jnp.bitwise_and(LANES - turn, LANES - 1)
                moved = [
                    pltpu.roll(
                        pad[other_layer, side, skip + tile, pl.ds(start_r, CHUNK), :], back, 1
                    )
                    for tile in range(tiles + 1)
                ]
                here = lane < LANES - turn
                image_row = row_at + (first_row + row - shift_r)
                inside = (image_row >= 0) & (image_row < grid_shape[0])
                upper = inside & (jnp.full((CHUNK, LANES), side, jnp.int32) == 0)
                lower = inside & (jnp.full((CHUNK, LANES), side, jnp.int32) == 1)
                for tile in range(tiles):
                    value = jnp.where(here, moved[tile], moved[tile + 1])
                    if tile == 0:
                        value = jnp.where(lane >= shift_c - first_col, value, 0.0)
                    if tile == tiles - 1:
                        last = grid_shape[1] + shift_c - first_col - tile * LANES
                        value = jnp.where(lane < last, value, 0.0)
                    totals[0][tile] = totals[0][tile] + jnp.where(upper, value, 0.0)
                    totals[1][tile] = totals[1][tile] + jnp.where(lower, value, 0.0)
            for side, base in enumerate((0, rows - REACH)):
                for tile in range(tiles):
                    lanes = slice(tile * LANES, (tile + 1) * LANES)
                    out[layer, pl.ds(base + part, CHUNK), lanes] += totals[side][tile]
            return carry

        lax.fori_loop(0, REACH // CHUNK, step, 0)
        weight = weight_of(table, entry, layer)
        at = lax.broadcasted_iota(jnp.int32, (8, cols), 0)
        even = even_edge[layer, REACH : REACH + 8, :]
        other = odd_edge[layer, REACH : REACH + 8, :]
        even_v = [even_rows[layer, start : start + 8, :] for start in (0, REACH - 8)]
        other_v = [odd_rows[layer, start : start + 8, :] for start in (0, REACH - 8)]
        for start, edge_c, edge_v, spot, source in (
            (0, jnp.where(odd_y, even, other), jnp.where(odd_y, even_v[1], other_v[1]), 0, 1),
            (
                rows - 8, jnp.where(odd_y, other, even), jnp.where(odd_y, other_v[0], even_v[0]),
                7, 7,
            ),
        ):
            edge_c = pltpu.roll(edge_c, source, 0)
            edge_v = pltpu.roll(edge_v, source, 0)
            value = field[layer, start : start + 8, :]
            own_c = coeff[layer, start : start + 8, :]
            extra = weight * (edge_c * value - (own_c + edge_c) * edge_v)
            out[layer, start : start + 8, :] += jnp.where(at == spot, extra, 0.0)
    fit = None if base is None else fit_of(sums)[3]
    carry = (jnp.zeros((8, LANES), jnp.float32),) * products.shape[0]
    inner = [slice(tile * LANES, (tile + 1) * LANES) for tile in range(1, tiles - 1)]
    for layer in range(2):

        def add(i, carry, layer=layer):
            chunk = pl.ds(pl.multiple_of(i * CHUNK, CHUNK), CHUNK)
            start, own, result = (
                None if ref is None else [ref[layer, chunk, lanes] for lanes in inner]
                for ref in (base, field, out)
            )
            more = products_of(own, result, start, fit)
            return tuple(a + b for a, b in zip(carry, more, strict=True))

        carry = lax.fori_loop(0, rows // CHUNK, add, carry, unroll=UNROLL)
    for index, value in enumerate(carry):
        products[index] = value


def finish_chunk(grid_shape, layer, row, field, coeff, out, pad, ends, shifts, weight):
    rows, cols = field.shape[1:]
    tiles = cols // LANES
    first_row = lax.axis_index("gy") * rows + row
    first_col = lax.axis_index("gx") * cols
    lane = lane_of((CHUNK, LANES))
    row_at = lax.broadcasted_iota(jnp.int32, (CHUNK, LANES), 0)
    cut = (slice(0, LANES), slice(cols - LANES, cols))
    own = [field[layer, pl.ds(row, CHUNK), lanes] for lanes in cut]
    result = []
    for side, spot in ((0, 0), (1, LANES - 1)):
        at = layer * (rows // 8) + lax.shift_right_logical(row, 3)
        edge_c = jnp.concatenate(
            [
                pltpu.roll(ends[side], jnp.bitwise_and(LANES + spot - at - i, LANES - 1), 1)
                for i in range(CHUNK // 8)
            ]
        )
        edge_v = pad[layer, side, pl.ds(REACH + row, CHUNK), :]
        edge_v = pltpu.roll(edge_v, LANES - 1 if side else 1, 1)
        own_c = coeff[layer, pl.ds(row, CHUNK), cut[side]]
        extra = weight * (edge_c * own[side] - (own_c + edge_c) * edge_v)
        extra = jnp.where(lane == spot, extra, 0.0)
        result.append(out[layer, pl.ds(row, CHUNK), cut[side]] + extra)
    for direction in range(shifts.shape[0]):
        shift_r, shift_c = shifts[direction, layer, 0], shifts[direction, layer, 1]
        start_r = REACH + row + shifts[direction, 1 - layer, 0] - shift_r
        step_c = shifts[direction, 1 - layer, 1] - shift_c
        side = jnp.where(step_c < 0, 0, 1)
        back = jnp.bitwise_and(LANES - step_c, LANES - 1)
        moved = pltpu.roll(pad[1 - layer, side, pl.ds(start_r, CHUNK), :], back, 1)
        image_row = row_at + (first_row - shift_r)
        moved = jnp.where((image_row >= 0) & (image_row < grid_shape[0]), moved, 0.0)
        low, low_end = shift_c - first_col, jnp.where(step_c < 0, -step_c, 0)
        high = jnp.where(step_c < 0, LANES, LANES - step_c)
        high_end = grid_shape[1] + shift_c - first_col - (tiles - 1) * LANES
        result[0] = result[0] + jnp.where((lane >= low) & (lane < low_end), moved, 0.0)
        result[1] = result[1] + jnp.where((lane >= high) & (lane < high_end), moved, 0.0)
    for side in range(2):
        out[layer, pl.ds(row, CHUNK), cut[side]] = result[side]
    return own, result


def finish(
    grid_shape, base, fit, field, coeff, even_cols, odd_cols, even_corners, odd_corners, even_ends,
    odd_ends, products, shifts, table, entry, out, pad,
):
    rows, cols = field.shape[1:]
    odd_x = is_odd("gx")
    for even_ref, odd_ref, start, place, depth in (
        (even_cols, odd_cols, 0, REACH, rows),
        (even_corners, odd_corners, 0, 0, REACH),
        (even_corners, odd_corners, REACH, REACH + rows, REACH),
    ):
        even, other = even_ref[start : start + depth, :], odd_ref[start : start + depth, :]
        for side, packed in ((0, jnp.where(odd_x, even, other)), (1, jnp.where(odd_x, other, even))):
            pad[0, side, place : place + depth, :] = packed
            pad[1, side, place : place + depth, :] = pltpu.roll(packed, HALF, 1)
    even, other = even_ends[rows : rows + 8, :], odd_ends[rows : rows + 8, :]
    ends = (jnp.where(odd_x, even, other), jnp.where(odd_x, other, even))
    cut = (slice(0, LANES), slice(cols - LANES, cols))
    carry = tuple(products[index] for index in range(products.shape[0]))
    for layer in range(2):
        weight = weight_of(table, entry, layer)

        def step(i, carry, layer=layer, weight=weight):
            row = pl.multiple_of(i * CHUNK, CHUNK)
            own, result = finish_chunk(
                grid_shape, layer, row, field, coeff, out, pad, ends, shifts, weight
            )
            chunk = pl.ds(row, CHUNK)
            start = None if base is None else [base[layer, chunk, lanes] for lanes in cut]
            more = products_of(own, result, start, fit)
            return tuple(a + b for a, b in zip(carry, more, strict=True))

        carry = lax.fori_loop(0, rows // CHUNK, step, carry, unroll=UNROLL)
    return carry


def first_kernel(
    grid_shape, before, field, coeff, even_cols, odd_cols, even_corners, odd_corners, products,
    shifts, table, entry, out, sums, even_out, odd_out, pad,
):
    del before
    rows = field.shape[1]
    carry = finish(
        grid_shape, None, None, field, coeff, even_cols, odd_cols, even_corners, odd_corners, even_cols,
        odd_cols, products, shifts, table, entry, out, pad,
    )
    for index, value in enumerate(carry):
        sums[index] = value
    odd_y = is_odd("gy")
    low, high = out[:, 0:REACH, :], out[:, rows - REACH :, :]
    even_out[...] = jnp.where(odd_y, low, high)
    odd_out[...] = jnp.where(odd_y, high, low)


def second_kernel(
    grid_shape, before, base, field, coeff, even_cols, odd_cols, even_corners, odd_corners, even_ends,
    odd_ends, products, sums, shifts, table, entry, out, parts, pad,
):
    del before
    gamma, delta, omega, fit = fit_of(sums)
    carry = finish(
        grid_shape, base, fit, field, coeff, even_cols, odd_cols, even_corners, odd_corners, even_ends,
        odd_ends, products, shifts, table, entry, out, pad,
    )
    rest2, rest_w, slope_rest, n_rest, slope_w, n_w = (
        jnp.sum(value, keepdims=True) for value in carry
    )
    lane = lane_of((8, LANES))
    row = jnp.zeros((8, LANES), jnp.float32)
    for at, value in (
        (0, rest2), (1, slope_rest), (8, 2.0 * rest_w), (9, n_rest + slope_w),
        (16, omega), (17, n_w), (24, fit), (25, fit), (32, gamma), (33, delta),
    ):
        row = jnp.where(lane == at, value, row)
    for start in range(0, parts.shape[0], 8):
        parts[start : start + 8, :] = row


def pick(row, lane, at):
    return jnp.sum(jnp.where(lane == at, row, 0.0), keepdims=True)


def last_kernel(
    parts, base, w_vec, n_vec, solution_out, residual_out, solution_part, residual_part, sems
):
    gathered = parts[...]
    count = gathered.shape[0]
    lane = lane_of((8, LANES))
    total = sum(gathered[8 * i : 8 * i + 8] for i in range(count // 8))
    gamma, delta = pick(total, lane, 32), pick(total, lane, 33)
    alpha = gamma / delta
    gap = alpha - pltpu.roll(gathered, LANES - 24, 1)
    moved = gathered - gap * pltpu.roll(gathered, LANES - 8, 1)
    moved = moved + gap * gap * pltpu.roll(gathered, LANES - 16, 1)
    total = sum(moved[8 * i : 8 * i + 8] for i in range(count // 8))
    gamma_next, delta_next = pick(total, lane, 0), pick(total, lane, 1)
    beta = gamma_next / gamma
    alpha_next = gamma_next / (delta_next - beta * gamma_next / alpha)
    layers, rows = base.shape[:2]
    depth = rows // PIECES
    copies = []
    for layer in range(layers):
        for piece in range(PIECES):
            part = pl.ds(piece * depth, depth)
            start, w_start = base[layer, part, :], w_vec[layer, part, :]
            residual = start - alpha * w_start
            w_next = w_start - alpha * n_vec[layer, part, :]
            solution_part[layer, part, :] = alpha * start + alpha_next * (residual + beta * start)
            residual_part[layer, part, :] = residual - alpha_next * (w_next + beta * w_start)
            for which, (source, target) in enumerate(
                ((solution_part, solution_out), (residual_part, residual_out))
            ):
                copy = pltpu.make_async_copy(
                    source.at[layer, part, :],
                    target.at[layer, part, :],
                    sems.at[which, layer, piece],
                )
                copy.start()
                copies.append(copy)
    for copy in copies:
        copy.wait()


def on_tensor_core(kernel, name, operands, scalars, out_shape, scratch, microseconds, in_place=False):
    return pl.pallas_call(
        kernel,
        out_shape=out_shape,
        in_specs=[VMEM_SPEC] * len(operands) + [SMEM_SPEC] * len(scalars),
        out_specs=(VMEM_SPEC,) * len(out_shape),
        scratch_shapes=[pltpu.VMEM(shape, jnp.float32) for shape in scratch],
        input_output_aliases={0: 0} if in_place else {},
        compiler_params=pltpu.CompilerParams(vmem_limit_bytes=VMEM_BYTES),
        cost_estimate=pl.CostEstimate(
            flops=0, bytes_accessed=3_000_000 * microseconds, transcendentals=0
        ),
        name=name,
    )(*operands, *scalars)


def on_device(right_side, coefficient, strength_table, layer_entry, shifts):
    layers, rows, cols = right_side.shape
    count_y, count_x = lax.axis_size("gy"), lax.axis_size("gx")
    devices = count_x * count_y
    tiles = cols // LANES
    grid_shape = (rows * count_y, cols * count_x)
    full = jax.ShapeDtypeStruct((layers, rows, cols), jnp.float32)
    edge = jax.ShapeDtypeStruct((layers, REACH, cols), jnp.float32)
    scalars = (shifts, strength_table, layer_entry)
    own_pads = [(2, tiles + 2, rows + 2 * REACH, LANES), (2, tiles + 2, rows + 16, LANES)]
    row_pads = [(2, 2, tiles + 2, 2 * REACH, LANES)]
    side_pads = [(2, 2, rows + 2 * REACH, LANES)]

    def sums_of(count):
        return jax.ShapeDtypeStruct((count, 8, LANES), jnp.float32)

    def bind(kernel):
        def bound(*refs):
            kernel(grid_shape, *refs)

        return bound

    def rows_first(before, field, coeff, even, odd, packed, *refs):
        del before, packed
        rows_kernel(grid_shape, field, coeff, even, odd, even, odd, None, None, *refs)

    def rows_second(before, field, coeff, even, odd, even_edge, odd_edge, packed, *refs):
        del before, packed
        rows_kernel(grid_shape, field, coeff, even, odd, even_edge, odd_edge, *refs)

    def own_first(field, coeff, shifts, table, entry, out, ends, *pads):
        own_kernel(grid_shape, field, coeff, shifts, table, entry, out, ends, *pads)

    def own_second(field, coeff, shifts, table, entry, out, *pads):
        own_kernel(grid_shape, field, coeff, shifts, table, entry, out, None, *pads)

    rows0 = swap(*edge_rows(right_side, coefficient), "gy")
    w_own, ends = on_tensor_core(
        own_first, "own_first", (right_side, coefficient), scalars, (full, sums_of(2)), own_pads, 6
    )
    cols0 = swap(*pack_sides(right_side, ends, True), "gx")
    packed = pack_corners(*rows0)
    corners0 = swap(*packed, "gx")
    w_rows, products = on_tensor_core(
        rows_first, "rows_first", (w_own, right_side, coefficient, *rows0, packed[0]), scalars,
        (full, sums_of(3)), row_pads, 3, True,
    )
    w_vec, sums, even, odd = on_tensor_core(
        bind(first_kernel), "first_apply",
        (w_rows, right_side, coefficient, *cols0, *corners0, products), scalars,
        (full, sums_of(3), edge, edge), side_pads, 3, True,
    )
    rows1 = swap(even, odd, "gy")
    (n_own,) = on_tensor_core(
        own_second, "own_second", (w_vec, coefficient), scalars, (full,), own_pads, 6
    )
    cols1 = swap(*pack_sides(w_vec, n_own, False), "gx")
    packed = pack_corners(*rows1)
    corners1 = swap(*packed, "gx")
    n_rows, products = on_tensor_core(
        rows_second, "rows_second",
        (n_own, w_vec, coefficient, *rows1, *rows0, packed[0], right_side, sums), scalars,
        (full, sums_of(6)), row_pads, 3, True,
    )
    n_vec, parts = on_tensor_core(
        bind(second_kernel), "second_apply",
        (n_rows, right_side, w_vec, coefficient, *cols1, *corners1, *cols0, products, sums), scalars,
        (full, jax.ShapeDtypeStruct((devices, LANES), jnp.float32)), side_pads, 3, True,
    )
    gathered = lax.all_to_all(parts, ("gx", "gy"), 0, 0, tiled=True)
    return pl.pallas_call(
        last_kernel,
        out_shape=(full, full),
        in_specs=[VMEM_SPEC] * 4,
        out_specs=(pl.BlockSpec(memory_space=pltpu.HBM),) * 2,
        scratch_shapes=[
            pltpu.VMEM((layers, rows, cols), jnp.float32),
            pltpu.VMEM((layers, rows, cols), jnp.float32),
            pltpu.SemaphoreType.DMA((2, layers, PIECES)),
        ],
        compiler_params=pltpu.CompilerParams(vmem_limit_bytes=VMEM_BYTES),
        name="last_update",
    )(gathered, right_side, w_vec, n_vec)


def solution(mesh):
    placed = (P(None, "gy", "gx"), P(None, "gy", "gx"), P(), P(), P())
    return jax.shard_map(
        on_device,
        mesh=mesh,
        in_specs=placed,
        out_specs=(P(None, "gy", "gx"), P(None, "gy", "gx")),
        check_vma=False,
    )
```

```python
import jax
import jax.numpy as jnp
from jax import lax
from jax.experimental import pallas as pl
from jax.experimental.pallas import tpu as pltpu
from jax.sharding import PartitionSpec as P

REACH = 64
LANES = 128
HALF = 64
CHUNK = 32
UNROLL = 8
PIECES = 4
VMEM_BYTES = 32 * 1024 * 1024
EDGE_BYTES = 53 * 1024 * 1024
VMEM_SPEC = pl.BlockSpec(memory_space=pltpu.VMEM)
SMEM_SPEC = pl.BlockSpec(memory_space=pltpu.SMEM)


def even_swap(count):
    return [(i, i ^ 1) for i in range(count)]


def odd_swap(count):
    return [(i, i + 1 if i % 2 else i - 1) for i in range(1, count - 1)]


def is_odd(axis):
    return lax.rem(lax.axis_index(axis), 2) == 1


def swap(even, odd, axis):
    count = lax.axis_size(axis)
    return (
        lax.ppermute(even, axis, even_swap(count)),
        lax.ppermute(odd, axis, odd_swap(count)),
    )


def lane_of(shape):
    return lax.broadcasted_iota(jnp.int32, shape, 1)


def pack_columns(first, second, high):
    low_lanes = lane_of(first.shape) < HALF
    turned = pltpu.roll(second, HALF, 1)
    if high:
        return jnp.where(low_lanes, turned, first)
    return jnp.where(low_lanes, first, turned)


def packed_edges(load, cols):
    edges = (slice(0, LANES), slice(cols - LANES, cols))
    return [pack_columns(load(0, edge), load(1, edge), high) for high, edge in enumerate(edges)]


def store_packed(even_ref, odd_ref, start, low, high):
    odd = is_odd("gx")
    rows = low.shape[0]
    even_ref[start : start + rows, :] = jnp.where(odd, low, high)
    odd_ref[start : start + rows, :] = jnp.where(odd, high, low)


def pack_sides_kernel(with_ends, field, after, even_out, odd_out):
    rows, cols = field.shape[1:]
    low, high = packed_edges(lambda layer, edge: field[layer, :, edge], cols)
    store_packed(even_out, odd_out, 0, low, high)
    if with_ends:
        store_packed(even_out, odd_out, rows, after[0], after[1])


def pack_corners_kernel(even_rows, odd_rows, even_out, odd_out):
    cols = even_rows.shape[2]
    odd_y = is_odd("gy")
    for start, above in ((0, True), (REACH, False)):

        def halo(layer, edge, above=above):
            even = even_rows[layer, 0:REACH, edge]
            other = odd_rows[layer, 0:REACH, edge]
            return jnp.where(odd_y == above, even, other)

        store_packed(even_out, odd_out, start, *packed_edges(halo, cols))


def pack(kernel, operands, rows, name):
    out = jax.ShapeDtypeStruct((rows, LANES), jnp.float32)
    return pl.pallas_call(
        kernel,
        out_shape=(out, out),
        in_specs=[VMEM_SPEC] * len(operands),
        out_specs=(VMEM_SPEC,) * 2,
        compiler_params=pltpu.CompilerParams(vmem_limit_bytes=VMEM_BYTES),
        name=name,
    )(*operands)


def pack_sides(field, after, with_ends):
    def kernel(*refs):
        pack_sides_kernel(with_ends, *refs)

    return pack(kernel, (field, after), field.shape[1] + (8 if with_ends else 0), "pack_sides")


def pack_corners(even_rows, odd_rows):
    return pack(pack_corners_kernel, (even_rows, odd_rows), 2 * REACH, "pack_corners")


def edge_kernel(field, coeff, even_out, odd_out, sems):
    rows = field.shape[1]
    odd_y = is_odd("gy")
    copies = []
    for index, (out, at_top) in enumerate(((even_out, odd_y), (odd_out, jnp.logical_not(odd_y)))):
        for part, (source, place, depth) in enumerate(((field, 0, REACH), (coeff, REACH, 8))):
            start = pl.multiple_of(jnp.where(at_top, 0, rows - depth), 8)
            copies.append(
                pltpu.make_async_copy(
                    source.at[:, pl.ds(start, depth), :],
                    out.at[:, pl.ds(place, depth), :],
                    sems.at[index, part],
                )
            )
    for copy in copies:
        copy.start()
    for copy in copies:
        copy.wait()


def edge_rows(field, coeff):
    layers, _, cols = field.shape
    out = jax.ShapeDtypeStruct((layers, REACH + 8, cols), jnp.float32)
    return pl.pallas_call(
        edge_kernel,
        out_shape=(out, out),
        in_specs=[pl.BlockSpec(memory_space=pltpu.HBM)] * 2,
        out_specs=(VMEM_SPEC,) * 2,
        scratch_shapes=[pltpu.SemaphoreType.DMA((2, 2))],
        compiler_params=pltpu.CompilerParams(vmem_limit_bytes=EDGE_BYTES),
        name="edge_rows",
    )(field, coeff)


def zero_rim(pad, depth, rows):
    tiles = pad.shape[1]
    for layer in range(2):
        for tile in range(tiles):
            if tile in (0, tiles - 1):
                pad[layer, tile] = jnp.zeros(pad.shape[2:], jnp.float32)
            else:
                pad[layer, tile, 0:depth, :] = jnp.zeros((depth, LANES), jnp.float32)
                pad[layer, tile, depth + rows :, :] = jnp.zeros((depth, LANES), jnp.float32)


def fill_own(pad, depth, field):
    rows, cols = field.shape[1:]
    for layer in range(2):
        for tile in range(cols // LANES):
            lanes = slice(tile * LANES, (tile + 1) * LANES)
            pad[layer, 1 + tile, depth : depth + rows, :] = field[layer, :, lanes]


def neighbours_across(load, tiles):
    lane = lane_of((CHUNK, LANES))
    values = [load(tile) for tile in range(tiles + 2)]
    back = [pltpu.roll(value, 1, 1) for value in values[:-1]]
    ahead = [pltpu.roll(value, LANES - 1, 1) for value in values[1:]]
    left = [jnp.where(lane == 0, back[i], back[i + 1]) for i in range(tiles)]
    right = [jnp.where(lane == LANES - 1, ahead[i + 1], ahead[i]) for i in range(tiles)]
    return values[1:-1], left, right


def apply_chunk(layer, row, pad, coeff_pad, shifts, weight, grid_shape, tile_shape):
    dirs = shifts.shape[0]
    rows, cols = tile_shape
    tiles = cols // LANES
    other = 1 - layer
    lane = lane_of((CHUNK, LANES))
    row_at = lax.broadcasted_iota(jnp.int32, (CHUNK, LANES), 0)
    first_row = lax.axis_index("gy") * rows + row
    first_col = lax.axis_index("gx") * cols

    def field_at(tile):
        return pad[layer, tile, pl.ds(REACH + row, CHUNK), :]

    def coeff_at(tile):
        return coeff_pad[layer, tile, pl.ds(8 + row, CHUNK), :]

    own, left, right = neighbours_across(field_at, tiles)
    own_c, left_c, right_c = neighbours_across(coeff_at, tiles)
    result = []
    for tile in range(tiles):
        value, coeff = own[tile], own_c[tile]
        above = pad[layer, 1 + tile, pl.ds(REACH - 1 + row, CHUNK), :]
        below = pad[layer, 1 + tile, pl.ds(REACH + 1 + row, CHUNK), :]
        above_c = coeff_pad[layer, 1 + tile, pl.ds(7 + row, CHUNK), :]
        below_c = coeff_pad[layer, 1 + tile, pl.ds(9 + row, CHUNK), :]
        total = (coeff + above_c) * (value - above) + (coeff + below_c) * (value - below)
        total += (coeff + left_c[tile]) * (value - left[tile])
        total += (coeff + right_c[tile]) * (value - right[tile])
        result.append(weight * total)
    for direction in range(dirs):
        shift_r, shift_c = shifts[direction, layer, 0], shifts[direction, layer, 1]
        start_r = REACH + row + shifts[direction, other, 0] - shift_r
        start_c = LANES + shifts[direction, other, 1] - shift_c
        skip = lax.shift_right_logical(start_c, 7)
        turn = jnp.bitwise_and(start_c, LANES - 1)
        back = jnp.bitwise_and(LANES - turn, LANES - 1)
        moved = [
            pltpu.roll(pad[other, skip + tile, pl.ds(start_r, CHUNK), :], back, 1)
            for tile in range(tiles + 1)
        ]
        here = lane < LANES - turn
        image_row = row_at + (first_row - shift_r)
        inside = (image_row >= 0) & (image_row < grid_shape[0])
        for tile in range(tiles):
            mask = inside
            if tile == 0:
                mask = mask & (lane >= shift_c - first_col)
            if tile == tiles - 1:
                mask = mask & (lane < grid_shape[1] + shift_c - first_col - tile * LANES)
            value = own[tile] + jnp.where(here, moved[tile], moved[tile + 1])
            result[tile] = result[tile] + jnp.where(mask, value, 0.0)
    return result


def fold(parts):
    total = sum(parts[1:], parts[0])
    pieces = [total[8 * i : 8 * i + 8] for i in range(total.shape[0] // 8)]
    return sum(pieces[1:], pieces[0])


def dot_of(first, second):
    return fold([a * b for a, b in zip(first, second, strict=True)])


def weight_of(table, entry, layer):
    return 0.5 * table[entry[layer]]


def pack_ends(coeff, ends):
    rows, cols = coeff.shape[1:]
    lane = lane_of((8, LANES))
    for high, edge in enumerate((slice(0, LANES), slice(cols - LANES, cols))):
        packed = jnp.zeros((8, LANES), jnp.float32)
        for layer in range(2):
            for group in range(rows // 8):
                at = layer * (rows // 8) + group
                turn = (at + high) % LANES
                value = coeff[layer, 8 * group : 8 * group + 8, edge]
                value = pltpu.roll(value, turn, 1) if turn else value
                packed = jnp.where(lane == at, value, packed)
        ends[high] = packed


def own_kernel(grid_shape, field, coeff, shifts, table, entry, out, ends, pad, coeff_pad):
    rows, cols = field.shape[1:]
    zero_rim(pad, REACH, rows)
    zero_rim(coeff_pad, 8, rows)
    fill_own(pad, REACH, field)
    fill_own(coeff_pad, 8, coeff)
    if ends is not None:
        pack_ends(coeff, ends)
    for layer in range(2):
        weight = weight_of(table, entry, layer)

        def step(i, carry, layer=layer, weight=weight):
            row = pl.multiple_of(i * CHUNK, CHUNK)
            result = apply_chunk(
                layer, row, pad, coeff_pad, shifts, weight, grid_shape, (rows, cols)
            )
            for tile, value in enumerate(result):
                out[layer, pl.ds(row, CHUNK), tile * LANES : (tile + 1) * LANES] = value
            return carry

        lax.fori_loop(0, rows // CHUNK, step, 0, unroll=UNROLL)


def products_of(own, result, base, fit):
    if base is None:
        pairs = ((own, own), (own, result), (result, result))
    else:
        rest = [a - fit * b for a, b in zip(base, own, strict=True)]
        slope = [a - fit * b for a, b in zip(own, result, strict=True)]
        pairs = (
            (rest, rest), (rest, own), (slope, rest), (result, rest), (slope, own), (result, own),
        )
    return tuple(dot_of(*pair) for pair in pairs)


def fit_of(sums):
    gamma, delta, omega = (jnp.sum(sums[index], keepdims=True) for index in range(3))
    fit = jnp.where(omega > 0.0, delta / jnp.where(omega > 0.0, omega, 1.0), 0.0)
    return gamma, delta, omega, jnp.clip(fit, -1.0, 1.0)


def rows_kernel(
    grid_shape, field, coeff, even_rows, odd_rows, even_edge, odd_edge, even_cols, odd_cols, even_ends,
    odd_ends, base, sums, shifts, table, entry, out, products, side_pad, pad,
):
    rows, cols = field.shape[1:]
    tiles = cols // LANES
    odd_y = is_odd("gy")
    first_row = lax.axis_index("gy") * rows
    first_col = lax.axis_index("gx") * cols
    zeros = jnp.zeros((REACH, LANES), jnp.float32)
    for layer in range(2):
        for side in range(2):
            for tile in (0, tiles + 1):
                pad[layer, side, tile, 0:REACH, :] = zeros
                pad[layer, side, tile, REACH:, :] = zeros
        for tile in range(tiles):
            lanes = slice(tile * LANES, (tile + 1) * LANES)
            even = even_rows[layer, 0:REACH, lanes]
            other = odd_rows[layer, 0:REACH, lanes]
            pad[layer, 0, 1 + tile, 0:REACH, :] = jnp.where(odd_y, even, other)
            pad[layer, 0, 1 + tile, REACH:, :] = zeros
            pad[layer, 1, 1 + tile, 0:REACH, :] = zeros
            pad[layer, 1, 1 + tile, REACH:, :] = jnp.where(odd_y, other, even)
    lane = lane_of((CHUNK, LANES))
    row_at = lax.broadcasted_iota(jnp.int32, (CHUNK, LANES), 0)
    for layer in range(2):
        other_layer = 1 - layer

        def step(i, carry, layer=layer, other_layer=other_layer):
            part = pl.multiple_of(i * CHUNK, CHUNK)
            totals = [[jnp.zeros((CHUNK, LANES), jnp.float32)] * tiles for _ in range(2)]
            for direction in range(shifts.shape[0]):
                shift_r, shift_c = shifts[direction, layer, 0], shifts[direction, layer, 1]
                step_r = shifts[direction, other_layer, 0] - shift_r
                start_c = LANES + shifts[direction, other_layer, 1] - shift_c
                side = jnp.where(step_r < 0, 0, 1)
                start_r = part + step_r + jnp.where(step_r < 0, REACH, 0)
                row = part + jnp.where(step_r < 0, 0, rows - REACH)
                skip = lax.shift_right_logical(start_c, 7)
                turn = jnp.bitwise_and(start_c, LANES - 1)
                back = jnp.bitwise_and(LANES - turn, LANES - 1)
                moved = [
                    pltpu.roll(
                        pad[other_layer, side, skip + tile, pl.ds(start_r, CHUNK), :], back, 1
                    )
                    for tile in range(tiles + 1)
                ]
                here = lane < LANES - turn
                image_row = row_at + (first_row + row - shift_r)
                inside = (image_row >= 0) & (image_row < grid_shape[0])
                upper = inside & (jnp.full((CHUNK, LANES), side, jnp.int32) == 0)
                lower = inside & (jnp.full((CHUNK, LANES), side, jnp.int32) == 1)
                for tile in range(tiles):
                    value = jnp.where(here, moved[tile], moved[tile + 1])
                    if tile == 0:
                        value = jnp.where(lane >= shift_c - first_col, value, 0.0)
                    if tile == tiles - 1:
                        last = grid_shape[1] + shift_c - first_col - tile * LANES
                        value = jnp.where(lane < last, value, 0.0)
                    totals[0][tile] = totals[0][tile] + jnp.where(upper, value, 0.0)
                    totals[1][tile] = totals[1][tile] + jnp.where(lower, value, 0.0)
            for side, base in enumerate((0, rows - REACH)):
                for tile in range(tiles):
                    lanes = slice(tile * LANES, (tile + 1) * LANES)
                    out[layer, pl.ds(base + part, CHUNK), lanes] += totals[side][tile]
            return carry

        lax.fori_loop(0, REACH // CHUNK, step, 0)
        weight = weight_of(table, entry, layer)
        at = lax.broadcasted_iota(jnp.int32, (8, cols), 0)
        even = even_edge[layer, REACH : REACH + 8, :]
        other = odd_edge[layer, REACH : REACH + 8, :]
        even_v = [even_rows[layer, start : start + 8, :] for start in (0, REACH - 8)]
        other_v = [odd_rows[layer, start : start + 8, :] for start in (0, REACH - 8)]
        for start, edge_c, edge_v, spot, source in (
            (0, jnp.where(odd_y, even, other), jnp.where(odd_y, even_v[1], other_v[1]), 0, 1),
            (
                rows - 8, jnp.where(odd_y, other, even), jnp.where(odd_y, other_v[0], even_v[0]),
                7, 7,
            ),
        ):
            edge_c = pltpu.roll(edge_c, source, 0)
            edge_v = pltpu.roll(edge_v, source, 0)
            value = field[layer, start : start + 8, :]
            own_c = coeff[layer, start : start + 8, :]
            extra = weight * (edge_c * value - (own_c + edge_c) * edge_v)
            out[layer, start : start + 8, :] += jnp.where(at == spot, extra, 0.0)
    fit = None if base is None else fit_of(sums)[3]
    carry = (jnp.zeros((8, LANES), jnp.float32),) * products.shape[0]
    inner = [slice(tile * LANES, (tile + 1) * LANES) for tile in range(1, tiles - 1)]
    for layer in range(2):

        def add(i, carry, layer=layer):
            chunk = pl.ds(pl.multiple_of(i * CHUNK, CHUNK), CHUNK)
            start, own, result = (
                None if ref is None else [ref[layer, chunk, lanes] for lanes in inner]
                for ref in (base, field, out)
            )
            more = products_of(own, result, start, fit)
            return tuple(a + b for a, b in zip(carry, more, strict=True))

        carry = lax.fori_loop(0, rows // CHUNK, add, carry, unroll=UNROLL)
    fill_sides(side_pad, even_cols, odd_cols, 0, REACH, rows)
    carry = finish(
        range(REACH // CHUNK, (rows - REACH) // CHUNK), carry, grid_shape, base, fit, field, coeff,
        even_ends, odd_ends, shifts, table, entry, out, side_pad,
    )
    for index, value in enumerate(carry):
        products[index] = value


def finish_chunk(grid_shape, layer, row, field, coeff, out, pad, ends, shifts, weight):
    rows, cols = field.shape[1:]
    tiles = cols // LANES
    first_row = lax.axis_index("gy") * rows + row
    first_col = lax.axis_index("gx") * cols
    lane = lane_of((CHUNK, LANES))
    row_at = lax.broadcasted_iota(jnp.int32, (CHUNK, LANES), 0)
    cut = (slice(0, LANES), slice(cols - LANES, cols))
    own = [field[layer, pl.ds(row, CHUNK), lanes] for lanes in cut]
    result = []
    for side, spot in ((0, 0), (1, LANES - 1)):
        at = layer * (rows // 8) + row // 8
        edge_c = jnp.concatenate(
            [
                pltpu.roll(ends[side], (spot - at - i) % LANES, 1)
                for i in range(CHUNK // 8)
            ]
        )
        edge_v = pad[layer, side, pl.ds(REACH + row, CHUNK), :]
        edge_v = pltpu.roll(edge_v, LANES - 1 if side else 1, 1)
        own_c = coeff[layer, pl.ds(row, CHUNK), cut[side]]
        extra = weight * (edge_c * own[side] - (own_c + edge_c) * edge_v)
        extra = jnp.where(lane == spot, extra, 0.0)
        result.append(out[layer, pl.ds(row, CHUNK), cut[side]] + extra)
    for direction in range(shifts.shape[0]):
        shift_r, shift_c = shifts[direction, layer, 0], shifts[direction, layer, 1]
        start_r = REACH + row + shifts[direction, 1 - layer, 0] - shift_r
        step_c = shifts[direction, 1 - layer, 1] - shift_c
        side = jnp.where(step_c < 0, 0, 1)
        back = jnp.bitwise_and(LANES - step_c, LANES - 1)
        moved = pltpu.roll(pad[1 - layer, side, pl.ds(start_r, CHUNK), :], back, 1)
        image_row = row_at + (first_row - shift_r)
        moved = jnp.where((image_row >= 0) & (image_row < grid_shape[0]), moved, 0.0)
        low, low_end = shift_c - first_col, jnp.where(step_c < 0, -step_c, 0)
        high = jnp.where(step_c < 0, LANES, LANES - step_c)
        high_end = grid_shape[1] + shift_c - first_col - (tiles - 1) * LANES
        result[0] = result[0] + jnp.where((lane >= low) & (lane < low_end), moved, 0.0)
        result[1] = result[1] + jnp.where((lane >= high) & (lane < high_end), moved, 0.0)
    for side in range(2):
        out[layer, pl.ds(row, CHUNK), cut[side]] = result[side]
    return own, result


def fill_sides(pad, even_ref, odd_ref, start, place, depth):
    odd_x = is_odd("gx")
    even, other = even_ref[start : start + depth, :], odd_ref[start : start + depth, :]
    for side, packed in ((0, jnp.where(odd_x, even, other)), (1, jnp.where(odd_x, other, even))):
        pad[0, side, place : place + depth, :] = packed
        pad[1, side, place : place + depth, :] = pltpu.roll(packed, HALF, 1)


def finish(
    chunks, carry, grid_shape, base, fit, field, coeff, even_ends, odd_ends, shifts, table, entry, out,
    pad,
):
    rows, cols = field.shape[1:]
    odd_x = is_odd("gx")
    even, other = even_ends[rows : rows + 8, :], odd_ends[rows : rows + 8, :]
    ends = (jnp.where(odd_x, even, other), jnp.where(odd_x, other, even))
    cut = (slice(0, LANES), slice(cols - LANES, cols))
    for layer in range(2):
        weight = weight_of(table, entry, layer)
        for row in (chunk * CHUNK for chunk in chunks):
            own, result = finish_chunk(
                grid_shape, layer, row, field, coeff, out, pad, ends, shifts, weight
            )
            start = None if base is None else [base[layer, row : row + CHUNK, x] for x in cut]
            more = products_of(own, result, start, fit)
            carry = tuple(a + b for a, b in zip(carry, more, strict=True))
    return carry


def finish_ends(grid_shape, even_corners, odd_corners, products, pad, field, *rest):
    rows = field.shape[1]
    fill_sides(pad, even_corners, odd_corners, 0, 0, REACH)
    fill_sides(pad, even_corners, odd_corners, REACH, REACH + rows, REACH)
    depth = REACH // CHUNK
    chunks = [*range(depth), *range(rows // CHUNK - depth, rows // CHUNK)]
    carry = tuple(products[index] for index in range(products.shape[0]))
    base, fit, *others = rest
    return finish(chunks, carry, grid_shape, base, fit, field, *others, pad)


def first_kernel(
    grid_shape, before, pad_before, field, coeff, even_ends, odd_ends, even_corners, odd_corners,
    products, shifts, table, entry, out, pad, sums, even_out, odd_out,
):
    del before, pad_before
    rows = field.shape[1]
    carry = finish_ends(
        grid_shape, even_corners, odd_corners, products, pad, field, None, None, coeff, even_ends,
        odd_ends, shifts, table, entry, out,
    )
    for index, value in enumerate(carry):
        sums[index] = value
    odd_y = is_odd("gy")
    low, high = out[:, 0:REACH, :], out[:, rows - REACH :, :]
    even_out[...] = jnp.where(odd_y, low, high)
    odd_out[...] = jnp.where(odd_y, high, low)


def second_kernel(
    grid_shape, before, pad_before, base, field, coeff, even_ends, odd_ends, even_corners, odd_corners,
    products, sums, shifts, table, entry, out, pad, parts,
):
    del before, pad_before
    gamma, delta, omega, fit = fit_of(sums)
    carry = finish_ends(
        grid_shape, even_corners, odd_corners, products, pad, field, base, fit, coeff, even_ends,
        odd_ends, shifts, table, entry, out,
    )
    rest2, rest_w, slope_rest, n_rest, slope_w, n_w = (
        jnp.sum(value, keepdims=True) for value in carry
    )
    lane = lane_of((8, LANES))
    row = jnp.zeros((8, LANES), jnp.float32)
    for at, value in (
        (0, rest2), (1, slope_rest), (8, 2.0 * rest_w), (9, n_rest + slope_w),
        (16, omega), (17, n_w), (24, fit), (25, fit), (32, gamma), (33, delta),
    ):
        row = jnp.where(lane == at, value, row)
    for start in range(0, parts.shape[0], 8):
        parts[start : start + 8, :] = row


def pick(row, lane, at):
    return jnp.sum(jnp.where(lane == at, row, 0.0), keepdims=True)


def last_kernel(
    parts, base, w_vec, n_vec, solution_out, residual_out, solution_part, residual_part, sems
):
    gathered = parts[...]
    count = gathered.shape[0]
    lane = lane_of((8, LANES))
    total = sum(gathered[8 * i : 8 * i + 8] for i in range(count // 8))
    gamma, delta = pick(total, lane, 32), pick(total, lane, 33)
    alpha = gamma / delta
    gap = alpha - pltpu.roll(gathered, LANES - 24, 1)
    moved = gathered - gap * pltpu.roll(gathered, LANES - 8, 1)
    moved = moved + gap * gap * pltpu.roll(gathered, LANES - 16, 1)
    total = sum(moved[8 * i : 8 * i + 8] for i in range(count // 8))
    gamma_next, delta_next = pick(total, lane, 0), pick(total, lane, 1)
    beta = gamma_next / gamma
    alpha_next = gamma_next / (delta_next - beta * gamma_next / alpha)
    layers, rows = base.shape[:2]
    depth = rows // PIECES
    copies = []
    for layer in range(layers):
        for piece in range(PIECES):
            part = pl.ds(piece * depth, depth)
            start, w_start = base[layer, part, :], w_vec[layer, part, :]
            residual = start - alpha * w_start
            w_next = w_start - alpha * n_vec[layer, part, :]
            solution_part[layer, part, :] = alpha * start + alpha_next * (residual + beta * start)
            residual_part[layer, part, :] = residual - alpha_next * (w_next + beta * w_start)
            for which, (source, target) in enumerate(
                ((solution_part, solution_out), (residual_part, residual_out))
            ):
                copy = pltpu.make_async_copy(
                    source.at[layer, part, :],
                    target.at[layer, part, :],
                    sems.at[which, layer, piece],
                )
                copy.start()
                copies.append(copy)
    for copy in copies:
        copy.wait()


def on_tensor_core(kernel, name, operands, scalars, out_shape, scratch, microseconds, in_place=0):
    return pl.pallas_call(
        kernel,
        out_shape=out_shape,
        in_specs=[VMEM_SPEC] * len(operands) + [SMEM_SPEC] * len(scalars),
        out_specs=(VMEM_SPEC,) * len(out_shape),
        scratch_shapes=[pltpu.VMEM(shape, jnp.float32) for shape in scratch],
        input_output_aliases={index: index for index in range(in_place)},
        compiler_params=pltpu.CompilerParams(vmem_limit_bytes=VMEM_BYTES),
        cost_estimate=pl.CostEstimate(
            flops=0, bytes_accessed=3_000_000 * microseconds, transcendentals=0
        ),
        name=name,
    )(*operands, *scalars)


def on_device(right_side, coefficient, strength_table, layer_entry, shifts):
    layers, rows, cols = right_side.shape
    count_y, count_x = lax.axis_size("gy"), lax.axis_size("gx")
    devices = count_x * count_y
    tiles = cols // LANES
    grid_shape = (rows * count_y, cols * count_x)
    full = jax.ShapeDtypeStruct((layers, rows, cols), jnp.float32)
    edge = jax.ShapeDtypeStruct((layers, REACH, cols), jnp.float32)
    scalars = (shifts, strength_table, layer_entry)
    own_pads = [(2, tiles + 2, rows + 2 * REACH, LANES), (2, tiles + 2, rows + 16, LANES)]
    row_pads = [(2, 2, tiles + 2, 2 * REACH, LANES)]
    side_pad = jax.ShapeDtypeStruct((2, 2, rows + 2 * REACH, LANES), jnp.float32)

    def sums_of(count):
        return jax.ShapeDtypeStruct((count, 8, LANES), jnp.float32)

    def bind(kernel):
        def bound(*refs):
            kernel(grid_shape, *refs)

        return bound

    def rows_first(before, packed, field, coeff, even, odd, even_cols, odd_cols, *refs):
        del before, packed
        rows_kernel(
            grid_shape, field, coeff, even, odd, even, odd, even_cols, odd_cols, even_cols, odd_cols,
            None, None, *refs,
        )

    def rows_second(before, packed, *refs):
        del before, packed
        rows_kernel(grid_shape, *refs)

    def own_first(field, coeff, shifts, table, entry, out, ends, *pads):
        own_kernel(grid_shape, field, coeff, shifts, table, entry, out, ends, *pads)

    def own_second(field, coeff, shifts, table, entry, out, *pads):
        own_kernel(grid_shape, field, coeff, shifts, table, entry, out, None, *pads)

    rows0 = swap(*edge_rows(right_side, coefficient), "gy")
    w_own, ends = on_tensor_core(
        own_first, "own_first", (right_side, coefficient), scalars, (full, sums_of(2)), own_pads, 6
    )
    cols0 = swap(*pack_sides(right_side, ends, True), "gx")
    packed = pack_corners(*rows0)
    corners0 = swap(*packed, "gx")
    w_rows, products, sides = on_tensor_core(
        rows_first, "rows_first", (w_own, packed[0], right_side, coefficient, *rows0, *cols0), scalars,
        (full, sums_of(3), side_pad), row_pads, 3, 1,
    )
    w_vec, _, sums, even, odd = on_tensor_core(
        bind(first_kernel), "first_apply",
        (w_rows, sides, right_side, coefficient, *cols0, *corners0, products), scalars,
        (full, side_pad, sums_of(3), edge, edge), [], 3, 2,
    )
    rows1 = swap(even, odd, "gy")
    (n_own,) = on_tensor_core(
        own_second, "own_second", (w_vec, coefficient), scalars, (full,), own_pads, 6
    )
    cols1 = swap(*pack_sides(w_vec, n_own, False), "gx")
    packed = pack_corners(*rows1)
    corners1 = swap(*packed, "gx")
    n_rows, products, sides = on_tensor_core(
        rows_second, "rows_second",
        (n_own, packed[0], w_vec, coefficient, *rows1, *rows0, *cols1, *cols0, right_side, sums),
        scalars, (full, sums_of(6), side_pad), row_pads, 3, 1,
    )
    n_vec, _, parts = on_tensor_core(
        bind(second_kernel), "second_apply",
        (n_rows, sides, right_side, w_vec, coefficient, *cols0, *corners1, products, sums), scalars,
        (full, side_pad, jax.ShapeDtypeStruct((devices, LANES), jnp.float32)), [], 3, 2,
    )
    gathered = lax.all_to_all(parts, ("gx", "gy"), 0, 0, tiled=True)
    return pl.pallas_call(
        last_kernel,
        out_shape=(full, full),
        in_specs=[VMEM_SPEC] * 4,
        out_specs=(pl.BlockSpec(memory_space=pltpu.HBM),) * 2,
        scratch_shapes=[
            pltpu.VMEM((layers, rows, cols), jnp.float32),
            pltpu.VMEM((layers, rows, cols), jnp.float32),
            pltpu.SemaphoreType.DMA((2, layers, PIECES)),
        ],
        compiler_params=pltpu.CompilerParams(vmem_limit_bytes=VMEM_BYTES),
        name="last_update",
    )(gathered, right_side, w_vec, n_vec)


def solution(mesh):
    placed = (P(None, "gy", "gx"), P(None, "gy", "gx"), P(), P(), P())
    return jax.shard_map(
        on_device,
        mesh=mesh,
        in_specs=placed,
        out_specs=(P(None, "gy", "gx"), P(None, "gy", "gx")),
        check_vma=False,
    )
```

```python
import jax
import jax.numpy as jnp
from jax import lax
from jax.experimental import pallas as pl
from jax.experimental.pallas import tpu as pltpu
from jax.sharding import PartitionSpec as P

REACH = 64
LANES = 128
HALF = 64
CHUNK = 32
UNROLL = 8
PIECES = 4
VMEM_BYTES = 32 * 1024 * 1024
EDGE_BYTES = 53 * 1024 * 1024
VMEM_SPEC = pl.BlockSpec(memory_space=pltpu.VMEM)
SMEM_SPEC = pl.BlockSpec(memory_space=pltpu.SMEM)


def even_swap(count):
    return [(i, i ^ 1) for i in range(count)]


def odd_swap(count):
    return [(i, i + 1 if i % 2 else i - 1) for i in range(1, count - 1)]


def is_odd(axis):
    return lax.rem(lax.axis_index(axis), 2) == 1


def swap(even, odd, axis):
    count = lax.axis_size(axis)
    return (
        lax.ppermute(even, axis, even_swap(count)),
        lax.ppermute(odd, axis, odd_swap(count)),
    )


def lane_of(shape):
    return lax.broadcasted_iota(jnp.int32, shape, 1)


def pack_columns(first, second, high):
    low_lanes = lane_of(first.shape) < HALF
    turned = pltpu.roll(second, HALF, 1)
    if high:
        return jnp.where(low_lanes, turned, first)
    return jnp.where(low_lanes, first, turned)


def packed_edges(load, cols):
    edges = (slice(0, LANES), slice(cols - LANES, cols))
    return [pack_columns(load(0, edge), load(1, edge), high) for high, edge in enumerate(edges)]


def store_packed(even_ref, odd_ref, start, low, high):
    odd = is_odd("gx")
    rows = low.shape[0]
    even_ref[start : start + rows, :] = jnp.where(odd, low, high)
    odd_ref[start : start + rows, :] = jnp.where(odd, high, low)


def pack_sides_kernel(with_ends, field, after, even_out, odd_out):
    rows, cols = field.shape[1:]
    low, high = packed_edges(lambda layer, edge: field[layer, :, edge], cols)
    store_packed(even_out, odd_out, 0, low, high)
    if with_ends:
        store_packed(even_out, odd_out, rows, after[0], after[1])


def pack_corners_kernel(even_rows, odd_rows, even_out, odd_out):
    cols = even_rows.shape[2]
    odd_y = is_odd("gy")
    for start, above in ((0, True), (REACH, False)):

        def halo(layer, edge, above=above):
            even = even_rows[layer, 0:REACH, edge]
            other = odd_rows[layer, 0:REACH, edge]
            return jnp.where(odd_y == above, even, other)

        store_packed(even_out, odd_out, start, *packed_edges(halo, cols))


def pack(kernel, operands, rows, name):
    out = jax.ShapeDtypeStruct((rows, LANES), jnp.float32)
    return pl.pallas_call(
        kernel,
        out_shape=(out, out),
        in_specs=[VMEM_SPEC] * len(operands),
        out_specs=(VMEM_SPEC,) * 2,
        compiler_params=pltpu.CompilerParams(vmem_limit_bytes=VMEM_BYTES),
        name=name,
    )(*operands)


def pack_sides(field, after, with_ends):
    def kernel(*refs):
        pack_sides_kernel(with_ends, *refs)

    return pack(kernel, (field, after), field.shape[1] + (8 if with_ends else 0), "pack_sides")


def pack_corners(even_rows, odd_rows):
    return pack(pack_corners_kernel, (even_rows, odd_rows), 2 * REACH, "pack_corners")


def edge_kernel(field, coeff, even_out, odd_out, sems):
    rows = field.shape[1]
    odd_y = is_odd("gy")
    copies = []
    for index, (out, at_top) in enumerate(((even_out, odd_y), (odd_out, jnp.logical_not(odd_y)))):
        for part, (source, place, depth) in enumerate(((field, 0, REACH), (coeff, REACH, 8))):
            start = pl.multiple_of(jnp.where(at_top, 0, rows - depth), 8)
            copies.append(
                pltpu.make_async_copy(
                    source.at[:, pl.ds(start, depth), :],
                    out.at[:, pl.ds(place, depth), :],
                    sems.at[index, part],
                )
            )
    for copy in copies:
        copy.start()
    for copy in copies:
        copy.wait()


def edge_rows(field, coeff):
    layers, _, cols = field.shape
    out = jax.ShapeDtypeStruct((layers, REACH + 8, cols), jnp.float32)
    return pl.pallas_call(
        edge_kernel,
        out_shape=(out, out),
        in_specs=[pl.BlockSpec(memory_space=pltpu.HBM)] * 2,
        out_specs=(VMEM_SPEC,) * 2,
        scratch_shapes=[pltpu.SemaphoreType.DMA((2, 2))],
        compiler_params=pltpu.CompilerParams(vmem_limit_bytes=EDGE_BYTES),
        name="edge_rows",
    )(field, coeff)


def zero_rim(pad, depth, rows):
    zeros = jnp.zeros((depth, LANES), jnp.float32)
    for layer in range(2):
        for tile in range(pad.shape[1]):
            pad[layer, tile, 0:depth, :] = zeros
            pad[layer, tile, depth + rows :, :] = zeros


def fill_own(pad, depth, field):
    rows, cols = field.shape[1:]
    for layer in range(2):
        for tile in range(cols // LANES):
            lanes = slice(tile * LANES, (tile + 1) * LANES)
            pad[layer, tile, depth : depth + rows, :] = field[layer, :, lanes]


def move_across(tiles, step_c, lane):
    count = len(tiles)
    back = jnp.bitwise_and(LANES - step_c, LANES - 1)
    from_left = lane < jnp.where(step_c < 0, -step_c, 0)
    from_right = lane >= jnp.where(step_c < 0, LANES, LANES - step_c)
    turned = [0.0] + [pltpu.roll(tile, back, 1) for tile in tiles] + [0.0]
    return [
        jnp.where(from_left, turned[i], jnp.where(from_right, turned[i + 2], turned[i + 1]))
        for i in range(count)
    ]


def from_the_right(tiles, lane, last):
    ahead = [pltpu.roll(tile, LANES - 1, 1) for tile in tiles]
    return [
        jnp.where(lane == LANES - 1, after, tile)
        for tile, after in zip(ahead, [*ahead[1:], last], strict=True)
    ]


def apply_chunk(
    layer, row, pad, coeff_pad, across, across_out, shifts, weight, grid_shape, tile_shape
):
    rows, cols = tile_shape
    tiles = cols // LANES
    other = 1 - layer
    lane = lane_of((CHUNK, LANES))
    row_at = lax.broadcasted_iota(jnp.int32, (CHUNK, LANES), 0)
    first_row = lax.axis_index("gy") * rows + row
    first_col = lax.axis_index("gx") * cols
    cut = [slice(tile * LANES, (tile + 1) * LANES) for tile in range(tiles)]

    def at(ref, tile, start):
        return ref[layer, tile, pl.ds(start, CHUNK), :]

    own = [at(pad, tile, REACH + row) for tile in range(tiles)]
    own_c = [at(coeff_pad, tile, 8 + row) for tile in range(tiles)]
    if across is None:
        right_c = from_the_right(own_c, lane, 0.0)
        both = [a + b for a, b in zip(own_c, right_c, strict=True)]
        for value, lanes in zip(both, cut, strict=True):
            across_out[layer, pl.ds(row, CHUNK), lanes] = value
    else:
        both = [across[layer, pl.ds(row, CHUNK), lanes] for lanes in cut]
    right = from_the_right(own, lane, own[-1])
    flow = [c * (a - b) for c, a, b in zip(both, own, right, strict=True)]
    turned = [pltpu.roll(value, 1, 1) for value in flow]
    result = []
    for tile in range(tiles):
        value, coeff = own[tile], own_c[tile]
        above, below = at(pad, tile, REACH - 1 + row), at(pad, tile, REACH + 1 + row)
        above_c, below_c = at(coeff_pad, tile, 7 + row), at(coeff_pad, tile, 9 + row)
        total = (coeff + above_c) * (value - above) + (coeff + below_c) * (value - below)
        inflow = jnp.where(lane == 0, turned[tile - 1] if tile else 0.0, turned[tile])
        result.append(weight * (total + flow[tile] - inflow))
    for direction in range(shifts.shape[0]):
        shift_r, shift_c = shifts[direction, layer, 0], shifts[direction, layer, 1]
        start_r = REACH + row + shifts[direction, other, 0] - shift_r
        source = [pad[other, tile, pl.ds(start_r, CHUNK), :] for tile in range(tiles)]
        moved = move_across(source, shifts[direction, other, 1] - shift_c, lane)
        image_row = row_at + (first_row - shift_r)
        inside = (image_row >= 0) & (image_row < grid_shape[0])
        for tile in range(tiles):
            mask = inside
            if tile == 0:
                mask = mask & (lane >= shift_c - first_col)
            if tile == tiles - 1:
                mask = mask & (lane < grid_shape[1] + shift_c - first_col - tile * LANES)
            result[tile] = result[tile] + jnp.where(mask, own[tile] + moved[tile], 0.0)
    return result


def fold(parts):
    total = sum(parts[1:], parts[0])
    pieces = [total[8 * i : 8 * i + 8] for i in range(total.shape[0] // 8)]
    return sum(pieces[1:], pieces[0])


def dot_of(first, second):
    return fold([a * b for a, b in zip(first, second, strict=True)])


def weight_of(table, entry, layer):
    return 0.5 * table[entry[layer]]


def pack_ends(coeff, ends):
    rows, cols = coeff.shape[1:]
    lane = lane_of((8, LANES))
    for high, edge in enumerate((slice(0, LANES), slice(cols - LANES, cols))):
        packed = jnp.zeros((8, LANES), jnp.float32)
        for layer in range(2):
            for group in range(rows // 8):
                at = layer * (rows // 8) + group
                turn = (at + high) % LANES
                value = coeff[layer, 8 * group : 8 * group + 8, edge]
                value = pltpu.roll(value, turn, 1) if turn else value
                packed = jnp.where(lane == at, value, packed)
        ends[high] = packed


def own_kernel(
    grid_shape, field, coeff, across, shifts, table, entry, out, ends, across_out, pad, coeff_pad
):
    rows, cols = field.shape[1:]
    zero_rim(pad, REACH, rows)
    zero_rim(coeff_pad, 8, rows)
    fill_own(pad, REACH, field)
    fill_own(coeff_pad, 8, coeff)
    if ends is not None:
        pack_ends(coeff, ends)
    for layer in range(2):
        weight = weight_of(table, entry, layer)

        def step(i, carry, layer=layer, weight=weight):
            row = pl.multiple_of(i * CHUNK, CHUNK)
            result = apply_chunk(
                layer, row, pad, coeff_pad, across, across_out, shifts, weight, grid_shape, (rows, cols)
            )
            for tile, value in enumerate(result):
                out[layer, pl.ds(row, CHUNK), tile * LANES : (tile + 1) * LANES] = value
            return carry

        lax.fori_loop(0, rows // CHUNK, step, 0, unroll=UNROLL)


def products_of(own, result, base, fit):
    if base is None:
        pairs = ((own, own), (own, result), (result, result))
    else:
        rest = [a - fit * b for a, b in zip(base, own, strict=True)]
        slope = [a - fit * b for a, b in zip(own, result, strict=True)]
        pairs = (
            (rest, rest), (rest, own), (slope, rest), (result, rest), (slope, own), (result, own),
        )
    return tuple(dot_of(*pair) for pair in pairs)


def fit_of(sums):
    gamma, delta, omega = (jnp.sum(sums[index], keepdims=True) for index in range(3))
    fit = jnp.where(omega > 0.0, delta / jnp.where(omega > 0.0, omega, 1.0), 0.0)
    return gamma, delta, omega, jnp.clip(fit, -1.0, 1.0)


def rows_kernel(
    grid_shape, field, coeff, even_rows, odd_rows, even_edge, odd_edge, even_cols, odd_cols, even_ends,
    odd_ends, base, sums, shifts, table, entry, out, products, side_pad, pad,
):
    rows, cols = field.shape[1:]
    tiles = cols // LANES
    odd_y = is_odd("gy")
    first_row = lax.axis_index("gy") * rows
    first_col = lax.axis_index("gx") * cols
    zeros = jnp.zeros((REACH, LANES), jnp.float32)
    for layer in range(2):
        for tile in range(tiles):
            lanes = slice(tile * LANES, (tile + 1) * LANES)
            even = even_rows[layer, 0:REACH, lanes]
            other = odd_rows[layer, 0:REACH, lanes]
            pad[layer, 0, tile, 0:REACH, :] = jnp.where(odd_y, even, other)
            pad[layer, 0, tile, REACH:, :] = zeros
            pad[layer, 1, tile, 0:REACH, :] = zeros
            pad[layer, 1, tile, REACH:, :] = jnp.where(odd_y, other, even)
    lane = lane_of((CHUNK, LANES))
    row_at = lax.broadcasted_iota(jnp.int32, (CHUNK, LANES), 0)
    for layer in range(2):
        other_layer = 1 - layer

        def step(i, carry, layer=layer, other_layer=other_layer):
            part = pl.multiple_of(i * CHUNK, CHUNK)
            totals = [[jnp.zeros((CHUNK, LANES), jnp.float32)] * tiles for _ in range(2)]
            for direction in range(shifts.shape[0]):
                shift_r, shift_c = shifts[direction, layer, 0], shifts[direction, layer, 1]
                step_r = shifts[direction, other_layer, 0] - shift_r
                side = jnp.where(step_r < 0, 0, 1)
                start_r = part + step_r + jnp.where(step_r < 0, REACH, 0)
                row = part + jnp.where(step_r < 0, 0, rows - REACH)
                source = [
                    pad[other_layer, side, tile, pl.ds(start_r, CHUNK), :] for tile in range(tiles)
                ]
                moved = move_across(source, shifts[direction, other_layer, 1] - shift_c, lane)
                image_row = row_at + (first_row + row - shift_r)
                inside = (image_row >= 0) & (image_row < grid_shape[0])
                upper = inside & (jnp.full((CHUNK, LANES), side, jnp.int32) == 0)
                lower = inside & (jnp.full((CHUNK, LANES), side, jnp.int32) == 1)
                for tile in range(tiles):
                    value = moved[tile]
                    if tile == 0:
                        value = jnp.where(lane >= shift_c - first_col, value, 0.0)
                    if tile == tiles - 1:
                        last = grid_shape[1] + shift_c - first_col - tile * LANES
                        value = jnp.where(lane < last, value, 0.0)
                    totals[0][tile] = totals[0][tile] + jnp.where(upper, value, 0.0)
                    totals[1][tile] = totals[1][tile] + jnp.where(lower, value, 0.0)
            for side, base in enumerate((0, rows - REACH)):
                for tile in range(tiles):
                    lanes = slice(tile * LANES, (tile + 1) * LANES)
                    out[layer, pl.ds(base + part, CHUNK), lanes] += totals[side][tile]
            return carry

        lax.fori_loop(0, REACH // CHUNK, step, 0, unroll=True)
        weight = weight_of(table, entry, layer)
        at = lax.broadcasted_iota(jnp.int32, (8, cols), 0)
        even = even_edge[layer, REACH : REACH + 8, :]
        other = odd_edge[layer, REACH : REACH + 8, :]
        even_v = [even_rows[layer, start : start + 8, :] for start in (0, REACH - 8)]
        other_v = [odd_rows[layer, start : start + 8, :] for start in (0, REACH - 8)]
        for start, edge_c, edge_v, spot, source in (
            (0, jnp.where(odd_y, even, other), jnp.where(odd_y, even_v[1], other_v[1]), 0, 1),
            (
                rows - 8, jnp.where(odd_y, other, even), jnp.where(odd_y, other_v[0], even_v[0]),
                7, 7,
            ),
        ):
            edge_c = pltpu.roll(edge_c, source, 0)
            edge_v = pltpu.roll(edge_v, source, 0)
            value = field[layer, start : start + 8, :]
            own_c = coeff[layer, start : start + 8, :]
            extra = weight * (edge_c * value - (own_c + edge_c) * edge_v)
            out[layer, start : start + 8, :] += jnp.where(at == spot, extra, 0.0)
    fit = None if base is None else fit_of(sums)[3]
    carry = (jnp.zeros((8, LANES), jnp.float32),) * products.shape[0]
    inner = [slice(tile * LANES, (tile + 1) * LANES) for tile in range(1, tiles - 1)]
    for layer in range(2):

        def add(i, carry, layer=layer):
            chunk = pl.ds(pl.multiple_of(i * CHUNK, CHUNK), CHUNK)
            start, own, result = (
                None if ref is None else [ref[layer, chunk, lanes] for lanes in inner]
                for ref in (base, field, out)
            )
            more = products_of(own, result, start, fit)
            return tuple(a + b for a, b in zip(carry, more, strict=True))

        carry = lax.fori_loop(0, rows // CHUNK, add, carry, unroll=UNROLL)
    fill_sides(side_pad, even_cols, odd_cols, 0, REACH, rows)
    carry = finish(
        range(REACH // CHUNK, (rows - REACH) // CHUNK), carry, grid_shape, base, fit, field, coeff,
        even_ends, odd_ends, shifts, table, entry, out, side_pad,
    )
    for index, value in enumerate(carry):
        products[index] = value


def finish_chunk(grid_shape, layer, row, field, coeff, out, pad, ends, shifts, weight):
    rows, cols = field.shape[1:]
    tiles = cols // LANES
    first_row = lax.axis_index("gy") * rows + row
    first_col = lax.axis_index("gx") * cols
    lane = lane_of((CHUNK, LANES))
    row_at = lax.broadcasted_iota(jnp.int32, (CHUNK, LANES), 0)
    cut = (slice(0, LANES), slice(cols - LANES, cols))
    own = [field[layer, pl.ds(row, CHUNK), lanes] for lanes in cut]
    result = []
    for side, spot in ((0, 0), (1, LANES - 1)):
        at = layer * (rows // 8) + row // 8
        edge_c = jnp.concatenate(
            [
                pltpu.roll(ends[side], (spot - at - i) % LANES, 1)
                for i in range(CHUNK // 8)
            ]
        )
        edge_v = pad[layer, side, pl.ds(REACH + row, CHUNK), :]
        edge_v = pltpu.roll(edge_v, LANES - 1 if side else 1, 1)
        own_c = coeff[layer, pl.ds(row, CHUNK), cut[side]]
        extra = weight * ((own_c + edge_c) * (own[side] - edge_v))
        extra = jnp.where(lane == spot, extra, 0.0)
        result.append(out[layer, pl.ds(row, CHUNK), cut[side]] + extra)
    for direction in range(shifts.shape[0]):
        shift_r, shift_c = shifts[direction, layer, 0], shifts[direction, layer, 1]
        start_r = REACH + row + shifts[direction, 1 - layer, 0] - shift_r
        step_c = shifts[direction, 1 - layer, 1] - shift_c
        side = jnp.where(step_c < 0, 0, 1)
        back = jnp.bitwise_and(LANES - step_c, LANES - 1)
        moved = pltpu.roll(pad[1 - layer, side, pl.ds(start_r, CHUNK), :], back, 1)
        image_row = row_at + (first_row - shift_r)
        moved = jnp.where((image_row >= 0) & (image_row < grid_shape[0]), moved, 0.0)
        low, low_end = shift_c - first_col, jnp.where(step_c < 0, -step_c, 0)
        high = jnp.where(step_c < 0, LANES, LANES - step_c)
        high_end = grid_shape[1] + shift_c - first_col - (tiles - 1) * LANES
        result[0] = result[0] + jnp.where((lane >= low) & (lane < low_end), moved, 0.0)
        result[1] = result[1] + jnp.where((lane >= high) & (lane < high_end), moved, 0.0)
    for side in range(2):
        out[layer, pl.ds(row, CHUNK), cut[side]] = result[side]
    return own, result


def fill_sides(pad, even_ref, odd_ref, start, place, depth):
    odd_x = is_odd("gx")
    even, other = even_ref[start : start + depth, :], odd_ref[start : start + depth, :]
    for side, packed in ((0, jnp.where(odd_x, even, other)), (1, jnp.where(odd_x, other, even))):
        pad[0, side, place : place + depth, :] = packed
        pad[1, side, place : place + depth, :] = pltpu.roll(packed, HALF, 1)


def finish(
    chunks, carry, grid_shape, base, fit, field, coeff, even_ends, odd_ends, shifts, table, entry, out,
    pad,
):
    rows, cols = field.shape[1:]
    odd_x = is_odd("gx")
    even, other = even_ends[rows : rows + 8, :], odd_ends[rows : rows + 8, :]
    ends = (jnp.where(odd_x, even, other), jnp.where(odd_x, other, even))
    cut = (slice(0, LANES), slice(cols - LANES, cols))
    for layer in range(2):
        weight = weight_of(table, entry, layer)
        for row in (chunk * CHUNK for chunk in chunks):
            own, result = finish_chunk(
                grid_shape, layer, row, field, coeff, out, pad, ends, shifts, weight
            )
            start = None if base is None else [base[layer, row : row + CHUNK, x] for x in cut]
            more = products_of(own, result, start, fit)
            carry = tuple(a + b for a, b in zip(carry, more, strict=True))
    return carry


def finish_ends(grid_shape, even_corners, odd_corners, products, pad, field, *rest):
    rows = field.shape[1]
    fill_sides(pad, even_corners, odd_corners, 0, 0, REACH)
    fill_sides(pad, even_corners, odd_corners, REACH, REACH + rows, REACH)
    depth = REACH // CHUNK
    chunks = [*range(depth), *range(rows // CHUNK - depth, rows // CHUNK)]
    carry = tuple(products[index] for index in range(products.shape[0]))
    base, fit, *others = rest
    return finish(chunks, carry, grid_shape, base, fit, field, *others, pad)


def first_kernel(
    grid_shape, before, pad_before, field, coeff, even_ends, odd_ends, even_corners, odd_corners,
    products, shifts, table, entry, out, pad, sums, even_out, odd_out,
):
    del before, pad_before
    rows = field.shape[1]
    carry = finish_ends(
        grid_shape, even_corners, odd_corners, products, pad, field, None, None, coeff, even_ends,
        odd_ends, shifts, table, entry, out,
    )
    for index, value in enumerate(carry):
        sums[index] = value
    odd_y = is_odd("gy")
    low, high = out[:, 0:REACH, :], out[:, rows - REACH :, :]
    even_out[...] = jnp.where(odd_y, low, high)
    odd_out[...] = jnp.where(odd_y, high, low)


def second_kernel(
    grid_shape, before, pad_before, base, field, coeff, even_ends, odd_ends, even_corners, odd_corners,
    products, sums, shifts, table, entry, out, pad, parts,
):
    del before, pad_before
    gamma, delta, omega, fit = fit_of(sums)
    carry = finish_ends(
        grid_shape, even_corners, odd_corners, products, pad, field, base, fit, coeff, even_ends,
        odd_ends, shifts, table, entry, out,
    )
    rest2, rest_w, slope_rest, n_rest, slope_w, n_w = (
        jnp.sum(value, keepdims=True) for value in carry
    )
    lane = lane_of((8, LANES))
    row = jnp.zeros((8, LANES), jnp.float32)
    for at, value in (
        (0, rest2), (1, slope_rest), (8, 2.0 * rest_w), (9, n_rest + slope_w),
        (16, omega), (17, n_w), (24, fit), (25, fit), (32, gamma), (33, delta),
    ):
        row = jnp.where(lane == at, value, row)
    for start in range(0, parts.shape[0], 8):
        parts[start : start + 8, :] = row


def pick(row, lane, at):
    return jnp.sum(jnp.where(lane == at, row, 0.0), keepdims=True)


def last_kernel(
    parts, base, w_vec, n_vec, solution_out, residual_out, solution_part, residual_part, sems
):
    gathered = parts[...]
    count = gathered.shape[0]
    lane = lane_of((8, LANES))
    total = sum(gathered[8 * i : 8 * i + 8] for i in range(count // 8))
    gamma, delta = pick(total, lane, 32), pick(total, lane, 33)
    alpha = gamma / delta
    gap = alpha - pltpu.roll(gathered, LANES - 24, 1)
    moved = gathered - gap * pltpu.roll(gathered, LANES - 8, 1)
    moved = moved + gap * gap * pltpu.roll(gathered, LANES - 16, 1)
    total = sum(moved[8 * i : 8 * i + 8] for i in range(count // 8))
    gamma_next, delta_next = pick(total, lane, 0), pick(total, lane, 1)
    beta = gamma_next / gamma
    alpha_next = gamma_next / (delta_next - beta * gamma_next / alpha)
    layers, rows = base.shape[:2]
    depth = rows // PIECES
    copies = []
    for layer in range(layers):
        for piece in range(PIECES):
            part = pl.ds(piece * depth, depth)
            start, w_start = base[layer, part, :], w_vec[layer, part, :]
            residual = start - alpha * w_start
            w_next = w_start - alpha * n_vec[layer, part, :]
            solution_part[layer, part, :] = alpha * start + alpha_next * (residual + beta * start)
            residual_part[layer, part, :] = residual - alpha_next * (w_next + beta * w_start)
            for which, (source, target) in enumerate(
                ((solution_part, solution_out), (residual_part, residual_out))
            ):
                copy = pltpu.make_async_copy(
                    source.at[layer, part, :],
                    target.at[layer, part, :],
                    sems.at[which, layer, piece],
                )
                copy.start()
                copies.append(copy)
    for copy in copies:
        copy.wait()


def on_tensor_core(kernel, name, operands, scalars, out_shape, scratch, microseconds, in_place=0):
    return pl.pallas_call(
        kernel,
        out_shape=out_shape,
        in_specs=[VMEM_SPEC] * len(operands) + [SMEM_SPEC] * len(scalars),
        out_specs=(VMEM_SPEC,) * len(out_shape),
        scratch_shapes=[pltpu.VMEM(shape, jnp.float32) for shape in scratch],
        input_output_aliases={index: index for index in range(in_place)},
        compiler_params=pltpu.CompilerParams(vmem_limit_bytes=VMEM_BYTES),
        cost_estimate=pl.CostEstimate(
            flops=0, bytes_accessed=3_000_000 * microseconds, transcendentals=0
        ),
        name=name,
    )(*operands, *scalars)


def on_device(right_side, coefficient, strength_table, layer_entry, shifts):
    layers, rows, cols = right_side.shape
    count_y, count_x = lax.axis_size("gy"), lax.axis_size("gx")
    devices = count_x * count_y
    tiles = cols // LANES
    grid_shape = (rows * count_y, cols * count_x)
    full = jax.ShapeDtypeStruct((layers, rows, cols), jnp.float32)
    edge = jax.ShapeDtypeStruct((layers, REACH, cols), jnp.float32)
    scalars = (shifts, strength_table, layer_entry)
    own_pads = [(2, tiles, rows + 2 * REACH, LANES), (2, tiles, rows + 16, LANES)]
    row_pads = [(2, 2, tiles, 2 * REACH, LANES)]
    side_pad = jax.ShapeDtypeStruct((2, 2, rows + 2 * REACH, LANES), jnp.float32)

    def sums_of(count):
        return jax.ShapeDtypeStruct((count, 8, LANES), jnp.float32)

    def bind(kernel):
        def bound(*refs):
            kernel(grid_shape, *refs)

        return bound

    def rows_first(before, packed, field, coeff, even, odd, even_cols, odd_cols, *refs):
        del before, packed
        rows_kernel(
            grid_shape, field, coeff, even, odd, even, odd, even_cols, odd_cols, even_cols, odd_cols,
            None, None, *refs,
        )

    def rows_second(before, packed, *refs):
        del before, packed
        rows_kernel(grid_shape, *refs)

    def own_first(field, coeff, *refs):
        own_kernel(grid_shape, field, coeff, None, *refs)

    def own_second(field, coeff, across, shifts, table, entry, out, *pads):
        own_kernel(grid_shape, field, coeff, across, shifts, table, entry, out, None, None, *pads)

    rows0 = swap(*edge_rows(right_side, coefficient), "gy")
    w_own, ends, across = on_tensor_core(
        own_first, "own_first", (right_side, coefficient), scalars, (full, sums_of(2), full), own_pads,
        6,
    )
    cols0 = swap(*pack_sides(right_side, ends, True), "gx")
    packed = pack_corners(*rows0)
    corners0 = swap(*packed, "gx")
    w_rows, products, sides = on_tensor_core(
        rows_first, "rows_first", (w_own, packed[0], right_side, coefficient, *rows0, *cols0), scalars,
        (full, sums_of(3), side_pad), row_pads, 3, 1,
    )
    w_vec, _, sums, even, odd = on_tensor_core(
        bind(first_kernel), "first_apply",
        (w_rows, sides, right_side, coefficient, *cols0, *corners0, products), scalars,
        (full, side_pad, sums_of(3), edge, edge), [], 3, 2,
    )
    rows1 = swap(even, odd, "gy")
    (n_own,) = on_tensor_core(
        own_second, "own_second", (w_vec, coefficient, across), scalars, (full,), own_pads, 6
    )
    cols1 = swap(*pack_sides(w_vec, n_own, False), "gx")
    packed = pack_corners(*rows1)
    corners1 = swap(*packed, "gx")
    n_rows, products, sides = on_tensor_core(
        rows_second, "rows_second",
        (n_own, packed[0], w_vec, coefficient, *rows1, *rows0, *cols1, *cols0, right_side, sums),
        scalars, (full, sums_of(6), side_pad), row_pads, 3, 1,
    )
    n_vec, _, parts = on_tensor_core(
        bind(second_kernel), "second_apply",
        (n_rows, sides, right_side, w_vec, coefficient, *cols0, *corners1, products, sums), scalars,
        (full, side_pad, jax.ShapeDtypeStruct((devices, LANES), jnp.float32)), [], 3, 2,
    )
    gathered = lax.all_to_all(parts, ("gx", "gy"), 0, 0, tiled=True)
    return pl.pallas_call(
        last_kernel,
        out_shape=(full, full),
        in_specs=[VMEM_SPEC] * 4,
        out_specs=(pl.BlockSpec(memory_space=pltpu.HBM),) * 2,
        scratch_shapes=[
            pltpu.VMEM((layers, rows, cols), jnp.float32),
            pltpu.VMEM((layers, rows, cols), jnp.float32),
            pltpu.SemaphoreType.DMA((2, layers, PIECES)),
        ],
        compiler_params=pltpu.CompilerParams(vmem_limit_bytes=VMEM_BYTES),
        name="last_update",
    )(gathered, right_side, w_vec, n_vec)


def solution(mesh):
    placed = (P(None, "gy", "gx"), P(None, "gy", "gx"), P(), P(), P())
    return jax.shard_map(
        on_device,
        mesh=mesh,
        in_specs=placed,
        out_specs=(P(None, "gy", "gx"), P(None, "gy", "gx")),
        check_vma=False,
    )
```

```python
import functools

import jax
import jax.numpy as jnp
from jax import lax
from jax.experimental import pallas as pl
from jax.experimental.pallas import tpu as pltpu
from jax.sharding import PartitionSpec as P

SMAX = 32
REACH = 2 * SMAX
LANES = 128
HALF = 64
CHUNK = 32
UNROLL = 8
PIECES = 4
VMEM_BYTES = 32 * 1024 * 1024
EDGE_BYTES = 53 * 1024 * 1024
VMEM_SPEC = pl.BlockSpec(memory_space=pltpu.VMEM)
SMEM_SPEC = pl.BlockSpec(memory_space=pltpu.SMEM)


def even_swap(count):
    return [(i, i ^ 1) for i in range(count)]


def odd_swap(count):
    return [(i, i + 1 if i % 2 else i - 1) for i in range(1, count - 1)]


def is_odd(axis):
    return lax.rem(lax.axis_index(axis), 2) == 1


def swap(even, odd, axis):
    count = lax.axis_size(axis)
    return (
        lax.ppermute(even, axis, even_swap(count)),
        lax.ppermute(odd, axis, odd_swap(count)),
    )


def lane_of(shape):
    return lax.broadcasted_iota(jnp.int32, shape, 1)


def pack_columns(first, second, high):
    low_lanes = lane_of(first.shape) < HALF
    turned = pltpu.roll(second, HALF, 1)
    if high:
        return jnp.where(low_lanes, turned, first)
    return jnp.where(low_lanes, first, turned)


def packed_edges(load, cols):
    edges = (slice(0, LANES), slice(cols - LANES, cols))
    return [pack_columns(load(0, edge), load(1, edge), high) for high, edge in enumerate(edges)]


def store_packed(even_ref, odd_ref, start, low, high):
    odd = is_odd("gx")
    rows = low.shape[0]
    even_ref[start : start + rows, :] = jnp.where(odd, low, high)
    odd_ref[start : start + rows, :] = jnp.where(odd, high, low)


def pack_corners_kernel(even_rows, odd_rows, even_out, odd_out):
    cols = even_rows.shape[2]
    odd_y = is_odd("gy")
    for start, above in ((0, True), (REACH, False)):

        def halo(layer, edge, above=above):
            even = even_rows[layer, 0:REACH, edge]
            other = odd_rows[layer, 0:REACH, edge]
            return jnp.where(odd_y == above, even, other)

        store_packed(even_out, odd_out, start, *packed_edges(halo, cols))


def pack(kernel, operands, rows, name):
    out = jax.ShapeDtypeStruct((rows, LANES), jnp.float32)
    return pl.pallas_call(
        kernel,
        out_shape=(out, out),
        in_specs=[VMEM_SPEC] * len(operands),
        out_specs=(VMEM_SPEC,) * 2,
        compiler_params=pltpu.CompilerParams(vmem_limit_bytes=VMEM_BYTES),
        name=name,
    )(*operands)


def pack_corners(even_rows, odd_rows):
    return pack(pack_corners_kernel, (even_rows, odd_rows), 2 * REACH, "pack_corners")


def edge_kernel(field, coeff, even_out, odd_out, sems):
    rows = field.shape[1]
    odd_y = is_odd("gy")
    copies = []
    for index, (out, at_top) in enumerate(((even_out, odd_y), (odd_out, jnp.logical_not(odd_y)))):
        for part, (source, place, depth) in enumerate(((field, 0, REACH), (coeff, REACH, 8))):
            start = pl.multiple_of(jnp.where(at_top, 0, rows - depth), 8)
            copies.append(
                pltpu.make_async_copy(
                    source.at[:, pl.ds(start, depth), :],
                    out.at[:, pl.ds(place, depth), :],
                    sems.at[index, part],
                )
            )
    for copy in copies:
        copy.start()
    for copy in copies:
        copy.wait()


def edge_rows(field, coeff):
    layers, _, cols = field.shape
    out = jax.ShapeDtypeStruct((layers, REACH + 8, cols), jnp.float32)
    return pl.pallas_call(
        edge_kernel,
        out_shape=(out, out),
        in_specs=[pl.BlockSpec(memory_space=pltpu.HBM)] * 2,
        out_specs=(VMEM_SPEC,) * 2,
        scratch_shapes=[pltpu.SemaphoreType.DMA((2, 2))],
        compiler_params=pltpu.CompilerParams(vmem_limit_bytes=EDGE_BYTES),
        name="edge_rows",
    )(field, coeff)


def zero_rim(pad, depth, rows):
    zeros = jnp.zeros((depth, LANES), jnp.float32)
    for layer in range(2):
        for tile in range(pad.shape[1]):
            pad[layer, tile, 0:depth, :] = zeros
            pad[layer, tile, depth + rows :, :] = zeros


def fill_own(pad, depth, field):
    rows, cols = field.shape[1:]
    for layer in range(2):
        for tile in range(cols // LANES):
            lanes = slice(tile * LANES, (tile + 1) * LANES)
            pad[layer, tile, depth : depth + rows, :] = field[layer, :, lanes]


def move_across(tiles, step_c, lane):
    count = len(tiles)
    back = jnp.bitwise_and(LANES - step_c, LANES - 1)
    from_left = lane < jnp.where(step_c < 0, -step_c, 0)
    from_right = lane >= jnp.where(step_c < 0, LANES, LANES - step_c)
    turned = [0.0] + [pltpu.roll(tile, back, 1) for tile in tiles] + [0.0]
    return [
        jnp.where(from_left, turned[i], jnp.where(from_right, turned[i + 2], turned[i + 1]))
        for i in range(count)
    ]


def from_the_right(tiles, lane, last):
    ahead = [pltpu.roll(tile, LANES - 1, 1) for tile in tiles]
    return [
        jnp.where(lane == LANES - 1, after, tile)
        for tile, after in zip(ahead, [*ahead[1:], last], strict=True)
    ]


def near_end(row, rows):
    return row < SMAX or row + CHUNK > rows - SMAX


def apply_chunk(
    layer, row, pad, coeff_pad, across, across_out, shifts, weight, grid_shape, tile_shape
):
    rows, cols = tile_shape
    tiles = cols // LANES
    other = 1 - layer
    lane = lane_of((CHUNK, LANES))
    row_at = lax.broadcasted_iota(jnp.int32, (CHUNK, LANES), 0)
    first_row = lax.axis_index("gy") * rows + row
    first_col = lax.axis_index("gx") * cols
    cut = [slice(tile * LANES, (tile + 1) * LANES) for tile in range(tiles)]

    def at(ref, tile, start):
        return ref[layer, tile, pl.ds(start, CHUNK), :]

    own = [at(pad, tile, REACH + row) for tile in range(tiles)]
    own_c = [at(coeff_pad, tile, 8 + row) for tile in range(tiles)]
    if across is None:
        right_c = from_the_right(own_c, lane, 0.0)
        both = [a + b for a, b in zip(own_c, right_c, strict=True)]
        for value, lanes in zip(both, cut, strict=True):
            across_out[layer, pl.ds(row, CHUNK), lanes] = value
    else:
        both = [across[layer, pl.ds(row, CHUNK), lanes] for lanes in cut]
    right = from_the_right(own, lane, own[-1])
    flow = [c * (a - b) for c, a, b in zip(both, own, right, strict=True)]
    turned = [pltpu.roll(value, 1, 1) for value in flow]
    result = []
    for tile in range(tiles):
        value, coeff = own[tile], own_c[tile]
        above, below = at(pad, tile, REACH - 1 + row), at(pad, tile, REACH + 1 + row)
        above_c, below_c = at(coeff_pad, tile, 7 + row), at(coeff_pad, tile, 9 + row)
        total = (coeff + above_c) * (value - above) + (coeff + below_c) * (value - below)
        inflow = jnp.where(lane == 0, turned[tile - 1] if tile else 0.0, turned[tile])
        result.append(weight * (total + flow[tile] - inflow))
    for direction in range(shifts.shape[2]):
        shift_r, shift_c = shifts[layer, 0, direction], shifts[layer, 1, direction]
        start_r = REACH + row + shifts[other, 0, direction] - shift_r
        source = [pad[other, tile, pl.ds(start_r, CHUNK), :] for tile in range(tiles)]
        moved = move_across(source, shifts[other, 1, direction] - shift_c, lane)
        masks = [[] for _ in range(tiles)]
        masks[0].append(lane >= shift_c - first_col)
        masks[-1].append(lane < grid_shape[1] + shift_c - first_col - (tiles - 1) * LANES)
        if near_end(row, rows):
            image_row = row_at + (first_row - shift_r)
            inside = (image_row >= 0) & (image_row < grid_shape[0])
            for mask in masks:
                mask.append(inside)
        for tile in range(tiles):
            value = own[tile] + moved[tile]
            if masks[tile]:
                value = jnp.where(functools.reduce(jnp.logical_and, masks[tile]), value, 0.0)
            result[tile] = result[tile] + value
    return result


def fold(parts):
    total = sum(parts[1:], parts[0])
    pieces = [total[8 * i : 8 * i + 8] for i in range(total.shape[0] // 8)]
    return sum(pieces[1:], pieces[0])


def dot_of(first, second):
    return fold([a * b for a, b in zip(first, second, strict=True)])


def weight_of(table, entry, layer):
    return 0.5 * table[entry[layer]]


def packed_ends(coeff):
    ends = []
    rows, cols = coeff.shape[1:]
    lane = lane_of((8, LANES))
    for high, edge in enumerate((slice(0, LANES), slice(cols - LANES, cols))):
        packed = jnp.zeros((8, LANES), jnp.float32)
        for layer in range(2):
            for group in range(rows // 8):
                at = layer * (rows // 8) + group
                turn = (at + high) % LANES
                value = coeff[layer, 8 * group : 8 * group + 8, edge]
                value = pltpu.roll(value, turn, 1) if turn else value
                packed = jnp.where(lane == at, value, packed)
        ends.append(packed)
    return ends


def own_kernel(
    grid_shape, field, coeff, across, shifts, table, entry, out, even_side, odd_side, across_out, pad,
    coeff_pad,
):
    rows, cols = field.shape[1:]
    zero_rim(pad, REACH, rows)
    zero_rim(coeff_pad, 8, rows)
    fill_own(pad, REACH, field)
    fill_own(coeff_pad, 8, coeff)
    low, high = packed_edges(lambda layer, edge: field[layer, :, edge], cols)
    store_packed(even_side, odd_side, 0, low, high)
    if across is None:
        store_packed(even_side, odd_side, rows, *packed_ends(coeff))
    for layer in range(2):
        weight = weight_of(table, entry, layer)
        for row in range(0, rows, CHUNK):
            result = apply_chunk(
                layer, row, pad, coeff_pad, across, across_out, shifts, weight, grid_shape, (rows, cols)
            )
            for tile, value in enumerate(result):
                out[layer, row : row + CHUNK, tile * LANES : (tile + 1) * LANES] = value


def products_of(own, result, base, fit):
    if base is None:
        pairs = ((own, own), (own, result), (result, result))
    else:
        rest = [a - fit * b for a, b in zip(base, own, strict=True)]
        slope = [a - fit * b for a, b in zip(own, result, strict=True)]
        pairs = (
            (rest, rest), (rest, own), (slope, rest), (result, rest), (slope, own), (result, own),
        )
    return tuple(dot_of(*pair) for pair in pairs)


def fit_of(sums):
    gamma, delta, omega = (jnp.sum(sums[index], keepdims=True) for index in range(3))
    fit = jnp.where(omega > 0.0, delta / jnp.where(omega > 0.0, omega, 1.0), 0.0)
    return gamma, delta, omega, jnp.clip(fit, -1.0, 1.0)


def rows_kernel(
    grid_shape, field, coeff, even_rows, odd_rows, even_edge, odd_edge, even_cols, odd_cols, even_ends,
    odd_ends, base, sums, shifts, table, entry, out, products, side_pad, pad,
):
    rows, cols = field.shape[1:]
    tiles = cols // LANES
    odd_y = is_odd("gy")
    first_row = lax.axis_index("gy") * rows
    first_col = lax.axis_index("gx") * cols
    zeros = jnp.zeros((REACH, LANES), jnp.float32)
    for layer in range(2):
        for tile in range(tiles):
            lanes = slice(tile * LANES, (tile + 1) * LANES)
            even = even_rows[layer, 0:REACH, lanes]
            other = odd_rows[layer, 0:REACH, lanes]
            pad[layer, 0, tile, 0:REACH, :] = jnp.where(odd_y, even, other)
            pad[layer, 0, tile, REACH:, :] = zeros
            pad[layer, 1, tile, 0:REACH, :] = zeros
            pad[layer, 1, tile, REACH:, :] = jnp.where(odd_y, other, even)
    lane = lane_of((CHUNK, LANES))
    row_at = lax.broadcasted_iota(jnp.int32, (CHUNK, LANES), 0)
    for layer in range(2):
        other_layer = 1 - layer

        def step(i, carry, layer=layer, other_layer=other_layer):
            part = pl.multiple_of(i * CHUNK, CHUNK)
            totals = [[jnp.zeros((CHUNK, LANES), jnp.float32)] * tiles for _ in range(2)]
            for direction in range(shifts.shape[2]):
                shift_r, shift_c = shifts[layer, 0, direction], shifts[layer, 1, direction]
                step_r = shifts[other_layer, 0, direction] - shift_r
                side = jnp.where(step_r < 0, 0, 1)
                start_r = part + step_r + jnp.where(step_r < 0, REACH, 0)
                row = part + jnp.where(step_r < 0, 0, rows - REACH)
                source = [
                    pad[other_layer, side, tile, pl.ds(start_r, CHUNK), :] for tile in range(tiles)
                ]
                moved = move_across(source, shifts[other_layer, 1, direction] - shift_c, lane)
                image_row = row_at + (first_row + row - shift_r)
                inside = (image_row >= 0) & (image_row < grid_shape[0])
                upper = inside & (jnp.full((CHUNK, LANES), side, jnp.int32) == 0)
                lower = inside & (jnp.full((CHUNK, LANES), side, jnp.int32) == 1)
                for tile in range(tiles):
                    value = moved[tile]
                    if tile == 0:
                        value = jnp.where(lane >= shift_c - first_col, value, 0.0)
                    if tile == tiles - 1:
                        last = grid_shape[1] + shift_c - first_col - tile * LANES
                        value = jnp.where(lane < last, value, 0.0)
                    totals[0][tile] = totals[0][tile] + jnp.where(upper, value, 0.0)
                    totals[1][tile] = totals[1][tile] + jnp.where(lower, value, 0.0)
            for side, base in enumerate((0, rows - REACH)):
                for tile in range(tiles):
                    lanes = slice(tile * LANES, (tile + 1) * LANES)
                    out[layer, pl.ds(base + part, CHUNK), lanes] += totals[side][tile]
            return carry

        lax.fori_loop(0, REACH // CHUNK, step, 0, unroll=True)
        weight = weight_of(table, entry, layer)
        at = lax.broadcasted_iota(jnp.int32, (8, cols), 0)
        even = even_edge[layer, REACH : REACH + 8, :]
        other = odd_edge[layer, REACH : REACH + 8, :]
        even_v = [even_rows[layer, start : start + 8, :] for start in (0, REACH - 8)]
        other_v = [odd_rows[layer, start : start + 8, :] for start in (0, REACH - 8)]
        for start, edge_c, edge_v, spot, source in (
            (0, jnp.where(odd_y, even, other), jnp.where(odd_y, even_v[1], other_v[1]), 0, 1),
            (
                rows - 8, jnp.where(odd_y, other, even), jnp.where(odd_y, other_v[0], even_v[0]),
                7, 7,
            ),
        ):
            edge_c = pltpu.roll(edge_c, source, 0)
            edge_v = pltpu.roll(edge_v, source, 0)
            value = field[layer, start : start + 8, :]
            own_c = coeff[layer, start : start + 8, :]
            extra = weight * (edge_c * value - (own_c + edge_c) * edge_v)
            out[layer, start : start + 8, :] += jnp.where(at == spot, extra, 0.0)
    fit = None if base is None else fit_of(sums)[3]
    carry = (jnp.zeros((8, LANES), jnp.float32),) * products.shape[0]
    inner = [slice(tile * LANES, (tile + 1) * LANES) for tile in range(1, tiles - 1)]
    for layer in range(2):

        def add(i, carry, layer=layer):
            chunk = pl.ds(pl.multiple_of(i * CHUNK, CHUNK), CHUNK)
            start, own, result = (
                None if ref is None else [ref[layer, chunk, lanes] for lanes in inner]
                for ref in (base, field, out)
            )
            more = products_of(own, result, start, fit)
            return tuple(a + b for a, b in zip(carry, more, strict=True))

        carry = lax.fori_loop(0, rows // CHUNK, add, carry, unroll=UNROLL)
    fill_sides(side_pad, even_cols, odd_cols, 0, REACH, rows)
    carry = finish(
        range(REACH // CHUNK, (rows - REACH) // CHUNK), carry, grid_shape, base, fit, field, coeff,
        even_ends, odd_ends, shifts, table, entry, out, side_pad,
    )
    for index, value in enumerate(carry):
        products[index] = value


def finish_chunk(grid_shape, layer, row, field, coeff, out, pad, ends, shifts, weight):
    rows, cols = field.shape[1:]
    tiles = cols // LANES
    first_row = lax.axis_index("gy") * rows + row
    first_col = lax.axis_index("gx") * cols
    lane = lane_of((CHUNK, LANES))
    row_at = lax.broadcasted_iota(jnp.int32, (CHUNK, LANES), 0)
    cut = (slice(0, LANES), slice(cols - LANES, cols))
    own = [field[layer, pl.ds(row, CHUNK), lanes] for lanes in cut]
    result = []
    for side, spot in ((0, 0), (1, LANES - 1)):
        at = layer * (rows // 8) + row // 8
        edge_c = jnp.concatenate(
            [
                pltpu.roll(ends[side], (spot - at - i) % LANES, 1)
                for i in range(CHUNK // 8)
            ]
        )
        edge_v = pad[layer, side, pl.ds(REACH + row, CHUNK), :]
        edge_v = pltpu.roll(edge_v, LANES - 1 if side else 1, 1)
        own_c = coeff[layer, pl.ds(row, CHUNK), cut[side]]
        extra = weight * ((own_c + edge_c) * (own[side] - edge_v))
        extra = jnp.where(lane == spot, extra, 0.0)
        result.append(out[layer, pl.ds(row, CHUNK), cut[side]] + extra)
    for direction in range(shifts.shape[2]):
        shift_r, shift_c = shifts[layer, 0, direction], shifts[layer, 1, direction]
        start_r = REACH + row + shifts[1 - layer, 0, direction] - shift_r
        step_c = shifts[1 - layer, 1, direction] - shift_c
        side = jnp.where(step_c < 0, 0, 1)
        back = jnp.bitwise_and(LANES - step_c, LANES - 1)
        moved = pltpu.roll(pad[1 - layer, side, pl.ds(start_r, CHUNK), :], back, 1)
        if near_end(row, rows):
            image_row = row_at + (first_row - shift_r)
            moved = jnp.where((image_row >= 0) & (image_row < grid_shape[0]), moved, 0.0)
        low, low_end = shift_c - first_col, jnp.where(step_c < 0, -step_c, 0)
        high = jnp.where(step_c < 0, LANES, LANES - step_c)
        high_end = grid_shape[1] + shift_c - first_col - (tiles - 1) * LANES
        result[0] = result[0] + jnp.where((lane >= low) & (lane < low_end), moved, 0.0)
        result[1] = result[1] + jnp.where((lane >= high) & (lane < high_end), moved, 0.0)
    for side in range(2):
        out[layer, pl.ds(row, CHUNK), cut[side]] = result[side]
    return own, result


def fill_sides(pad, even_ref, odd_ref, start, place, depth):
    odd_x = is_odd("gx")
    even, other = even_ref[start : start + depth, :], odd_ref[start : start + depth, :]
    for side, packed in ((0, jnp.where(odd_x, even, other)), (1, jnp.where(odd_x, other, even))):
        pad[0, side, place : place + depth, :] = packed
        pad[1, side, place : place + depth, :] = pltpu.roll(packed, HALF, 1)


def finish(
    chunks, carry, grid_shape, base, fit, field, coeff, even_ends, odd_ends, shifts, table, entry, out,
    pad,
):
    rows, cols = field.shape[1:]
    odd_x = is_odd("gx")
    even, other = even_ends[rows : rows + 8, :], odd_ends[rows : rows + 8, :]
    ends = (jnp.where(odd_x, even, other), jnp.where(odd_x, other, even))
    cut = (slice(0, LANES), slice(cols - LANES, cols))
    for layer in range(2):
        weight = weight_of(table, entry, layer)
        for row in (chunk * CHUNK for chunk in chunks):
            own, result = finish_chunk(
                grid_shape, layer, row, field, coeff, out, pad, ends, shifts, weight
            )
            start = None if base is None else [base[layer, row : row + CHUNK, x] for x in cut]
            more = products_of(own, result, start, fit)
            carry = tuple(a + b for a, b in zip(carry, more, strict=True))
    return carry


def finish_ends(grid_shape, even_corners, odd_corners, products, pad, field, *rest):
    rows = field.shape[1]
    fill_sides(pad, even_corners, odd_corners, 0, 0, REACH)
    fill_sides(pad, even_corners, odd_corners, REACH, REACH + rows, REACH)
    depth = REACH // CHUNK
    chunks = [*range(depth), *range(rows // CHUNK - depth, rows // CHUNK)]
    carry = tuple(products[index] for index in range(products.shape[0]))
    base, fit, *others = rest
    return finish(chunks, carry, grid_shape, base, fit, field, *others, pad)


def first_kernel(
    grid_shape, before, pad_before, field, coeff, even_ends, odd_ends, even_corners, odd_corners,
    products, shifts, table, entry, out, pad, sums, even_out, odd_out,
):
    del before, pad_before
    rows = field.shape[1]
    carry = finish_ends(
        grid_shape, even_corners, odd_corners, products, pad, field, None, None, coeff, even_ends,
        odd_ends, shifts, table, entry, out,
    )
    for index, value in enumerate(carry):
        sums[index] = value
    odd_y = is_odd("gy")
    low, high = out[:, 0:REACH, :], out[:, rows - REACH :, :]
    even_out[...] = jnp.where(odd_y, low, high)
    odd_out[...] = jnp.where(odd_y, high, low)


def second_kernel(
    grid_shape, before, pad_before, base, field, coeff, even_ends, odd_ends, even_corners, odd_corners,
    products, sums, shifts, table, entry, out, pad, parts,
):
    del before, pad_before
    gamma, delta, omega, fit = fit_of(sums)
    carry = finish_ends(
        grid_shape, even_corners, odd_corners, products, pad, field, base, fit, coeff, even_ends,
        odd_ends, shifts, table, entry, out,
    )
    rest2, rest_w, slope_rest, n_rest, slope_w, n_w = (
        jnp.sum(value, keepdims=True) for value in carry
    )
    lane = lane_of((8, LANES))
    row = jnp.zeros((8, LANES), jnp.float32)
    for at, value in (
        (0, rest2), (1, slope_rest), (8, 2.0 * rest_w), (9, n_rest + slope_w),
        (16, omega), (17, n_w), (24, fit), (25, fit), (32, gamma), (33, delta),
    ):
        row = jnp.where(lane == at, value, row)
    for start in range(0, parts.shape[0], 8):
        parts[start : start + 8, :] = row


def pick(row, lane, at):
    return jnp.sum(jnp.where(lane == at, row, 0.0), keepdims=True)


def last_kernel(
    parts, base, w_vec, n_vec, solution_out, residual_out, solution_part, residual_part, sems
):
    gathered = parts[...]
    count = gathered.shape[0]
    lane = lane_of((8, LANES))
    total = sum(gathered[8 * i : 8 * i + 8] for i in range(count // 8))
    gamma, delta = pick(total, lane, 32), pick(total, lane, 33)
    alpha = gamma / delta
    gap = alpha - pltpu.roll(gathered, LANES - 24, 1)
    moved = gathered - gap * pltpu.roll(gathered, LANES - 8, 1)
    moved = moved + gap * gap * pltpu.roll(gathered, LANES - 16, 1)
    total = sum(moved[8 * i : 8 * i + 8] for i in range(count // 8))
    gamma_next, delta_next = pick(total, lane, 0), pick(total, lane, 1)
    beta = gamma_next / gamma
    alpha_next = gamma_next / (delta_next - beta * gamma_next / alpha)
    layers, rows = base.shape[:2]
    depth = rows // PIECES
    copies = []
    for layer in range(layers):
        for piece in range(PIECES):
            part = pl.ds(piece * depth, depth)
            start, w_start = base[layer, part, :], w_vec[layer, part, :]
            residual = start - alpha * w_start
            w_next = w_start - alpha * n_vec[layer, part, :]
            solution_part[layer, part, :] = alpha * start + alpha_next * (residual + beta * start)
            residual_part[layer, part, :] = residual - alpha_next * (w_next + beta * w_start)
            for which, (source, target) in enumerate(
                ((solution_part, solution_out), (residual_part, residual_out))
            ):
                copy = pltpu.make_async_copy(
                    source.at[layer, part, :],
                    target.at[layer, part, :],
                    sems.at[which, layer, piece],
                )
                copy.start()
                copies.append(copy)
    for copy in copies:
        copy.wait()


def on_tensor_core(kernel, name, operands, scalars, out_shape, scratch, microseconds, in_place=0):
    return pl.pallas_call(
        kernel,
        out_shape=out_shape,
        in_specs=[VMEM_SPEC] * len(operands) + [SMEM_SPEC] * len(scalars),
        out_specs=(VMEM_SPEC,) * len(out_shape),
        scratch_shapes=[pltpu.VMEM(shape, jnp.float32) for shape in scratch],
        input_output_aliases={index: index for index in range(in_place)},
        compiler_params=pltpu.CompilerParams(vmem_limit_bytes=VMEM_BYTES),
        cost_estimate=pl.CostEstimate(
            flops=0, bytes_accessed=3_000_000 * microseconds, transcendentals=0
        ),
        name=name,
    )(*operands, *scalars)


def on_device(right_side, coefficient, strength_table, layer_entry, shifts):
    layers, rows, cols = right_side.shape
    count_y, count_x = lax.axis_size("gy"), lax.axis_size("gx")
    devices = count_x * count_y
    tiles = cols // LANES
    grid_shape = (rows * count_y, cols * count_x)
    full = jax.ShapeDtypeStruct((layers, rows, cols), jnp.float32)
    edge = jax.ShapeDtypeStruct((layers, REACH, cols), jnp.float32)
    scalars = (jnp.transpose(shifts, (1, 2, 0)), strength_table, layer_entry)
    own_pads = [(2, tiles, rows + 2 * REACH, LANES), (2, tiles, rows + 16, LANES)]
    row_pads = [(2, 2, tiles, 2 * REACH, LANES)]
    side_pad = jax.ShapeDtypeStruct((2, 2, rows + 2 * REACH, LANES), jnp.float32)

    def side_of(count):
        return jax.ShapeDtypeStruct((count, LANES), jnp.float32)

    def sums_of(count):
        return jax.ShapeDtypeStruct((count, 8, LANES), jnp.float32)

    def bind(kernel):
        def bound(*refs):
            kernel(grid_shape, *refs)

        return bound

    def rows_first(before, packed, field, coeff, even, odd, even_cols, odd_cols, *refs):
        del before, packed
        rows_kernel(
            grid_shape, field, coeff, even, odd, even, odd, even_cols, odd_cols, even_cols, odd_cols,
            None, None, *refs,
        )

    def rows_second(before, packed, *refs):
        del before, packed
        rows_kernel(grid_shape, *refs)

    def own_first(field, coeff, *refs):
        own_kernel(grid_shape, field, coeff, None, *refs)

    def own_second(field, coeff, across, shifts, table, entry, out, even, odd, *pads):
        own_kernel(grid_shape, field, coeff, across, shifts, table, entry, out, even, odd, None, *pads)

    rows0 = swap(*edge_rows(right_side, coefficient), "gy")
    w_own, *columns, across = on_tensor_core(
        own_first, "own_first", (right_side, coefficient), scalars,
        (full, side_of(rows + 8), side_of(rows + 8), full), own_pads, 6,
    )
    cols0 = swap(*columns, "gx")
    packed = pack_corners(*rows0)
    corners0 = swap(*packed, "gx")
    w_rows, products, sides = on_tensor_core(
        rows_first, "rows_first", (w_own, packed[0], right_side, coefficient, *rows0, *cols0), scalars,
        (full, sums_of(3), side_pad), row_pads, 3, 1,
    )
    w_vec, _, sums, even, odd = on_tensor_core(
        bind(first_kernel), "first_apply",
        (w_rows, sides, right_side, coefficient, *cols0, *corners0, products), scalars,
        (full, side_pad, sums_of(3), edge, edge), [], 3, 2,
    )
    rows1 = swap(even, odd, "gy")
    n_own, *columns = on_tensor_core(
        own_second, "own_second", (w_vec, coefficient, across), scalars,
        (full, side_of(rows), side_of(rows)), own_pads, 6,
    )
    cols1 = swap(*columns, "gx")
    packed = pack_corners(*rows1)
    corners1 = swap(*packed, "gx")
    n_rows, products, sides = on_tensor_core(
        rows_second, "rows_second",
        (n_own, packed[0], w_vec, coefficient, *rows1, *rows0, *cols1, *cols0, right_side, sums),
        scalars, (full, sums_of(6), side_pad), row_pads, 3, 1,
    )
    n_vec, _, parts = on_tensor_core(
        bind(second_kernel), "second_apply",
        (n_rows, sides, right_side, w_vec, coefficient, *cols0, *corners1, products, sums), scalars,
        (full, side_pad, jax.ShapeDtypeStruct((devices, LANES), jnp.float32)), [], 3, 2,
    )
    gathered = lax.all_to_all(parts, ("gx", "gy"), 0, 0, tiled=True)
    return pl.pallas_call(
        last_kernel,
        out_shape=(full, full),
        in_specs=[VMEM_SPEC] * 4,
        out_specs=(pl.BlockSpec(memory_space=pltpu.HBM),) * 2,
        scratch_shapes=[
            pltpu.VMEM((layers, rows, cols), jnp.float32),
            pltpu.VMEM((layers, rows, cols), jnp.float32),
            pltpu.SemaphoreType.DMA((2, layers, PIECES)),
        ],
        compiler_params=pltpu.CompilerParams(vmem_limit_bytes=VMEM_BYTES),
        name="last_update",
    )(gathered, right_side, w_vec, n_vec)


def solution(mesh):
    placed = (P(None, "gy", "gx"), P(None, "gy", "gx"), P(), P(), P())
    return jax.shard_map(
        on_device,
        mesh=mesh,
        in_specs=placed,
        out_specs=(P(None, "gy", "gx"), P(None, "gy", "gx")),
        check_vma=False,
    )
```

```python
import functools

import jax
import jax.numpy as jnp
from jax import lax
from jax.experimental import pallas as pl
from jax.experimental.pallas import tpu as pltpu
from jax.sharding import PartitionSpec as P

SMAX = 32
REACH = 2 * SMAX
LANES = 128
HALF = 64
CHUNK = 32
OWN_CHUNK = 64
UNROLL = 8
PIECES = 4
VMEM_BYTES = 32 * 1024 * 1024
EDGE_BYTES = 53 * 1024 * 1024
VMEM_SPEC = pl.BlockSpec(memory_space=pltpu.VMEM)
SMEM_SPEC = pl.BlockSpec(memory_space=pltpu.SMEM)


def pairs_from(start, count):
    low = range(start, count - 1, 2)
    return [(i, i + 1) for i in low] + [(i + 1, i) for i in low]


FIRST = {"gy": 1, "gx": 0}


def is_odd(axis):
    return lax.rem(lax.axis_index(axis) + FIRST[axis], 2) == 1


def swap(even, odd, axis):
    count = lax.axis_size(axis)
    return (
        lax.ppermute(even, axis, pairs_from(FIRST[axis], count)),
        lax.ppermute(odd, axis, pairs_from(1 - FIRST[axis], count)),
    )


def lane_of(shape):
    return lax.broadcasted_iota(jnp.int32, shape, 1)


def pack_columns(first, second, high):
    low_lanes = lane_of(first.shape) < HALF
    turned = pltpu.roll(second, HALF, 1)
    if high:
        return jnp.where(low_lanes, turned, first)
    return jnp.where(low_lanes, first, turned)


def packed_edges(load, cols):
    edges = (slice(0, LANES), slice(cols - LANES, cols))
    return [pack_columns(load(0, edge), load(1, edge), high) for high, edge in enumerate(edges)]


def store_packed(even_ref, odd_ref, start, low, high):
    odd = is_odd("gx")
    rows = low.shape[0]
    even_ref[start : start + rows, :] = jnp.where(odd, low, high)
    odd_ref[start : start + rows, :] = jnp.where(odd, high, low)


def pack_corners_kernel(even_rows, odd_rows, even_out, odd_out):
    cols = even_rows.shape[2]
    odd_y = is_odd("gy")
    for start, above in ((0, True), (REACH, False)):

        def halo(layer, edge, above=above):
            even = even_rows[layer, 0:REACH, edge]
            other = odd_rows[layer, 0:REACH, edge]
            return jnp.where(odd_y == above, even, other)

        store_packed(even_out, odd_out, start, *packed_edges(halo, cols))


def pack(kernel, operands, rows, name):
    out = jax.ShapeDtypeStruct((rows, LANES), jnp.float32)
    return pl.pallas_call(
        kernel,
        out_shape=(out, out),
        in_specs=[VMEM_SPEC] * len(operands),
        out_specs=(VMEM_SPEC,) * 2,
        compiler_params=pltpu.CompilerParams(vmem_limit_bytes=VMEM_BYTES),
        name=name,
    )(*operands)


def pack_corners(even_rows, odd_rows):
    return pack(pack_corners_kernel, (even_rows, odd_rows), 2 * REACH, "pack_corners")


def edge_kernel(field, coeff, even_out, odd_out, sems):
    rows = field.shape[1]
    odd_y = is_odd("gy")
    copies = []
    for index, (out, at_top) in enumerate(((even_out, odd_y), (odd_out, jnp.logical_not(odd_y)))):
        for part, (source, place, depth) in enumerate(((field, 0, REACH), (coeff, REACH, 8))):
            start = pl.multiple_of(jnp.where(at_top, 0, rows - depth), 8)
            copies.append(
                pltpu.make_async_copy(
                    source.at[:, pl.ds(start, depth), :],
                    out.at[:, pl.ds(place, depth), :],
                    sems.at[index, part],
                )
            )
    for copy in copies:
        copy.start()
    for copy in copies:
        copy.wait()


def edge_rows(field, coeff):
    layers, _, cols = field.shape
    out = jax.ShapeDtypeStruct((layers, REACH + 8, cols), jnp.float32)
    return pl.pallas_call(
        edge_kernel,
        out_shape=(out, out),
        in_specs=[pl.BlockSpec(memory_space=pltpu.HBM)] * 2,
        out_specs=(VMEM_SPEC,) * 2,
        scratch_shapes=[pltpu.SemaphoreType.DMA((2, 2))],
        compiler_params=pltpu.CompilerParams(vmem_limit_bytes=EDGE_BYTES),
        name="edge_rows",
    )(field, coeff)


def zero_rim(pad, depth, rows):
    zeros = jnp.zeros((depth, LANES), jnp.float32)
    for layer in range(2):
        for tile in range(pad.shape[1]):
            pad[layer, tile, 0:depth, :] = zeros
            pad[layer, tile, depth + rows :, :] = zeros


def fill_own(pad, depth, field):
    rows, cols = field.shape[1:]
    for layer in range(2):
        for tile in range(cols // LANES):
            lanes = slice(tile * LANES, (tile + 1) * LANES)
            pad[layer, tile, depth : depth + rows, :] = field[layer, :, lanes]


def move_across(tiles, step_c, lane):
    count = len(tiles)
    back = jnp.bitwise_and(LANES - step_c, LANES - 1)
    from_left = lane < jnp.where(step_c < 0, -step_c, 0)
    from_right = lane >= jnp.where(step_c < 0, LANES, LANES - step_c)
    turned = [0.0] + [pltpu.roll(tile, back, 1) for tile in tiles] + [0.0]
    return [
        jnp.where(from_left, turned[i], jnp.where(from_right, turned[i + 2], turned[i + 1]))
        for i in range(count)
    ]


def from_the_right(tiles, lane, last):
    ahead = [pltpu.roll(tile, LANES - 1, 1) for tile in tiles]
    return [
        jnp.where(lane == LANES - 1, after, tile)
        for tile, after in zip(ahead, [*ahead[1:], last], strict=True)
    ]


def near_end(row, depth, rows):
    return row < SMAX or row + depth > rows - SMAX


def apply_chunk(
    layer, row, pad, coeff_pad, across, across_out, shifts, weight, grid_shape, tile_shape
):
    rows, cols = tile_shape
    tiles = cols // LANES
    other = 1 - layer
    lane = lane_of((OWN_CHUNK, LANES))
    row_at = lax.broadcasted_iota(jnp.int32, (OWN_CHUNK, LANES), 0)
    first_row = lax.axis_index("gy") * rows + row
    first_col = lax.axis_index("gx") * cols
    cut = [slice(tile * LANES, (tile + 1) * LANES) for tile in range(tiles)]

    def at(ref, tile, start):
        return ref[layer, tile, pl.ds(start, OWN_CHUNK), :]

    own = [at(pad, tile, REACH + row) for tile in range(tiles)]
    own_c = [at(coeff_pad, tile, 8 + row) for tile in range(tiles)]
    if across is None:
        right_c = from_the_right(own_c, lane, 0.0)
        both = [a + b for a, b in zip(own_c, right_c, strict=True)]
        for value, lanes in zip(both, cut, strict=True):
            across_out[layer, pl.ds(row, OWN_CHUNK), lanes] = value
    else:
        both = [across[layer, pl.ds(row, OWN_CHUNK), lanes] for lanes in cut]
    right = from_the_right(own, lane, own[-1])
    flow = [c * (a - b) for c, a, b in zip(both, own, right, strict=True)]
    turned = [pltpu.roll(value, 1, 1) for value in flow]
    result = []
    for tile in range(tiles):
        value, coeff = own[tile], own_c[tile]
        above, below = at(pad, tile, REACH - 1 + row), at(pad, tile, REACH + 1 + row)
        above_c, below_c = at(coeff_pad, tile, 7 + row), at(coeff_pad, tile, 9 + row)
        total = (coeff + above_c) * (value - above) + (coeff + below_c) * (value - below)
        inflow = jnp.where(lane == 0, turned[tile - 1] if tile else 0.0, turned[tile])
        result.append(weight * (total + flow[tile] - inflow))
    for direction in range(shifts.shape[2]):
        shift_r, shift_c = shifts[layer, 0, direction], shifts[layer, 1, direction]
        start_r = REACH + row + shifts[other, 0, direction] - shift_r
        source = [pad[other, tile, pl.ds(start_r, OWN_CHUNK), :] for tile in range(tiles)]
        moved = move_across(source, shifts[other, 1, direction] - shift_c, lane)
        masks = [[] for _ in range(tiles)]
        masks[0].append(lane >= shift_c - first_col)
        masks[-1].append(lane < grid_shape[1] + shift_c - first_col - (tiles - 1) * LANES)
        if near_end(row, OWN_CHUNK, rows):
            image_row = row_at + (first_row - shift_r)
            inside = (image_row >= 0) & (image_row < grid_shape[0])
            for mask in masks:
                mask.append(inside)
        for tile in range(tiles):
            value = own[tile] + moved[tile]
            if masks[tile]:
                value = jnp.where(functools.reduce(jnp.logical_and, masks[tile]), value, 0.0)
            result[tile] = result[tile] + value
    return result


def fold(parts):
    total = sum(parts[1:], parts[0])
    pieces = [total[8 * i : 8 * i + 8] for i in range(total.shape[0] // 8)]
    return sum(pieces[1:], pieces[0])


def dot_of(first, second):
    return fold([a * b for a, b in zip(first, second, strict=True)])


def weight_of(table, entry, layer):
    return 0.5 * table[entry[layer]]


def packed_ends(coeff):
    ends = []
    rows, cols = coeff.shape[1:]
    lane = lane_of((8, LANES))
    for high, edge in enumerate((slice(0, LANES), slice(cols - LANES, cols))):
        packed = jnp.zeros((8, LANES), jnp.float32)
        for layer in range(2):
            for group in range(rows // 8):
                at = layer * (rows // 8) + group
                turn = (at + high) % LANES
                value = coeff[layer, 8 * group : 8 * group + 8, edge]
                value = pltpu.roll(value, turn, 1) if turn else value
                packed = jnp.where(lane == at, value, packed)
        ends.append(packed)
    return ends


def own_kernel(
    grid_shape, field, coeff, across, shifts, table, entry, out, even_side, odd_side, across_out,
    coeff_pad, pad,
):
    rows, cols = field.shape[1:]
    zero_rim(pad, REACH, rows)
    fill_own(pad, REACH, field)
    low, high = packed_edges(lambda layer, edge: field[layer, :, edge], cols)
    store_packed(even_side, odd_side, 0, low, high)
    if across is None:
        zero_rim(coeff_pad, 8, rows)
        fill_own(coeff_pad, 8, coeff)
        store_packed(even_side, odd_side, rows, *packed_ends(coeff))
    for layer in range(2):
        weight = weight_of(table, entry, layer)
        for row in range(0, rows, OWN_CHUNK):
            result = apply_chunk(
                layer, row, pad, coeff_pad, across, across_out, shifts, weight, grid_shape, (rows, cols)
            )
            for tile, value in enumerate(result):
                out[layer, row : row + OWN_CHUNK, tile * LANES : (tile + 1) * LANES] = value


def products_of(own, result, base, fit):
    if base is None:
        pairs = ((own, own), (own, result), (result, result))
    else:
        rest = [a - fit * b for a, b in zip(base, own, strict=True)]
        slope = [a - fit * b for a, b in zip(own, result, strict=True)]
        pairs = (
            (rest, rest), (rest, own), (slope, rest), (result, rest), (slope, own), (result, own),
        )
    return tuple(dot_of(*pair) for pair in pairs)


def fit_of(sums):
    gamma, delta, omega = (jnp.sum(sums[index], keepdims=True) for index in range(3))
    fit = jnp.where(omega > 0.0, delta / jnp.where(omega > 0.0, omega, 1.0), 0.0)
    return gamma, delta, omega, jnp.clip(fit, -1.0, 1.0)


def rows_kernel(
    grid_shape, field, coeff, even_rows, odd_rows, even_edge, odd_edge, even_cols, odd_cols, even_ends,
    odd_ends, base, sums, shifts, table, entry, out, products, side_pad, pad,
):
    rows, cols = field.shape[1:]
    tiles = cols // LANES
    odd_y = is_odd("gy")
    first_row = lax.axis_index("gy") * rows
    first_col = lax.axis_index("gx") * cols
    zeros = jnp.zeros((REACH, LANES), jnp.float32)
    for layer in range(2):
        for tile in range(tiles):
            lanes = slice(tile * LANES, (tile + 1) * LANES)
            even = even_rows[layer, 0:REACH, lanes]
            other = odd_rows[layer, 0:REACH, lanes]
            pad[layer, 0, tile, 0:REACH, :] = jnp.where(odd_y, even, other)
            pad[layer, 0, tile, REACH:, :] = zeros
            pad[layer, 1, tile, 0:REACH, :] = zeros
            pad[layer, 1, tile, REACH:, :] = jnp.where(odd_y, other, even)
    lane = lane_of((CHUNK, LANES))
    row_at = lax.broadcasted_iota(jnp.int32, (CHUNK, LANES), 0)
    for layer in range(2):
        other_layer = 1 - layer

        def step(i, carry, layer=layer, other_layer=other_layer):
            part = pl.multiple_of(i * CHUNK, CHUNK)
            totals = [[jnp.zeros((CHUNK, LANES), jnp.float32)] * tiles for _ in range(2)]
            for direction in range(shifts.shape[2]):
                shift_r, shift_c = shifts[layer, 0, direction], shifts[layer, 1, direction]
                step_r = shifts[other_layer, 0, direction] - shift_r
                side = jnp.where(step_r < 0, 0, 1)
                start_r = part + step_r + jnp.where(step_r < 0, REACH, 0)
                row = part + jnp.where(step_r < 0, 0, rows - REACH)
                source = [
                    pad[other_layer, side, tile, pl.ds(start_r, CHUNK), :] for tile in range(tiles)
                ]
                moved = move_across(source, shifts[other_layer, 1, direction] - shift_c, lane)
                image_row = row_at + (first_row + row - shift_r)
                inside = (image_row >= 0) & (image_row < grid_shape[0])
                upper = inside & (jnp.full((CHUNK, LANES), side, jnp.int32) == 0)
                lower = inside & (jnp.full((CHUNK, LANES), side, jnp.int32) == 1)
                for tile in range(tiles):
                    value = moved[tile]
                    if tile == 0:
                        value = jnp.where(lane >= shift_c - first_col, value, 0.0)
                    if tile == tiles - 1:
                        last = grid_shape[1] + shift_c - first_col - tile * LANES
                        value = jnp.where(lane < last, value, 0.0)
                    totals[0][tile] = totals[0][tile] + jnp.where(upper, value, 0.0)
                    totals[1][tile] = totals[1][tile] + jnp.where(lower, value, 0.0)
            for side, base in enumerate((0, rows - REACH)):
                for tile in range(tiles):
                    lanes = slice(tile * LANES, (tile + 1) * LANES)
                    out[layer, pl.ds(base + part, CHUNK), lanes] += totals[side][tile]
            return carry

        lax.fori_loop(0, REACH // CHUNK, step, 0, unroll=True)
        weight = weight_of(table, entry, layer)
        at = lax.broadcasted_iota(jnp.int32, (8, cols), 0)
        even = even_edge[layer, REACH : REACH + 8, :]
        other = odd_edge[layer, REACH : REACH + 8, :]
        even_v = [even_rows[layer, start : start + 8, :] for start in (0, REACH - 8)]
        other_v = [odd_rows[layer, start : start + 8, :] for start in (0, REACH - 8)]
        for start, edge_c, edge_v, spot, source in (
            (0, jnp.where(odd_y, even, other), jnp.where(odd_y, even_v[1], other_v[1]), 0, 1),
            (
                rows - 8, jnp.where(odd_y, other, even), jnp.where(odd_y, other_v[0], even_v[0]),
                7, 7,
            ),
        ):
            edge_c = pltpu.roll(edge_c, source, 0)
            edge_v = pltpu.roll(edge_v, source, 0)
            value = field[layer, start : start + 8, :]
            own_c = coeff[layer, start : start + 8, :]
            extra = weight * (edge_c * value - (own_c + edge_c) * edge_v)
            out[layer, start : start + 8, :] += jnp.where(at == spot, extra, 0.0)
    fit = None if base is None else fit_of(sums)[3]
    carry = (jnp.zeros((8, LANES), jnp.float32),) * products.shape[0]
    inner = [slice(tile * LANES, (tile + 1) * LANES) for tile in range(1, tiles - 1)]
    for layer in range(2):

        def add(i, carry, layer=layer):
            chunk = pl.ds(pl.multiple_of(i * CHUNK, CHUNK), CHUNK)
            start, own, result = (
                None if ref is None else [ref[layer, chunk, lanes] for lanes in inner]
                for ref in (base, field, out)
            )
            more = products_of(own, result, start, fit)
            return tuple(a + b for a, b in zip(carry, more, strict=True))

        carry = lax.fori_loop(0, rows // CHUNK, add, carry, unroll=UNROLL)
    fill_sides(side_pad, even_cols, odd_cols, 0, REACH, rows)
    carry = finish(
        range(REACH // CHUNK, (rows - REACH) // CHUNK), carry, grid_shape, base, fit, field, coeff,
        even_ends, odd_ends, shifts, table, entry, out, side_pad,
    )
    for index, value in enumerate(carry):
        products[index] = value


def finish_chunk(grid_shape, layer, row, field, coeff, out, pad, ends, shifts, weight):
    rows, cols = field.shape[1:]
    tiles = cols // LANES
    first_row = lax.axis_index("gy") * rows + row
    first_col = lax.axis_index("gx") * cols
    lane = lane_of((CHUNK, LANES))
    row_at = lax.broadcasted_iota(jnp.int32, (CHUNK, LANES), 0)
    cut = (slice(0, LANES), slice(cols - LANES, cols))
    own = [field[layer, pl.ds(row, CHUNK), lanes] for lanes in cut]
    result = []
    for side, spot in ((0, 0), (1, LANES - 1)):
        at = layer * (rows // 8) + row // 8
        edge_c = jnp.concatenate(
            [
                pltpu.roll(ends[side], (spot - at - i) % LANES, 1)
                for i in range(CHUNK // 8)
            ]
        )
        edge_v = pad[layer, side, pl.ds(REACH + row, CHUNK), :]
        edge_v = pltpu.roll(edge_v, LANES - 1 if side else 1, 1)
        own_c = coeff[layer, pl.ds(row, CHUNK), cut[side]]
        extra = weight * ((own_c + edge_c) * (own[side] - edge_v))
        extra = jnp.where(lane == spot, extra, 0.0)
        result.append(out[layer, pl.ds(row, CHUNK), cut[side]] + extra)
    for direction in range(shifts.shape[2]):
        shift_r, shift_c = shifts[layer, 0, direction], shifts[layer, 1, direction]
        start_r = REACH + row + shifts[1 - layer, 0, direction] - shift_r
        step_c = shifts[1 - layer, 1, direction] - shift_c
        side = jnp.where(step_c < 0, 0, 1)
        back = jnp.bitwise_and(LANES - step_c, LANES - 1)
        moved = pltpu.roll(pad[1 - layer, side, pl.ds(start_r, CHUNK), :], back, 1)
        if near_end(row, CHUNK, rows):
            image_row = row_at + (first_row - shift_r)
            moved = jnp.where((image_row >= 0) & (image_row < grid_shape[0]), moved, 0.0)
        low, low_end = shift_c - first_col, jnp.where(step_c < 0, -step_c, 0)
        high = jnp.where(step_c < 0, LANES, LANES - step_c)
        high_end = grid_shape[1] + shift_c - first_col - (tiles - 1) * LANES
        result[0] = result[0] + jnp.where((lane >= low) & (lane < low_end), moved, 0.0)
        result[1] = result[1] + jnp.where((lane >= high) & (lane < high_end), moved, 0.0)
    for side in range(2):
        out[layer, pl.ds(row, CHUNK), cut[side]] = result[side]
    return own, result


def fill_sides(pad, even_ref, odd_ref, start, place, depth):
    odd_x = is_odd("gx")
    even, other = even_ref[start : start + depth, :], odd_ref[start : start + depth, :]
    for side, packed in ((0, jnp.where(odd_x, even, other)), (1, jnp.where(odd_x, other, even))):
        pad[0, side, place : place + depth, :] = packed
        pad[1, side, place : place + depth, :] = pltpu.roll(packed, HALF, 1)


def finish(
    chunks, carry, grid_shape, base, fit, field, coeff, even_ends, odd_ends, shifts, table, entry, out,
    pad,
):
    rows, cols = field.shape[1:]
    odd_x = is_odd("gx")
    even, other = even_ends[rows : rows + 8, :], odd_ends[rows : rows + 8, :]
    ends = (jnp.where(odd_x, even, other), jnp.where(odd_x, other, even))
    cut = (slice(0, LANES), slice(cols - LANES, cols))
    for layer in range(2):
        weight = weight_of(table, entry, layer)
        for row in (chunk * CHUNK for chunk in chunks):
            own, result = finish_chunk(
                grid_shape, layer, row, field, coeff, out, pad, ends, shifts, weight
            )
            start = None if base is None else [base[layer, row : row + CHUNK, x] for x in cut]
            more = products_of(own, result, start, fit)
            carry = tuple(a + b for a, b in zip(carry, more, strict=True))
    return carry


def finish_ends(grid_shape, even_corners, odd_corners, products, pad, field, *rest):
    rows = field.shape[1]
    fill_sides(pad, even_corners, odd_corners, 0, 0, REACH)
    fill_sides(pad, even_corners, odd_corners, REACH, REACH + rows, REACH)
    depth = REACH // CHUNK
    chunks = [*range(depth), *range(rows // CHUNK - depth, rows // CHUNK)]
    carry = tuple(products[index] for index in range(products.shape[0]))
    base, fit, *others = rest
    return finish(chunks, carry, grid_shape, base, fit, field, *others, pad)


def first_kernel(
    grid_shape, before, pad_before, field, coeff, even_ends, odd_ends, even_corners, odd_corners,
    products, shifts, table, entry, out, pad, sums, even_out, odd_out,
):
    del before, pad_before
    rows = field.shape[1]
    carry = finish_ends(
        grid_shape, even_corners, odd_corners, products, pad, field, None, None, coeff, even_ends,
        odd_ends, shifts, table, entry, out,
    )
    for index, value in enumerate(carry):
        sums[index] = value
    odd_y = is_odd("gy")
    low, high = out[:, 0:REACH, :], out[:, rows - REACH :, :]
    even_out[...] = jnp.where(odd_y, low, high)
    odd_out[...] = jnp.where(odd_y, high, low)


def second_kernel(
    grid_shape, before, pad_before, base, field, coeff, even_ends, odd_ends, even_corners, odd_corners,
    products, sums, shifts, table, entry, out, pad, parts,
):
    del before, pad_before
    gamma, delta, omega, fit = fit_of(sums)
    carry = finish_ends(
        grid_shape, even_corners, odd_corners, products, pad, field, base, fit, coeff, even_ends,
        odd_ends, shifts, table, entry, out,
    )
    rest2, rest_w, slope_rest, n_rest, slope_w, n_w = (
        jnp.sum(value, keepdims=True) for value in carry
    )
    lane = lane_of((8, LANES))
    row = jnp.zeros((8, LANES), jnp.float32)
    for at, value in (
        (0, rest2), (1, slope_rest), (8, 2.0 * rest_w), (9, n_rest + slope_w),
        (16, omega), (17, n_w), (24, fit), (25, fit), (32, gamma), (33, delta),
    ):
        row = jnp.where(lane == at, value, row)
    for start in range(0, parts.shape[0], 8):
        parts[start : start + 8, :] = row


def pick(row, lane, at):
    return jnp.sum(jnp.where(lane == at, row, 0.0), keepdims=True)


def last_kernel(
    parts, base, w_vec, n_vec, solution_out, residual_out, solution_part, residual_part, sems
):
    gathered = parts[...]
    count = gathered.shape[0]
    lane = lane_of((8, LANES))
    total = sum(gathered[8 * i : 8 * i + 8] for i in range(count // 8))
    gamma, delta = pick(total, lane, 32), pick(total, lane, 33)
    alpha = gamma / delta
    gap = alpha - pltpu.roll(gathered, LANES - 24, 1)
    moved = gathered - gap * pltpu.roll(gathered, LANES - 8, 1)
    moved = moved + gap * gap * pltpu.roll(gathered, LANES - 16, 1)
    total = sum(moved[8 * i : 8 * i + 8] for i in range(count // 8))
    gamma_next, delta_next = pick(total, lane, 0), pick(total, lane, 1)
    beta = gamma_next / gamma
    alpha_next = gamma_next / (delta_next - beta * gamma_next / alpha)
    layers, rows = base.shape[:2]
    depth = rows // PIECES
    copies = []
    for layer in range(layers):
        for piece in range(PIECES):
            part = pl.ds(piece * depth, depth)
            start, w_start = base[layer, part, :], w_vec[layer, part, :]
            residual = start - alpha * w_start
            w_next = w_start - alpha * n_vec[layer, part, :]
            solution_part[layer, part, :] = alpha * start + alpha_next * (residual + beta * start)
            residual_part[layer, part, :] = residual - alpha_next * (w_next + beta * w_start)
            for which, (source, target) in enumerate(
                ((solution_part, solution_out), (residual_part, residual_out))
            ):
                copy = pltpu.make_async_copy(
                    source.at[layer, part, :],
                    target.at[layer, part, :],
                    sems.at[which, layer, piece],
                )
                copy.start()
                copies.append(copy)
    for copy in copies:
        copy.wait()


def on_tensor_core(kernel, name, operands, scalars, out_shape, scratch, microseconds, in_place=0):
    return pl.pallas_call(
        kernel,
        out_shape=out_shape,
        in_specs=[VMEM_SPEC] * len(operands) + [SMEM_SPEC] * len(scalars),
        out_specs=(VMEM_SPEC,) * len(out_shape),
        scratch_shapes=[pltpu.VMEM(shape, jnp.float32) for shape in scratch],
        input_output_aliases={index: index for index in range(in_place)},
        compiler_params=pltpu.CompilerParams(vmem_limit_bytes=VMEM_BYTES),
        cost_estimate=pl.CostEstimate(
            flops=0, bytes_accessed=3_000_000 * microseconds, transcendentals=0
        ),
        name=name,
    )(*operands, *scalars)


def on_device(right_side, coefficient, strength_table, layer_entry, shifts):
    layers, rows, cols = right_side.shape
    count_y, count_x = lax.axis_size("gy"), lax.axis_size("gx")
    devices = count_x * count_y
    tiles = cols // LANES
    grid_shape = (rows * count_y, cols * count_x)
    full = jax.ShapeDtypeStruct((layers, rows, cols), jnp.float32)
    edge = jax.ShapeDtypeStruct((layers, REACH, cols), jnp.float32)
    scalars = (jnp.transpose(shifts, (1, 2, 0)), strength_table, layer_entry)
    own_pads = [(2, tiles, rows + 2 * REACH, LANES)]
    coeff_room = jax.ShapeDtypeStruct((2, tiles, rows + 16, LANES), jnp.float32)
    row_pads = [(2, 2, tiles, 2 * REACH, LANES)]
    side_pad = jax.ShapeDtypeStruct((2, 2, rows + 2 * REACH, LANES), jnp.float32)

    def side_of(count):
        return jax.ShapeDtypeStruct((count, LANES), jnp.float32)

    def sums_of(count):
        return jax.ShapeDtypeStruct((count, 8, LANES), jnp.float32)

    def bind(kernel):
        def bound(*refs):
            kernel(grid_shape, *refs)

        return bound

    def rows_first(before, packed, field, coeff, even, odd, even_cols, odd_cols, *refs):
        del before, packed
        rows_kernel(
            grid_shape, field, coeff, even, odd, even, odd, even_cols, odd_cols, even_cols, odd_cols,
            None, None, *refs,
        )

    def rows_second(before, packed, *refs):
        del before, packed
        rows_kernel(grid_shape, *refs)

    def own_first(field, coeff, *refs):
        own_kernel(grid_shape, field, coeff, None, *refs)

    def own_second(field, coeff_pad, across, shifts, table, entry, out, even, odd, pad):
        own_kernel(
            grid_shape, field, None, across, shifts, table, entry, out, even, odd, None, coeff_pad, pad
        )

    rows0 = swap(*edge_rows(right_side, coefficient), "gy")
    w_own, *columns, across, coeff_pad = on_tensor_core(
        own_first, "own_first", (right_side, coefficient), scalars,
        (full, side_of(rows + 8), side_of(rows + 8), full, coeff_room), own_pads, 6,
    )
    cols0 = swap(*columns, "gx")
    packed = pack_corners(*rows0)
    corners0 = swap(*packed, "gx")
    w_rows, products, sides = on_tensor_core(
        rows_first, "rows_first", (w_own, packed[0], right_side, coefficient, *rows0, *cols0), scalars,
        (full, sums_of(3), side_pad), row_pads, 3, 1,
    )
    w_vec, _, sums, even, odd = on_tensor_core(
        bind(first_kernel), "first_apply",
        (w_rows, sides, right_side, coefficient, *cols0, *corners0, products), scalars,
        (full, side_pad, sums_of(3), edge, edge), [], 3, 2,
    )
    rows1 = swap(even, odd, "gy")
    n_own, *columns = on_tensor_core(
        own_second, "own_second", (w_vec, coeff_pad, across), scalars,
        (full, side_of(rows), side_of(rows)), own_pads, 6,
    )
    cols1 = swap(*columns, "gx")
    packed = pack_corners(*rows1)
    corners1 = swap(*packed, "gx")
    n_rows, products, sides = on_tensor_core(
        rows_second, "rows_second",
        (n_own, packed[0], w_vec, coefficient, *rows1, *rows0, *cols1, *cols0, right_side, sums),
        scalars, (full, sums_of(6), side_pad), row_pads, 3, 1,
    )
    n_vec, _, parts = on_tensor_core(
        bind(second_kernel), "second_apply",
        (n_rows, sides, right_side, w_vec, coefficient, *cols0, *corners1, products, sums), scalars,
        (full, side_pad, jax.ShapeDtypeStruct((devices, LANES), jnp.float32)), [], 3, 2,
    )
    gathered = lax.all_to_all(parts, ("gx", "gy"), 0, 0, tiled=True)
    return pl.pallas_call(
        last_kernel,
        out_shape=(full, full),
        in_specs=[VMEM_SPEC] * 4,
        out_specs=(pl.BlockSpec(memory_space=pltpu.HBM),) * 2,
        scratch_shapes=[
            pltpu.VMEM((layers, rows, cols), jnp.float32),
            pltpu.VMEM((layers, rows, cols), jnp.float32),
            pltpu.SemaphoreType.DMA((2, layers, PIECES)),
        ],
        compiler_params=pltpu.CompilerParams(vmem_limit_bytes=VMEM_BYTES),
        name="last_update",
    )(gathered, right_side, w_vec, n_vec)


def solution(mesh):
    placed = (P(None, "gy", "gx"), P(None, "gy", "gx"), P(), P(), P())
    return jax.shard_map(
        on_device,
        mesh=mesh,
        in_specs=placed,
        out_specs=(P(None, "gy", "gx"), P(None, "gy", "gx")),
        check_vma=False,
    )
```

```python
import functools

import jax
import jax.numpy as jnp
from jax import lax
from jax.experimental import pallas as pl
from jax.experimental.pallas import tpu as pltpu
from jax.sharding import PartitionSpec as P

SMAX = 32
REACH = 2 * SMAX
LANES = 128
HALF = 64
CHUNK = 32
OWN_CHUNK = 64
UNROLL = 8
PIECES = 4
VMEM_BYTES = 32 * 1024 * 1024
EDGE_BYTES = 53 * 1024 * 1024
VMEM_SPEC = pl.BlockSpec(memory_space=pltpu.VMEM)
SMEM_SPEC = pl.BlockSpec(memory_space=pltpu.SMEM)


def pairs_from(start, count):
    low = range(start, count - 1, 2)
    return [(i, i + 1) for i in low] + [(i + 1, i) for i in low]


FIRST = {"gy": 1, "gx": 0}


def is_odd(axis):
    return lax.rem(lax.axis_index(axis) + FIRST[axis], 2) == 1


def swap_even(even, axis):
    return lax.ppermute(even, axis, pairs_from(FIRST[axis], lax.axis_size(axis)))


def swap_odd(odd, axis):
    return lax.ppermute(odd, axis, pairs_from(1 - FIRST[axis], lax.axis_size(axis)))


def swap(even, odd, axis):
    return swap_even(even, axis), swap_odd(odd, axis)


def lane_of(shape):
    return lax.broadcasted_iota(jnp.int32, shape, 1)


def pack_columns(first, second, high):
    low_lanes = lane_of(first.shape) < HALF
    turned = pltpu.roll(second, HALF, 1)
    if high:
        return jnp.where(low_lanes, turned, first)
    return jnp.where(low_lanes, first, turned)


def packed_edges(load, cols):
    edges = (slice(0, LANES), slice(cols - LANES, cols))
    return [pack_columns(load(0, edge), load(1, edge), high) for high, edge in enumerate(edges)]


def store_packed(even_ref, odd_ref, start, low, high):
    odd = is_odd("gx")
    rows = low.shape[0]
    even_ref[start : start + rows, :] = jnp.where(odd, low, high)
    odd_ref[start : start + rows, :] = jnp.where(odd, high, low)


def pack_corners_kernel(even_rows, odd_rows, even_side, even_out, odd_out):
    cols = even_rows.shape[2]
    even_out[2 * REACH :, :] = even_side[...]
    odd_y = is_odd("gy")
    for start, above in ((0, True), (REACH, False)):

        def halo(layer, edge, above=above):
            even = even_rows[layer, 0:REACH, edge]
            other = odd_rows[layer, 0:REACH, edge]
            return jnp.where(odd_y == above, even, other)

        store_packed(even_out, odd_out, start, *packed_edges(halo, cols))


def pack_corners(even_rows, odd_rows, even_side, *after):
    def side_of(rows):
        return jax.ShapeDtypeStruct((rows, LANES), jnp.float32)

    def kernel(even_rows, odd_rows, even_side, *refs):
        pack_corners_kernel(even_rows, odd_rows, even_side, *refs[len(after) :])

    return pl.pallas_call(
        kernel,
        out_shape=(side_of(2 * REACH + even_side.shape[0]), side_of(2 * REACH)),
        in_specs=[VMEM_SPEC] * (3 + len(after)),
        out_specs=(VMEM_SPEC,) * 2,
        compiler_params=pltpu.CompilerParams(vmem_limit_bytes=VMEM_BYTES),
        name="pack_corners",
    )(even_rows, odd_rows, even_side, *after)


def pack_sides(field, coeff):
    rows, cols = field.shape[1:]

    def kernel(*refs):
        field, *ends, even_out, odd_out = refs
        low, high = packed_edges(lambda layer, edge: field[layer, :, edge], cols)
        store_packed(even_out, odd_out, 0, low, high)
        if ends:
            store_packed(even_out, odd_out, rows, *packed_ends(ends[0]))

    operands = [field] + ([] if coeff is None else [coeff])
    out = jax.ShapeDtypeStruct((rows + (0 if coeff is None else 8), LANES), jnp.float32)
    return pl.pallas_call(
        kernel,
        out_shape=(out, out),
        in_specs=[VMEM_SPEC] * len(operands),
        out_specs=(VMEM_SPEC,) * 2,
        compiler_params=pltpu.CompilerParams(vmem_limit_bytes=VMEM_BYTES),
        name="pack_sides",
    )(*operands)


def own_rows(side):
    return side.at[pl.ds(2 * REACH, side.shape[0] - 2 * REACH), :]


def edge_kernel(field, coeff, even_out, odd_out, sems):
    rows = field.shape[1]
    odd_y = is_odd("gy")
    copies = []
    for index, (out, at_top) in enumerate(((even_out, odd_y), (odd_out, jnp.logical_not(odd_y)))):
        for part, (source, place, depth) in enumerate(((field, 0, REACH), (coeff, REACH, 8))):
            start = pl.multiple_of(jnp.where(at_top, 0, rows - depth), 8)
            copies.append(
                pltpu.make_async_copy(
                    source.at[:, pl.ds(start, depth), :],
                    out.at[:, pl.ds(place, depth), :],
                    sems.at[index, part],
                )
            )
    for copy in copies:
        copy.start()
    for copy in copies:
        copy.wait()


def edge_rows(field, coeff):
    layers, _, cols = field.shape
    out = jax.ShapeDtypeStruct((layers, REACH + 8, cols), jnp.float32)
    return pl.pallas_call(
        edge_kernel,
        out_shape=(out, out),
        in_specs=[pl.BlockSpec(memory_space=pltpu.HBM)] * 2,
        out_specs=(VMEM_SPEC,) * 2,
        scratch_shapes=[pltpu.SemaphoreType.DMA((2, 2))],
        compiler_params=pltpu.CompilerParams(vmem_limit_bytes=EDGE_BYTES),
        name="edge_rows",
    )(field, coeff)


def zero_rim(pad, depth, rows):
    zeros = jnp.zeros((depth, LANES), jnp.float32)
    for layer in range(2):
        for tile in range(pad.shape[1]):
            pad[layer, tile, 0:depth, :] = zeros
            pad[layer, tile, depth + rows :, :] = zeros


def fill_own(pad, depth, field):
    rows, cols = field.shape[1:]
    for layer in range(2):
        for tile in range(cols // LANES):
            lanes = slice(tile * LANES, (tile + 1) * LANES)
            pad[layer, tile, depth : depth + rows, :] = field[layer, :, lanes]


def move_across(tiles, step_c, lane):
    count = len(tiles)
    back = jnp.bitwise_and(LANES - step_c, LANES - 1)
    from_left = lane < jnp.where(step_c < 0, -step_c, 0)
    from_right = lane >= jnp.where(step_c < 0, LANES, LANES - step_c)
    turned = [0.0] + [pltpu.roll(tile, back, 1) for tile in tiles] + [0.0]
    return [
        jnp.where(from_left, turned[i], jnp.where(from_right, turned[i + 2], turned[i + 1]))
        for i in range(count)
    ]


def from_the_right(tiles, lane, last):
    ahead = [pltpu.roll(tile, LANES - 1, 1) for tile in tiles]
    return [
        jnp.where(lane == LANES - 1, after, tile)
        for tile, after in zip(ahead, [*ahead[1:], last], strict=True)
    ]


def near_end(row, depth, rows):
    return row < SMAX or row + depth > rows - SMAX


def apply_chunk(
    layer, row, pad, coeff_pad, across, across_out, shifts, weight, grid_shape, tile_shape
):
    rows, cols = tile_shape
    tiles = cols // LANES
    other = 1 - layer
    lane = lane_of((OWN_CHUNK, LANES))
    row_at = lax.broadcasted_iota(jnp.int32, (OWN_CHUNK, LANES), 0)
    first_row = lax.axis_index("gy") * rows + row
    first_col = lax.axis_index("gx") * cols
    cut = [slice(tile * LANES, (tile + 1) * LANES) for tile in range(tiles)]

    def at(ref, tile, start):
        return ref[layer, tile, pl.ds(start, OWN_CHUNK), :]

    own = [at(pad, tile, REACH + row) for tile in range(tiles)]
    own_c = [at(coeff_pad, tile, 8 + row) for tile in range(tiles)]
    if across is None:
        right_c = from_the_right(own_c, lane, 0.0)
        both = [a + b for a, b in zip(own_c, right_c, strict=True)]
        for value, lanes in zip(both, cut, strict=True):
            across_out[layer, pl.ds(row, OWN_CHUNK), lanes] = value
    else:
        both = [across[layer, pl.ds(row, OWN_CHUNK), lanes] for lanes in cut]
    right = from_the_right(own, lane, own[-1])
    flow = [c * (a - b) for c, a, b in zip(both, own, right, strict=True)]
    turned = [pltpu.roll(value, 1, 1) for value in flow]
    result = []
    for tile in range(tiles):
        value, coeff = own[tile], own_c[tile]
        above, below = at(pad, tile, REACH - 1 + row), at(pad, tile, REACH + 1 + row)
        above_c, below_c = at(coeff_pad, tile, 7 + row), at(coeff_pad, tile, 9 + row)
        total = (coeff + above_c) * (value - above) + (coeff + below_c) * (value - below)
        inflow = jnp.where(lane == 0, turned[tile - 1] if tile else 0.0, turned[tile])
        result.append(weight * (total + flow[tile] - inflow))
    for direction in range(shifts.shape[2]):
        shift_r, shift_c = shifts[layer, 0, direction], shifts[layer, 1, direction]
        start_r = REACH + row + shifts[other, 0, direction] - shift_r
        source = [pad[other, tile, pl.ds(start_r, OWN_CHUNK), :] for tile in range(tiles)]
        moved = move_across(source, shifts[other, 1, direction] - shift_c, lane)
        masks = [[] for _ in range(tiles)]
        masks[0].append(lane >= shift_c - first_col)
        masks[-1].append(lane < grid_shape[1] + shift_c - first_col - (tiles - 1) * LANES)
        if near_end(row, OWN_CHUNK, rows):
            image_row = row_at + (first_row - shift_r)
            inside = (image_row >= 0) & (image_row < grid_shape[0])
            for mask in masks:
                mask.append(inside)
        for tile in range(tiles):
            value = own[tile] + moved[tile]
            if masks[tile]:
                value = jnp.where(functools.reduce(jnp.logical_and, masks[tile]), value, 0.0)
            result[tile] = result[tile] + value
    return result


def fold(parts):
    total = sum(parts[1:], parts[0])
    pieces = [total[8 * i : 8 * i + 8] for i in range(total.shape[0] // 8)]
    return sum(pieces[1:], pieces[0])


def dot_of(first, second):
    return fold([a * b for a, b in zip(first, second, strict=True)])


def weight_of(table, entry, layer):
    return 0.5 * table[entry[layer]]


def packed_ends(coeff):
    ends = []
    rows, cols = coeff.shape[1:]
    lane = lane_of((8, LANES))
    for high, edge in enumerate((slice(0, LANES), slice(cols - LANES, cols))):
        packed = jnp.zeros((8, LANES), jnp.float32)
        for layer in range(2):
            for group in range(rows // 8):
                at = layer * (rows // 8) + group
                turn = (at + high) % LANES
                value = coeff[layer, 8 * group : 8 * group + 8, edge]
                value = pltpu.roll(value, turn, 1) if turn else value
                packed = jnp.where(lane == at, value, packed)
        ends.append(packed)
    return ends


def own_kernel(
    grid_shape, field, coeff, across, shifts, table, entry, out, across_out, coeff_pad, pad
):
    rows, cols = field.shape[1:]
    zero_rim(pad, REACH, rows)
    fill_own(pad, REACH, field)
    if across is None:
        zero_rim(coeff_pad, 8, rows)
        fill_own(coeff_pad, 8, coeff)
    for layer in range(2):
        weight = weight_of(table, entry, layer)
        for row in range(0, rows, OWN_CHUNK):
            result = apply_chunk(
                layer, row, pad, coeff_pad, across, across_out, shifts, weight, grid_shape, (rows, cols)
            )
            for tile, value in enumerate(result):
                out[layer, row : row + OWN_CHUNK, tile * LANES : (tile + 1) * LANES] = value


def products_of(own, result, base, fit):
    if base is None:
        pairs = ((own, own), (own, result), (result, result))
    else:
        rest = [a - fit * b for a, b in zip(base, own, strict=True)]
        slope = [a - fit * b for a, b in zip(own, result, strict=True)]
        pairs = (
            (rest, rest), (rest, own), (slope, rest), (result, rest), (slope, own), (result, own),
        )
    return tuple(dot_of(*pair) for pair in pairs)


def fit_of(sums):
    gamma, delta, omega = (jnp.sum(sums[index], keepdims=True) for index in range(3))
    fit = jnp.where(omega > 0.0, delta / jnp.where(omega > 0.0, omega, 1.0), 0.0)
    return gamma, delta, omega, jnp.clip(fit, -1.0, 1.0)


def rows_kernel(
    grid_shape, field, coeff, even_rows, odd_rows, even_edge, odd_edge, even_cols, odd_cols, even_ends,
    odd_ends, base, sums, shifts, table, entry, out, products, side_pad, pad,
):
    even_cols, even_ends = own_rows(even_cols), own_rows(even_ends)
    rows, cols = field.shape[1:]
    tiles = cols // LANES
    odd_y = is_odd("gy")
    first_row = lax.axis_index("gy") * rows
    first_col = lax.axis_index("gx") * cols
    zeros = jnp.zeros((REACH, LANES), jnp.float32)
    for layer in range(2):
        for tile in range(tiles):
            lanes = slice(tile * LANES, (tile + 1) * LANES)
            even = even_rows[layer, 0:REACH, lanes]
            other = odd_rows[layer, 0:REACH, lanes]
            pad[layer, 0, tile, 0:REACH, :] = jnp.where(odd_y, even, other)
            pad[layer, 0, tile, REACH:, :] = zeros
            pad[layer, 1, tile, 0:REACH, :] = zeros
            pad[layer, 1, tile, REACH:, :] = jnp.where(odd_y, other, even)
    lane = lane_of((CHUNK, LANES))
    row_at = lax.broadcasted_iota(jnp.int32, (CHUNK, LANES), 0)
    for layer in range(2):
        other_layer = 1 - layer

        def step(i, carry, layer=layer, other_layer=other_layer):
            part = pl.multiple_of(i * CHUNK, CHUNK)
            totals = [[jnp.zeros((CHUNK, LANES), jnp.float32)] * tiles for _ in range(2)]
            for direction in range(shifts.shape[2]):
                shift_r, shift_c = shifts[layer, 0, direction], shifts[layer, 1, direction]
                step_r = shifts[other_layer, 0, direction] - shift_r
                side = jnp.where(step_r < 0, 0, 1)
                start_r = part + step_r + jnp.where(step_r < 0, REACH, 0)
                row = part + jnp.where(step_r < 0, 0, rows - REACH)
                source = [
                    pad[other_layer, side, tile, pl.ds(start_r, CHUNK), :] for tile in range(tiles)
                ]
                moved = move_across(source, shifts[other_layer, 1, direction] - shift_c, lane)
                image_row = row_at + (first_row + row - shift_r)
                inside = (image_row >= 0) & (image_row < grid_shape[0])
                upper = inside & (jnp.full((CHUNK, LANES), side, jnp.int32) == 0)
                lower = inside & (jnp.full((CHUNK, LANES), side, jnp.int32) == 1)
                for tile in range(tiles):
                    value = moved[tile]
                    if tile == 0:
                        value = jnp.where(lane >= shift_c - first_col, value, 0.0)
                    if tile == tiles - 1:
                        last = grid_shape[1] + shift_c - first_col - tile * LANES
                        value = jnp.where(lane < last, value, 0.0)
                    totals[0][tile] = totals[0][tile] + jnp.where(upper, value, 0.0)
                    totals[1][tile] = totals[1][tile] + jnp.where(lower, value, 0.0)
            for side, base in enumerate((0, rows - REACH)):
                for tile in range(tiles):
                    lanes = slice(tile * LANES, (tile + 1) * LANES)
                    out[layer, pl.ds(base + part, CHUNK), lanes] += totals[side][tile]
            return carry

        lax.fori_loop(0, REACH // CHUNK, step, 0, unroll=True)
        weight = weight_of(table, entry, layer)
        at = lax.broadcasted_iota(jnp.int32, (8, cols), 0)
        even = even_edge[layer, REACH : REACH + 8, :]
        other = odd_edge[layer, REACH : REACH + 8, :]
        even_v = [even_rows[layer, start : start + 8, :] for start in (0, REACH - 8)]
        other_v = [odd_rows[layer, start : start + 8, :] for start in (0, REACH - 8)]
        for start, edge_c, edge_v, spot, source in (
            (0, jnp.where(odd_y, even, other), jnp.where(odd_y, even_v[1], other_v[1]), 0, 1),
            (
                rows - 8, jnp.where(odd_y, other, even), jnp.where(odd_y, other_v[0], even_v[0]),
                7, 7,
            ),
        ):
            edge_c = pltpu.roll(edge_c, source, 0)
            edge_v = pltpu.roll(edge_v, source, 0)
            value = field[layer, start : start + 8, :]
            own_c = coeff[layer, start : start + 8, :]
            extra = weight * (edge_c * value - (own_c + edge_c) * edge_v)
            out[layer, start : start + 8, :] += jnp.where(at == spot, extra, 0.0)
    fit = None if base is None else fit_of(sums)[3]
    carry = (jnp.zeros((8, LANES), jnp.float32),) * products.shape[0]
    inner = [slice(tile * LANES, (tile + 1) * LANES) for tile in range(1, tiles - 1)]
    for layer in range(2):

        def add(i, carry, layer=layer):
            chunk = pl.ds(pl.multiple_of(i * CHUNK, CHUNK), CHUNK)
            start, own, result = (
                None if ref is None else [ref[layer, chunk, lanes] for lanes in inner]
                for ref in (base, field, out)
            )
            more = products_of(own, result, start, fit)
            return tuple(a + b for a, b in zip(carry, more, strict=True))

        carry = lax.fori_loop(0, rows // CHUNK, add, carry, unroll=UNROLL)
    fill_sides(side_pad, even_cols, odd_cols, 0, REACH, rows)
    carry = finish(
        range(REACH // CHUNK, (rows - REACH) // CHUNK), carry, grid_shape, base, fit, field, coeff,
        even_ends, odd_ends, shifts, table, entry, out, side_pad,
    )
    for index, value in enumerate(carry):
        products[index] = value


def finish_chunk(grid_shape, layer, row, field, coeff, out, pad, ends, shifts, weight):
    rows, cols = field.shape[1:]
    tiles = cols // LANES
    first_row = lax.axis_index("gy") * rows + row
    first_col = lax.axis_index("gx") * cols
    lane = lane_of((CHUNK, LANES))
    row_at = lax.broadcasted_iota(jnp.int32, (CHUNK, LANES), 0)
    cut = (slice(0, LANES), slice(cols - LANES, cols))
    own = [field[layer, pl.ds(row, CHUNK), lanes] for lanes in cut]
    result = []
    for side, spot in ((0, 0), (1, LANES - 1)):
        at = layer * (rows // 8) + row // 8
        edge_c = jnp.concatenate(
            [
                pltpu.roll(ends[side], (spot - at - i) % LANES, 1)
                for i in range(CHUNK // 8)
            ]
        )
        edge_v = pad[layer, side, pl.ds(REACH + row, CHUNK), :]
        edge_v = pltpu.roll(edge_v, LANES - 1 if side else 1, 1)
        own_c = coeff[layer, pl.ds(row, CHUNK), cut[side]]
        extra = weight * ((own_c + edge_c) * (own[side] - edge_v))
        extra = jnp.where(lane == spot, extra, 0.0)
        result.append(out[layer, pl.ds(row, CHUNK), cut[side]] + extra)
    for direction in range(shifts.shape[2]):
        shift_r, shift_c = shifts[layer, 0, direction], shifts[layer, 1, direction]
        start_r = REACH + row + shifts[1 - layer, 0, direction] - shift_r
        step_c = shifts[1 - layer, 1, direction] - shift_c
        side = jnp.where(step_c < 0, 0, 1)
        back = jnp.bitwise_and(LANES - step_c, LANES - 1)
        moved = pltpu.roll(pad[1 - layer, side, pl.ds(start_r, CHUNK), :], back, 1)
        if near_end(row, CHUNK, rows):
            image_row = row_at + (first_row - shift_r)
            moved = jnp.where((image_row >= 0) & (image_row < grid_shape[0]), moved, 0.0)
        low, low_end = shift_c - first_col, jnp.where(step_c < 0, -step_c, 0)
        high = jnp.where(step_c < 0, LANES, LANES - step_c)
        high_end = grid_shape[1] + shift_c - first_col - (tiles - 1) * LANES
        result[0] = result[0] + jnp.where((lane >= low) & (lane < low_end), moved, 0.0)
        result[1] = result[1] + jnp.where((lane >= high) & (lane < high_end), moved, 0.0)
    for side in range(2):
        out[layer, pl.ds(row, CHUNK), cut[side]] = result[side]
    return own, result


def fill_sides(pad, even_ref, odd_ref, start, place, depth):
    odd_x = is_odd("gx")
    even, other = even_ref[start : start + depth, :], odd_ref[start : start + depth, :]
    for side, packed in ((0, jnp.where(odd_x, even, other)), (1, jnp.where(odd_x, other, even))):
        pad[0, side, place : place + depth, :] = packed
        pad[1, side, place : place + depth, :] = pltpu.roll(packed, HALF, 1)


def finish(
    chunks, carry, grid_shape, base, fit, field, coeff, even_ends, odd_ends, shifts, table, entry, out,
    pad,
):
    rows, cols = field.shape[1:]
    odd_x = is_odd("gx")
    even, other = even_ends[rows : rows + 8, :], odd_ends[rows : rows + 8, :]
    ends = (jnp.where(odd_x, even, other), jnp.where(odd_x, other, even))
    cut = (slice(0, LANES), slice(cols - LANES, cols))
    for layer in range(2):
        weight = weight_of(table, entry, layer)
        for row in (chunk * CHUNK for chunk in chunks):
            own, result = finish_chunk(
                grid_shape, layer, row, field, coeff, out, pad, ends, shifts, weight
            )
            start = None if base is None else [base[layer, row : row + CHUNK, x] for x in cut]
            more = products_of(own, result, start, fit)
            carry = tuple(a + b for a, b in zip(carry, more, strict=True))
    return carry


def finish_ends(grid_shape, even_corners, odd_corners, products, pad, field, *rest):
    rows = field.shape[1]
    fill_sides(pad, even_corners, odd_corners, 0, 0, REACH)
    fill_sides(pad, even_corners, odd_corners, REACH, REACH + rows, REACH)
    depth = REACH // CHUNK
    chunks = [*range(depth), *range(rows // CHUNK - depth, rows // CHUNK)]
    carry = tuple(products[index] for index in range(products.shape[0]))
    base, fit, *others = rest
    coeff, even_ends, *others = others
    return finish(
        chunks, carry, grid_shape, base, fit, field, coeff, own_rows(even_ends), *others, pad
    )


def first_kernel(
    grid_shape, before, pad_before, field, coeff, even_ends, odd_ends, even_corners, odd_corners,
    products, shifts, table, entry, out, pad, sums, even_out, odd_out,
):
    del before, pad_before
    rows = field.shape[1]
    carry = finish_ends(
        grid_shape, even_corners, odd_corners, products, pad, field, None, None, coeff, even_ends,
        odd_ends, shifts, table, entry, out,
    )
    for index, value in enumerate(carry):
        sums[index] = value
    odd_y = is_odd("gy")
    low, high = out[:, 0:REACH, :], out[:, rows - REACH :, :]
    even_out[...] = jnp.where(odd_y, low, high)
    odd_out[...] = jnp.where(odd_y, high, low)


def second_kernel(
    grid_shape, before, pad_before, base, field, coeff, even_ends, odd_ends, even_corners, odd_corners,
    products, sums, shifts, table, entry, out, pad, parts,
):
    del before, pad_before
    gamma, delta, omega, fit = fit_of(sums)
    carry = finish_ends(
        grid_shape, even_corners, odd_corners, products, pad, field, base, fit, coeff, even_ends,
        odd_ends, shifts, table, entry, out,
    )
    rest2, rest_w, slope_rest, n_rest, slope_w, n_w = (
        jnp.sum(value, keepdims=True) for value in carry
    )
    lane = lane_of((8, LANES))
    row = jnp.zeros((8, LANES), jnp.float32)
    for at, value in (
        (0, rest2), (1, slope_rest), (8, 2.0 * rest_w), (9, n_rest + slope_w),
        (16, omega), (17, n_w), (24, fit), (25, fit), (32, gamma), (33, delta),
    ):
        row = jnp.where(lane == at, value, row)
    for start in range(0, parts.shape[0], 8):
        parts[start : start + 8, :] = row


def pick(row, lane, at):
    return jnp.sum(jnp.where(lane == at, row, 0.0), keepdims=True)


def last_kernel(
    parts, base, w_vec, n_vec, solution_out, residual_out, solution_part, residual_part, sems
):
    gathered = parts[...]
    count = gathered.shape[0]
    lane = lane_of((8, LANES))
    total = sum(gathered[8 * i : 8 * i + 8] for i in range(count // 8))
    gamma, delta = pick(total, lane, 32), pick(total, lane, 33)
    alpha = gamma / delta
    gap = alpha - pltpu.roll(gathered, LANES - 24, 1)
    moved = gathered - gap * pltpu.roll(gathered, LANES - 8, 1)
    moved = moved + gap * gap * pltpu.roll(gathered, LANES - 16, 1)
    total = sum(moved[8 * i : 8 * i + 8] for i in range(count // 8))
    gamma_next, delta_next = pick(total, lane, 0), pick(total, lane, 1)
    beta = gamma_next / gamma
    alpha_next = gamma_next / (delta_next - beta * gamma_next / alpha)
    layers, rows = base.shape[:2]
    depth = rows // PIECES
    copies = []
    for layer in range(layers):
        for piece in range(PIECES):
            part = pl.ds(piece * depth, depth)
            start, w_start = base[layer, part, :], w_vec[layer, part, :]
            residual = start - alpha * w_start
            w_next = w_start - alpha * n_vec[layer, part, :]
            solution_part[layer, part, :] = alpha * start + alpha_next * (residual + beta * start)
            residual_part[layer, part, :] = residual - alpha_next * (w_next + beta * w_start)
            for which, (source, target) in enumerate(
                ((solution_part, solution_out), (residual_part, residual_out))
            ):
                copy = pltpu.make_async_copy(
                    source.at[layer, part, :],
                    target.at[layer, part, :],
                    sems.at[which, layer, piece],
                )
                copy.start()
                copies.append(copy)
    for copy in copies:
        copy.wait()


def on_tensor_core(kernel, name, operands, scalars, out_shape, scratch, microseconds, in_place=0):
    return pl.pallas_call(
        kernel,
        out_shape=out_shape,
        in_specs=[VMEM_SPEC] * len(operands) + [SMEM_SPEC] * len(scalars),
        out_specs=(VMEM_SPEC,) * len(out_shape),
        scratch_shapes=[pltpu.VMEM(shape, jnp.float32) for shape in scratch],
        input_output_aliases={index: index for index in range(in_place)},
        compiler_params=pltpu.CompilerParams(vmem_limit_bytes=VMEM_BYTES),
        cost_estimate=pl.CostEstimate(
            flops=0, bytes_accessed=3_000_000 * microseconds, transcendentals=0
        ),
        name=name,
    )(*operands, *scalars)


def on_device(right_side, coefficient, strength_table, layer_entry, shifts):
    layers, rows, cols = right_side.shape
    count_y, count_x = lax.axis_size("gy"), lax.axis_size("gx")
    devices = count_x * count_y
    tiles = cols // LANES
    grid_shape = (rows * count_y, cols * count_x)
    full = jax.ShapeDtypeStruct((layers, rows, cols), jnp.float32)
    edge = jax.ShapeDtypeStruct((layers, REACH, cols), jnp.float32)
    scalars = (jnp.transpose(shifts, (1, 2, 0)), strength_table, layer_entry)
    own_pads = [(2, tiles, rows + 2 * REACH, LANES)]
    coeff_room = jax.ShapeDtypeStruct((2, tiles, rows + 16, LANES), jnp.float32)
    row_pads = [(2, 2, tiles, 2 * REACH, LANES)]
    side_pad = jax.ShapeDtypeStruct((2, 2, rows + 2 * REACH, LANES), jnp.float32)

    def side_of(count):
        return jax.ShapeDtypeStruct((count, LANES), jnp.float32)

    def sums_of(count):
        return jax.ShapeDtypeStruct((count, 8, LANES), jnp.float32)

    def bind(kernel):
        def bound(*refs):
            kernel(grid_shape, *refs)

        return bound

    def rows_first(before, packed, field, coeff, even, odd, even_cols, odd_cols, *refs):
        del before, packed
        rows_kernel(
            grid_shape, field, coeff, even, odd, even, odd, even_cols, odd_cols, even_cols, odd_cols,
            None, None, *refs,
        )

    def rows_second(before, packed, *refs):
        del before, packed
        rows_kernel(grid_shape, *refs)

    def own_first(field, coeff, side, *refs):
        del side
        own_kernel(grid_shape, field, coeff, None, *refs)

    def own_second(field, coeff_pad, across, side, shifts, table, entry, out, pad):
        del side
        own_kernel(grid_shape, field, None, across, shifts, table, entry, out, None, coeff_pad, pad)

    rows0 = swap(*edge_rows(right_side, coefficient), "gy")
    even_side, odd_side = pack_sides(right_side, coefficient)
    odd_cols = swap_odd(odd_side, "gx")
    w_own, across, coeff_pad = on_tensor_core(
        own_first, "own_first", (right_side, coefficient, odd_side), scalars, (full, full, coeff_room),
        own_pads, 6,
    )
    packed = pack_corners(*rows0, even_side, odd_cols, w_own)
    cols0 = (swap_even(packed[0], "gx"), odd_cols)
    corners0 = (cols0[0], swap_odd(packed[1], "gx"))
    w_rows, products, sides = on_tensor_core(
        rows_first, "rows_first", (w_own, packed[1], right_side, coefficient, *rows0, *cols0), scalars,
        (full, sums_of(3), side_pad), row_pads, 3, 1,
    )
    w_vec, _, sums, even, odd = on_tensor_core(
        bind(first_kernel), "first_apply",
        (w_rows, sides, right_side, coefficient, *cols0, *corners0, products), scalars,
        (full, side_pad, sums_of(3), edge, edge), [], 3, 2,
    )
    rows1 = swap(even, odd, "gy")
    even_side, odd_side = pack_sides(w_vec, None)
    odd_cols = swap_odd(odd_side, "gx")
    (n_own,) = on_tensor_core(
        own_second, "own_second", (w_vec, coeff_pad, across, odd_side), scalars, (full,), own_pads, 6
    )
    packed = pack_corners(*rows1, even_side, odd_cols, n_own)
    cols1 = (swap_even(packed[0], "gx"), odd_cols)
    corners1 = (cols1[0], swap_odd(packed[1], "gx"))
    n_rows, products, sides = on_tensor_core(
        rows_second, "rows_second",
        (n_own, packed[1], w_vec, coefficient, *rows1, *rows0, *cols1, *cols0, right_side, sums),
        scalars, (full, sums_of(6), side_pad), row_pads, 3, 1,
    )
    n_vec, _, parts = on_tensor_core(
        bind(second_kernel), "second_apply",
        (n_rows, sides, right_side, w_vec, coefficient, *cols0, *corners1, products, sums), scalars,
        (full, side_pad, jax.ShapeDtypeStruct((devices, LANES), jnp.float32)), [], 3, 2,
    )
    gathered = lax.all_to_all(parts, ("gx", "gy"), 0, 0, tiled=True)
    return pl.pallas_call(
        last_kernel,
        out_shape=(full, full),
        in_specs=[VMEM_SPEC] * 4,
        out_specs=(pl.BlockSpec(memory_space=pltpu.HBM),) * 2,
        scratch_shapes=[
            pltpu.VMEM((layers, rows, cols), jnp.float32),
            pltpu.VMEM((layers, rows, cols), jnp.float32),
            pltpu.SemaphoreType.DMA((2, layers, PIECES)),
        ],
        compiler_params=pltpu.CompilerParams(vmem_limit_bytes=VMEM_BYTES),
        name="last_update",
    )(gathered, right_side, w_vec, n_vec)


def solution(mesh):
    placed = (P(None, "gy", "gx"), P(None, "gy", "gx"), P(), P(), P())
    return jax.shard_map(
        on_device,
        mesh=mesh,
        in_specs=placed,
        out_specs=(P(None, "gy", "gx"), P(None, "gy", "gx")),
        check_vma=False,
    )
```

```python
import functools

import jax
import jax.numpy as jnp
from jax import lax
from jax.experimental import pallas as pl
from jax.experimental.pallas import tpu as pltpu
from jax.sharding import PartitionSpec as P

SMAX = 32
REACH = 2 * SMAX
LANES = 128
HALF = 64
CHUNK = 32
OWN_CHUNK = 64
UNROLL = 8
PIECES = 4
VMEM_BYTES = 32 * 1024 * 1024
EDGE_BYTES = 53 * 1024 * 1024
VMEM_SPEC = pl.BlockSpec(memory_space=pltpu.VMEM)
SMEM_SPEC = pl.BlockSpec(memory_space=pltpu.SMEM)


def pairs_from(start, count):
    low = range(start, count - 1, 2)
    return [(i, i + 1) for i in low] + [(i + 1, i) for i in low]


FIRST = {"gy": 1, "gx": 1}


def is_odd(axis):
    return lax.rem(lax.axis_index(axis) + FIRST[axis], 2) == 1


def swap(even, odd, axis):
    count = lax.axis_size(axis)
    return (
        lax.ppermute(even, axis, pairs_from(FIRST[axis], count)),
        lax.ppermute(odd, axis, pairs_from(1 - FIRST[axis], count)),
    )


def lane_of(shape):
    return lax.broadcasted_iota(jnp.int32, shape, 1)


def pack_columns(first, second, high):
    low_lanes = lane_of(first.shape) < HALF
    turned = pltpu.roll(second, HALF, 1)
    if high:
        return jnp.where(low_lanes, turned, first)
    return jnp.where(low_lanes, first, turned)


def packed_edges(load, cols):
    edges = (slice(0, LANES), slice(cols - LANES, cols))
    return [pack_columns(load(0, edge), load(1, edge), high) for high, edge in enumerate(edges)]


def store_packed(even_ref, odd_ref, start, low, high):
    odd = is_odd("gx")
    rows = low.shape[0]
    even_ref[start : start + rows, :] = jnp.where(odd, low, high)
    odd_ref[start : start + rows, :] = jnp.where(odd, high, low)


def pack_corners_kernel(even_rows, odd_rows, even_out, odd_out):
    cols = even_rows.shape[2]
    odd_y = is_odd("gy")
    for start, above in ((0, True), (REACH, False)):

        def halo(layer, edge, above=above):
            even = even_rows[layer, 0:REACH, edge]
            other = odd_rows[layer, 0:REACH, edge]
            return jnp.where(odd_y == above, even, other)

        store_packed(even_out, odd_out, start, *packed_edges(halo, cols))


def pack(kernel, operands, rows, name):
    out = jax.ShapeDtypeStruct((rows, LANES), jnp.float32)
    return pl.pallas_call(
        kernel,
        out_shape=(out, out),
        in_specs=[VMEM_SPEC] * len(operands),
        out_specs=(VMEM_SPEC,) * 2,
        compiler_params=pltpu.CompilerParams(vmem_limit_bytes=VMEM_BYTES),
        name=name,
    )(*operands)


def pack_corners(even_rows, odd_rows):
    return pack(pack_corners_kernel, (even_rows, odd_rows), 2 * REACH, "pack_corners")


def edge_kernel(field, coeff, even_out, odd_out, sems):
    rows = field.shape[1]
    odd_y = is_odd("gy")
    copies = []
    for index, (out, at_top) in enumerate(((even_out, odd_y), (odd_out, jnp.logical_not(odd_y)))):
        for part, (source, place, depth) in enumerate(((field, 0, REACH), (coeff, REACH, 8))):
            start = pl.multiple_of(jnp.where(at_top, 0, rows - depth), 8)
            copies.append(
                pltpu.make_async_copy(
                    source.at[:, pl.ds(start, depth), :],
                    out.at[:, pl.ds(place, depth), :],
                    sems.at[index, part],
                )
            )
    for copy in copies:
        copy.start()
    for copy in copies:
        copy.wait()


def edge_rows(field, coeff):
    layers, _, cols = field.shape
    out = jax.ShapeDtypeStruct((layers, REACH + 8, cols), jnp.float32)
    return pl.pallas_call(
        edge_kernel,
        out_shape=(out, out),
        in_specs=[pl.BlockSpec(memory_space=pltpu.HBM)] * 2,
        out_specs=(VMEM_SPEC,) * 2,
        scratch_shapes=[pltpu.SemaphoreType.DMA((2, 2))],
        compiler_params=pltpu.CompilerParams(vmem_limit_bytes=EDGE_BYTES),
        name="edge_rows",
    )(field, coeff)


def zero_rim(pad, depth, rows):
    zeros = jnp.zeros((depth, LANES), jnp.float32)
    for layer in range(2):
        for tile in range(pad.shape[1]):
            pad[layer, tile, 0:depth, :] = zeros
            pad[layer, tile, depth + rows :, :] = zeros


def fill_own(pad, depth, field):
    rows, cols = field.shape[1:]
    for layer in range(2):
        for tile in range(cols // LANES):
            lanes = slice(tile * LANES, (tile + 1) * LANES)
            pad[layer, tile, depth : depth + rows, :] = field[layer, :, lanes]


def move_across(tiles, step_c, lane):
    count = len(tiles)
    back = jnp.bitwise_and(LANES - step_c, LANES - 1)
    from_left = lane < jnp.where(step_c < 0, -step_c, 0)
    from_right = lane >= jnp.where(step_c < 0, LANES, LANES - step_c)
    turned = [0.0] + [pltpu.roll(tile, back, 1) for tile in tiles] + [0.0]
    return [
        jnp.where(from_left, turned[i], jnp.where(from_right, turned[i + 2], turned[i + 1]))
        for i in range(count)
    ]


def from_the_right(tiles, lane, last):
    ahead = [pltpu.roll(tile, LANES - 1, 1) for tile in tiles]
    return [
        jnp.where(lane == LANES - 1, after, tile)
        for tile, after in zip(ahead, [*ahead[1:], last], strict=True)
    ]


def near_end(row, depth, rows):
    return row < SMAX or row + depth > rows - SMAX


def apply_chunk(
    layer, row, pad, coeff_pad, across, across_out, shifts, weight, grid_shape, tile_shape
):
    rows, cols = tile_shape
    tiles = cols // LANES
    other = 1 - layer
    lane = lane_of((OWN_CHUNK, LANES))
    row_at = lax.broadcasted_iota(jnp.int32, (OWN_CHUNK, LANES), 0)
    first_row = lax.axis_index("gy") * rows + row
    first_col = lax.axis_index("gx") * cols
    cut = [slice(tile * LANES, (tile + 1) * LANES) for tile in range(tiles)]

    def at(ref, tile, start):
        return ref[layer, tile, pl.ds(start, OWN_CHUNK), :]

    own = [at(pad, tile, REACH + row) for tile in range(tiles)]
    own_c = [at(coeff_pad, tile, 8 + row) for tile in range(tiles)]
    if across is None:
        right_c = from_the_right(own_c, lane, 0.0)
        both = [a + b for a, b in zip(own_c, right_c, strict=True)]
        for value, lanes in zip(both, cut, strict=True):
            across_out[layer, pl.ds(row, OWN_CHUNK), lanes] = value
    else:
        both = [across[layer, pl.ds(row, OWN_CHUNK), lanes] for lanes in cut]
    right = from_the_right(own, lane, own[-1])
    flow = [c * (a - b) for c, a, b in zip(both, own, right, strict=True)]
    turned = [pltpu.roll(value, 1, 1) for value in flow]
    result = []
    for tile in range(tiles):
        value, coeff = own[tile], own_c[tile]
        above, below = at(pad, tile, REACH - 1 + row), at(pad, tile, REACH + 1 + row)
        above_c, below_c = at(coeff_pad, tile, 7 + row), at(coeff_pad, tile, 9 + row)
        total = (coeff + above_c) * (value - above) + (coeff + below_c) * (value - below)
        inflow = jnp.where(lane == 0, turned[tile - 1] if tile else 0.0, turned[tile])
        result.append(weight * (total + flow[tile] - inflow))
    for direction in range(shifts.shape[2]):
        shift_r, shift_c = shifts[layer, 0, direction], shifts[layer, 1, direction]
        start_r = REACH + row + shifts[other, 0, direction] - shift_r
        source = [pad[other, tile, pl.ds(start_r, OWN_CHUNK), :] for tile in range(tiles)]
        moved = move_across(source, shifts[other, 1, direction] - shift_c, lane)
        masks = [[] for _ in range(tiles)]
        masks[0].append(lane >= shift_c - first_col)
        masks[-1].append(lane < grid_shape[1] + shift_c - first_col - (tiles - 1) * LANES)
        if near_end(row, OWN_CHUNK, rows):
            image_row = row_at + (first_row - shift_r)
            inside = (image_row >= 0) & (image_row < grid_shape[0])
            for mask in masks:
                mask.append(inside)
        for tile in range(tiles):
            value = own[tile] + moved[tile]
            if masks[tile]:
                value = jnp.where(functools.reduce(jnp.logical_and, masks[tile]), value, 0.0)
            result[tile] = result[tile] + value
    return result


def fold(parts):
    total = sum(parts[1:], parts[0])
    pieces = [total[8 * i : 8 * i + 8] for i in range(total.shape[0] // 8)]
    return sum(pieces[1:], pieces[0])


def dot_of(first, second):
    return fold([a * b for a, b in zip(first, second, strict=True)])


def weight_of(table, entry, layer):
    return 0.5 * table[entry[layer]]


def packed_ends(coeff):
    rows, cols = coeff.shape[1:]
    lane = lane_of((8, LANES))
    low = high = jnp.zeros((8, LANES), jnp.float32)
    for layer in range(2):
        for group in range(rows // 8):
            at = layer * (rows // 8) + group
            part = slice(8 * group, 8 * group + 8)
            first, last = coeff[layer, part, 0:LANES], coeff[layer, part, cols - LANES : cols]
            value = jnp.where(lane == 0, first, last)
            value = pltpu.roll(value, at, 1) if at else value
            low = jnp.where(lane == at, value, low)
            high = jnp.where(lane == (at - 1) % LANES, value, high)
    return low, pltpu.roll(high, 1, 1)


def own_kernel(
    grid_shape, field, coeff, across, shifts, table, entry, out, odd_side, even_side, across_out,
    coeff_pad, pad,
):
    rows, cols = field.shape[1:]
    zero_rim(pad, REACH, rows)
    fill_own(pad, REACH, field)
    low, high = packed_edges(lambda layer, edge: field[layer, :, edge], cols)
    store_packed(even_side, odd_side, 0, low, high)
    if across is None:
        zero_rim(coeff_pad, 8, rows)
        fill_own(coeff_pad, 8, coeff)
        store_packed(even_side, odd_side, rows, *packed_ends(coeff))
    for layer in range(2):
        weight = weight_of(table, entry, layer)
        for row in range(0, rows, OWN_CHUNK):
            result = apply_chunk(
                layer, row, pad, coeff_pad, across, across_out, shifts, weight, grid_shape, (rows, cols)
            )
            for tile, value in enumerate(result):
                out[layer, row : row + OWN_CHUNK, tile * LANES : (tile + 1) * LANES] = value


def products_of(own, result, base, fit):
    if base is None:
        pairs = ((own, own), (own, result), (result, result))
    else:
        rest = [a - fit * b for a, b in zip(base, own, strict=True)]
        slope = [a - fit * b for a, b in zip(own, result, strict=True)]
        pairs = (
            (rest, rest), (rest, own), (slope, rest), (result, rest), (slope, own), (result, own),
        )
    return tuple(dot_of(*pair) for pair in pairs)


def fit_of(sums):
    gamma, delta, omega = (jnp.sum(sums[index], keepdims=True) for index in range(3))
    fit = jnp.where(omega > 0.0, delta / jnp.where(omega > 0.0, omega, 1.0), 0.0)
    return gamma, delta, omega, jnp.clip(fit, -1.0, 1.0)


def rows_kernel(
    grid_shape, field, coeff, even_rows, odd_rows, even_edge, odd_edge, even_cols, odd_cols, even_ends,
    odd_ends, base, sums, shifts, table, entry, out, products, side_pad, pad,
):
    rows, cols = field.shape[1:]
    tiles = cols // LANES
    odd_y = is_odd("gy")
    first_row = lax.axis_index("gy") * rows
    first_col = lax.axis_index("gx") * cols
    zeros = jnp.zeros((REACH, LANES), jnp.float32)
    for layer in range(2):
        for tile in range(tiles):
            lanes = slice(tile * LANES, (tile + 1) * LANES)
            even = even_rows[layer, 0:REACH, lanes]
            other = odd_rows[layer, 0:REACH, lanes]
            pad[layer, 0, tile, 0:REACH, :] = jnp.where(odd_y, even, other)
            pad[layer, 0, tile, REACH:, :] = zeros
            pad[layer, 1, tile, 0:REACH, :] = zeros
            pad[layer, 1, tile, REACH:, :] = jnp.where(odd_y, other, even)
    lane = lane_of((CHUNK, LANES))
    row_at = lax.broadcasted_iota(jnp.int32, (CHUNK, LANES), 0)
    for layer in range(2):
        other_layer = 1 - layer

        def step(i, carry, layer=layer, other_layer=other_layer):
            part = pl.multiple_of(i * CHUNK, CHUNK)
            totals = [[jnp.zeros((CHUNK, LANES), jnp.float32)] * tiles for _ in range(2)]
            for direction in range(shifts.shape[2]):
                shift_r, shift_c = shifts[layer, 0, direction], shifts[layer, 1, direction]
                step_r = shifts[other_layer, 0, direction] - shift_r
                side = jnp.where(step_r < 0, 0, 1)
                start_r = part + step_r + jnp.where(step_r < 0, REACH, 0)
                row = part + jnp.where(step_r < 0, 0, rows - REACH)
                source = [
                    pad[other_layer, side, tile, pl.ds(start_r, CHUNK), :] for tile in range(tiles)
                ]
                moved = move_across(source, shifts[other_layer, 1, direction] - shift_c, lane)
                image_row = row_at + (first_row + row - shift_r)
                inside = (image_row >= 0) & (image_row < grid_shape[0])
                upper = inside & (jnp.full((CHUNK, LANES), side, jnp.int32) == 0)
                lower = inside & (jnp.full((CHUNK, LANES), side, jnp.int32) == 1)
                for tile in range(tiles):
                    value = moved[tile]
                    if tile == 0:
                        value = jnp.where(lane >= shift_c - first_col, value, 0.0)
                    if tile == tiles - 1:
                        last = grid_shape[1] + shift_c - first_col - tile * LANES
                        value = jnp.where(lane < last, value, 0.0)
                    totals[0][tile] = totals[0][tile] + jnp.where(upper, value, 0.0)
                    totals[1][tile] = totals[1][tile] + jnp.where(lower, value, 0.0)
            for side, base in enumerate((0, rows - REACH)):
                for tile in range(tiles):
                    lanes = slice(tile * LANES, (tile + 1) * LANES)
                    out[layer, pl.ds(base + part, CHUNK), lanes] += totals[side][tile]
            return carry

        lax.fori_loop(0, REACH // CHUNK, step, 0, unroll=True)
        weight = weight_of(table, entry, layer)
        at = lax.broadcasted_iota(jnp.int32, (8, cols), 0)
        even = even_edge[layer, REACH : REACH + 8, :]
        other = odd_edge[layer, REACH : REACH + 8, :]
        even_v = [even_rows[layer, start : start + 8, :] for start in (0, REACH - 8)]
        other_v = [odd_rows[layer, start : start + 8, :] for start in (0, REACH - 8)]
        for start, edge_c, edge_v, spot, source in (
            (0, jnp.where(odd_y, even, other), jnp.where(odd_y, even_v[1], other_v[1]), 0, 1),
            (
                rows - 8, jnp.where(odd_y, other, even), jnp.where(odd_y, other_v[0], even_v[0]),
                7, 7,
            ),
        ):
            edge_c = pltpu.roll(edge_c, source, 0)
            edge_v = pltpu.roll(edge_v, source, 0)
            value = field[layer, start : start + 8, :]
            own_c = coeff[layer, start : start + 8, :]
            extra = weight * (edge_c * value - (own_c + edge_c) * edge_v)
            out[layer, start : start + 8, :] += jnp.where(at == spot, extra, 0.0)
    fit = None if base is None else fit_of(sums)[3]
    carry = (jnp.zeros((8, LANES), jnp.float32),) * products.shape[0]
    inner = [slice(tile * LANES, (tile + 1) * LANES) for tile in range(1, tiles - 1)]
    for layer in range(2):

        def add(i, carry, layer=layer):
            chunk = pl.ds(pl.multiple_of(i * CHUNK, CHUNK), CHUNK)
            start, own, result = (
                None if ref is None else [ref[layer, chunk, lanes] for lanes in inner]
                for ref in (base, field, out)
            )
            more = products_of(own, result, start, fit)
            return tuple(a + b for a, b in zip(carry, more, strict=True))

        carry = lax.fori_loop(0, rows // CHUNK, add, carry, unroll=UNROLL)
    fill_sides(side_pad, even_cols, odd_cols, 0, REACH, rows)
    carry = finish(
        range(REACH // CHUNK, (rows - REACH) // CHUNK), carry, grid_shape, base, fit, field, coeff,
        even_ends, odd_ends, shifts, table, entry, out, side_pad,
    )
    for index, value in enumerate(carry):
        products[index] = value


def finish_chunk(grid_shape, layer, row, field, coeff, out, pad, ends, shifts, weight):
    rows, cols = field.shape[1:]
    tiles = cols // LANES
    first_row = lax.axis_index("gy") * rows + row
    first_col = lax.axis_index("gx") * cols
    lane = lane_of((CHUNK, LANES))
    row_at = lax.broadcasted_iota(jnp.int32, (CHUNK, LANES), 0)
    cut = (slice(0, LANES), slice(cols - LANES, cols))
    own = [field[layer, pl.ds(row, CHUNK), lanes] for lanes in cut]
    result = []
    for side, spot in ((0, 0), (1, LANES - 1)):
        at = layer * (rows // 8) + row // 8
        edge_c = jnp.concatenate(
            [
                pltpu.roll(ends[side], (spot - at - i) % LANES, 1)
                for i in range(CHUNK // 8)
            ]
        )
        edge_v = pad[layer, side, pl.ds(REACH + row, CHUNK), :]
        edge_v = pltpu.roll(edge_v, LANES - 1 if side else 1, 1)
        own_c = coeff[layer, pl.ds(row, CHUNK), cut[side]]
        extra = weight * ((own_c + edge_c) * (own[side] - edge_v))
        extra = jnp.where(lane == spot, extra, 0.0)
        result.append(out[layer, pl.ds(row, CHUNK), cut[side]] + extra)
    for direction in range(shifts.shape[2]):
        shift_r, shift_c = shifts[layer, 0, direction], shifts[layer, 1, direction]
        start_r = REACH + row + shifts[1 - layer, 0, direction] - shift_r
        step_c = shifts[1 - layer, 1, direction] - shift_c
        side = jnp.where(step_c < 0, 0, 1)
        back = jnp.bitwise_and(LANES - step_c, LANES - 1)
        moved = pltpu.roll(pad[1 - layer, side, pl.ds(start_r, CHUNK), :], back, 1)
        if near_end(row, CHUNK, rows):
            image_row = row_at + (first_row - shift_r)
            moved = jnp.where((image_row >= 0) & (image_row < grid_shape[0]), moved, 0.0)
        low, low_end = shift_c - first_col, jnp.where(step_c < 0, -step_c, 0)
        high = jnp.where(step_c < 0, LANES, LANES - step_c)
        high_end = grid_shape[1] + shift_c - first_col - (tiles - 1) * LANES
        result[0] = result[0] + jnp.where((lane >= low) & (lane < low_end), moved, 0.0)
        result[1] = result[1] + jnp.where((lane >= high) & (lane < high_end), moved, 0.0)
    for side in range(2):
        out[layer, pl.ds(row, CHUNK), cut[side]] = result[side]
    return own, result


def fill_sides(pad, even_ref, odd_ref, start, place, depth):
    odd_x = is_odd("gx")
    even, other = even_ref[start : start + depth, :], odd_ref[start : start + depth, :]
    for side, packed in ((0, jnp.where(odd_x, even, other)), (1, jnp.where(odd_x, other, even))):
        pad[0, side, place : place + depth, :] = packed
        pad[1, side, place : place + depth, :] = pltpu.roll(packed, HALF, 1)


def finish(
    chunks, carry, grid_shape, base, fit, field, coeff, even_ends, odd_ends, shifts, table, entry, out,
    pad,
):
    rows, cols = field.shape[1:]
    odd_x = is_odd("gx")
    even, other = even_ends[rows : rows + 8, :], odd_ends[rows : rows + 8, :]
    ends = (jnp.where(odd_x, even, other), jnp.where(odd_x, other, even))
    cut = (slice(0, LANES), slice(cols - LANES, cols))
    for layer in range(2):
        weight = weight_of(table, entry, layer)
        for row in (chunk * CHUNK for chunk in chunks):
            own, result = finish_chunk(
                grid_shape, layer, row, field, coeff, out, pad, ends, shifts, weight
            )
            start = None if base is None else [base[layer, row : row + CHUNK, x] for x in cut]
            more = products_of(own, result, start, fit)
            carry = tuple(a + b for a, b in zip(carry, more, strict=True))
    return carry


def finish_ends(grid_shape, even_corners, odd_corners, products, pad, field, *rest):
    rows = field.shape[1]
    fill_sides(pad, even_corners, odd_corners, 0, 0, REACH)
    fill_sides(pad, even_corners, odd_corners, REACH, REACH + rows, REACH)
    depth = REACH // CHUNK
    chunks = [*range(depth), *range(rows // CHUNK - depth, rows // CHUNK)]
    carry = tuple(products[index] for index in range(products.shape[0]))
    base, fit, *others = rest
    return finish(chunks, carry, grid_shape, base, fit, field, *others, pad)


def first_kernel(
    grid_shape, before, pad_before, field, coeff, even_ends, odd_ends, even_corners, odd_corners,
    products, shifts, table, entry, out, pad, sums, even_out, odd_out,
):
    del before, pad_before
    rows = field.shape[1]
    carry = finish_ends(
        grid_shape, even_corners, odd_corners, products, pad, field, None, None, coeff, even_ends,
        odd_ends, shifts, table, entry, out,
    )
    for index, value in enumerate(carry):
        sums[index] = value
    odd_y = is_odd("gy")
    low, high = out[:, 0:REACH, :], out[:, rows - REACH :, :]
    even_out[...] = jnp.where(odd_y, low, high)
    odd_out[...] = jnp.where(odd_y, high, low)


def second_kernel(
    grid_shape, before, pad_before, base, field, coeff, even_ends, odd_ends, even_corners, odd_corners,
    products, sums, shifts, table, entry, out, pad, parts,
):
    del before, pad_before
    gamma, delta, omega, fit = fit_of(sums)
    carry = finish_ends(
        grid_shape, even_corners, odd_corners, products, pad, field, base, fit, coeff, even_ends,
        odd_ends, shifts, table, entry, out,
    )
    rest2, rest_w, slope_rest, n_rest, slope_w, n_w = (
        jnp.sum(value, keepdims=True) for value in carry
    )
    lane = lane_of((8, LANES))
    row = jnp.zeros((8, LANES), jnp.float32)
    for at, value in (
        (0, rest2), (1, slope_rest), (8, 2.0 * rest_w), (9, n_rest + slope_w),
        (16, omega), (17, n_w), (24, fit), (25, fit), (32, gamma), (33, delta),
    ):
        row = jnp.where(lane == at, value, row)
    for start in range(0, parts.shape[0], 8):
        parts[start : start + 8, :] = row


def pick(row, lane, at):
    return jnp.sum(jnp.where(lane == at, row, 0.0), keepdims=True)


def last_kernel(
    parts, base, w_vec, n_vec, solution_out, residual_out, solution_part, residual_part, sems
):
    gathered = parts[...]
    count = gathered.shape[0]
    lane = lane_of((8, LANES))
    total = sum(gathered[8 * i : 8 * i + 8] for i in range(count // 8))
    gamma, delta = pick(total, lane, 32), pick(total, lane, 33)
    alpha = gamma / delta
    gap = alpha - pltpu.roll(gathered, LANES - 24, 1)
    moved = gathered - gap * pltpu.roll(gathered, LANES - 8, 1)
    moved = moved + gap * gap * pltpu.roll(gathered, LANES - 16, 1)
    total = sum(moved[8 * i : 8 * i + 8] for i in range(count // 8))
    gamma_next, delta_next = pick(total, lane, 0), pick(total, lane, 1)
    beta = gamma_next / gamma
    alpha_next = gamma_next / (delta_next - beta * gamma_next / alpha)
    layers, rows = base.shape[:2]
    depth = rows // PIECES
    copies = []
    for layer in range(layers):
        for piece in range(PIECES):
            part = pl.ds(piece * depth, depth)
            start, w_start = base[layer, part, :], w_vec[layer, part, :]
            residual = start - alpha * w_start
            w_next = w_start - alpha * n_vec[layer, part, :]
            solution_part[layer, part, :] = alpha * start + alpha_next * (residual + beta * start)
            residual_part[layer, part, :] = residual - alpha_next * (w_next + beta * w_start)
            for which, (source, target) in enumerate(
                ((solution_part, solution_out), (residual_part, residual_out))
            ):
                copy = pltpu.make_async_copy(
                    source.at[layer, part, :],
                    target.at[layer, part, :],
                    sems.at[which, layer, piece],
                )
                copy.start()
                copies.append(copy)
    for copy in copies:
        copy.wait()


def on_tensor_core(kernel, name, operands, scalars, out_shape, scratch, microseconds, in_place=0):
    return pl.pallas_call(
        kernel,
        out_shape=out_shape,
        in_specs=[VMEM_SPEC] * len(operands) + [SMEM_SPEC] * len(scalars),
        out_specs=(VMEM_SPEC,) * len(out_shape),
        scratch_shapes=[pltpu.VMEM(shape, jnp.float32) for shape in scratch],
        input_output_aliases={index: index for index in range(in_place)},
        compiler_params=pltpu.CompilerParams(vmem_limit_bytes=VMEM_BYTES),
        cost_estimate=pl.CostEstimate(
            flops=0, bytes_accessed=3_000_000 * microseconds, transcendentals=0
        ),
        name=name,
    )(*operands, *scalars)


def on_device(right_side, coefficient, strength_table, layer_entry, shifts):
    layers, rows, cols = right_side.shape
    count_y, count_x = lax.axis_size("gy"), lax.axis_size("gx")
    devices = count_x * count_y
    tiles = cols // LANES
    grid_shape = (rows * count_y, cols * count_x)
    full = jax.ShapeDtypeStruct((layers, rows, cols), jnp.float32)
    edge = jax.ShapeDtypeStruct((layers, REACH, cols), jnp.float32)
    scalars = (jnp.transpose(shifts, (1, 2, 0)), strength_table, layer_entry)
    own_pads = [(2, tiles, rows + 2 * REACH, LANES)]
    coeff_room = jax.ShapeDtypeStruct((2, tiles, rows + 16, LANES), jnp.float32)
    row_pads = [(2, 2, tiles, 2 * REACH, LANES)]
    side_pad = jax.ShapeDtypeStruct((2, 2, rows + 2 * REACH, LANES), jnp.float32)

    def side_of(count):
        return jax.ShapeDtypeStruct((count, LANES), jnp.float32)

    def sums_of(count):
        return jax.ShapeDtypeStruct((count, 8, LANES), jnp.float32)

    def bind(kernel):
        def bound(*refs):
            kernel(grid_shape, *refs)

        return bound

    def rows_first(before, packed, field, coeff, even, odd, even_cols, odd_cols, *refs):
        del before, packed
        rows_kernel(
            grid_shape, field, coeff, even, odd, even, odd, even_cols, odd_cols, even_cols, odd_cols,
            None, None, *refs,
        )

    def rows_second(before, packed, *refs):
        del before, packed
        rows_kernel(grid_shape, *refs)

    def own_first(field, coeff, *refs):
        own_kernel(grid_shape, field, coeff, None, *refs)

    def own_second(field, coeff_pad, across, shifts, table, entry, out, odd, even, pad):
        own_kernel(
            grid_shape, field, None, across, shifts, table, entry, out, odd, even, None, coeff_pad, pad
        )

    rows0 = swap(*edge_rows(right_side, coefficient), "gy")
    w_own, *columns, across, coeff_pad = on_tensor_core(
        own_first, "own_first", (right_side, coefficient), scalars,
        (full, side_of(rows + 8), side_of(rows + 8), full, coeff_room), own_pads, 6,
    )
    cols0 = swap(*columns[::-1], "gx")
    packed = pack_corners(*rows0)
    corners0 = swap(*packed, "gx")
    w_rows, products, sides = on_tensor_core(
        rows_first, "rows_first", (w_own, packed[1], right_side, coefficient, *rows0, *cols0), scalars,
        (full, sums_of(3), side_pad), row_pads, 3, 1,
    )
    w_vec, _, sums, even, odd = on_tensor_core(
        bind(first_kernel), "first_apply",
        (w_rows, sides, right_side, coefficient, *cols0, *corners0, products), scalars,
        (full, side_pad, sums_of(3), edge, edge), [], 3, 2,
    )
    rows1 = swap(even, odd, "gy")
    n_own, *columns = on_tensor_core(
        own_second, "own_second", (w_vec, coeff_pad, across), scalars,
        (full, side_of(rows), side_of(rows)), own_pads, 6,
    )
    cols1 = swap(*columns[::-1], "gx")
    packed = pack_corners(*rows1)
    corners1 = swap(*packed, "gx")
    n_rows, products, sides = on_tensor_core(
        rows_second, "rows_second",
        (n_own, packed[1], w_vec, coefficient, *rows1, *rows0, *cols1, *cols0, right_side, sums),
        scalars, (full, sums_of(6), side_pad), row_pads, 3, 1,
    )
    n_vec, _, parts = on_tensor_core(
        bind(second_kernel), "second_apply",
        (n_rows, sides, right_side, w_vec, coefficient, *cols0, *corners1, products, sums), scalars,
        (full, side_pad, jax.ShapeDtypeStruct((devices, LANES), jnp.float32)), [], 3, 2,
    )
    gathered = lax.all_to_all(parts, ("gx", "gy"), 0, 0, tiled=True)
    return pl.pallas_call(
        last_kernel,
        out_shape=(full, full),
        in_specs=[VMEM_SPEC] * 4,
        out_specs=(pl.BlockSpec(memory_space=pltpu.HBM),) * 2,
        scratch_shapes=[
            pltpu.VMEM((layers, rows, cols), jnp.float32),
            pltpu.VMEM((layers, rows, cols), jnp.float32),
            pltpu.SemaphoreType.DMA((2, layers, PIECES)),
        ],
        compiler_params=pltpu.CompilerParams(vmem_limit_bytes=VMEM_BYTES),
        name="last_update",
    )(gathered, right_side, w_vec, n_vec)


def solution(mesh):
    placed = (P(None, "gy", "gx"), P(None, "gy", "gx"), P(), P(), P())
    return jax.shard_map(
        on_device,
        mesh=mesh,
        in_specs=placed,
        out_specs=(P(None, "gy", "gx"), P(None, "gy", "gx")),
        check_vma=False,
    )
```

```python
import functools

import jax
import jax.numpy as jnp
from jax import lax
from jax.experimental import pallas as pl
from jax.experimental.pallas import tpu as pltpu
from jax.sharding import PartitionSpec as P

SMAX = 32
REACH = 2 * SMAX
LANES = 128
HALF = 64
CHUNK = 32
OWN_CHUNK = 64
UNROLL = 8
PIECES = 8
VMEM_BYTES = 32 * 1024 * 1024
EDGE_BYTES = 53 * 1024 * 1024
VMEM_SPEC = pl.BlockSpec(memory_space=pltpu.VMEM)
SMEM_SPEC = pl.BlockSpec(memory_space=pltpu.SMEM)


def pairs_from(start, count):
    low = range(start, count - 1, 2)
    return [(i, i + 1) for i in low] + [(i + 1, i) for i in low]


FIRST = {"gy": 1, "gx": 0}


def is_odd(axis):
    return lax.rem(lax.axis_index(axis) + FIRST[axis], 2) == 1


def swap(even, odd, axis):
    count = lax.axis_size(axis)
    return (
        lax.ppermute(even, axis, pairs_from(FIRST[axis], count)),
        lax.ppermute(odd, axis, pairs_from(1 - FIRST[axis], count)),
    )


def lane_of(shape):
    return lax.broadcasted_iota(jnp.int32, shape, 1)


def pack_columns(first, second, high):
    low_lanes = lane_of(first.shape) < HALF
    turned = pltpu.roll(second, HALF, 1)
    if high:
        return jnp.where(low_lanes, turned, first)
    return jnp.where(low_lanes, first, turned)


def packed_edges(load, cols):
    edges = (slice(0, LANES), slice(cols - LANES, cols))
    return [pack_columns(load(0, edge), load(1, edge), high) for high, edge in enumerate(edges)]


def store_packed(even_ref, odd_ref, start, low, high):
    odd = is_odd("gx")
    rows = low.shape[0]
    even_ref[start : start + rows, :] = jnp.where(odd, low, high)
    odd_ref[start : start + rows, :] = jnp.where(odd, high, low)


def pack_corners_kernel(even_rows, odd_rows, even_out, odd_out):
    cols = even_rows.shape[2]
    odd_y = is_odd("gy")
    for start, above in ((0, True), (REACH, False)):

        def halo(layer, edge, above=above):
            even = even_rows[layer, 0:REACH, edge]
            other = odd_rows[layer, 0:REACH, edge]
            return jnp.where(odd_y == above, even, other)

        store_packed(even_out, odd_out, start, *packed_edges(halo, cols))


def pack(kernel, operands, rows, name):
    out = jax.ShapeDtypeStruct((rows, LANES), jnp.float32)
    return pl.pallas_call(
        kernel,
        out_shape=(out, out),
        in_specs=[VMEM_SPEC] * len(operands),
        out_specs=(VMEM_SPEC,) * 2,
        compiler_params=pltpu.CompilerParams(vmem_limit_bytes=VMEM_BYTES),
        name=name,
    )(*operands)


def pack_corners(even_rows, odd_rows):
    return pack(pack_corners_kernel, (even_rows, odd_rows), 2 * REACH, "pack_corners")


def edge_kernel(field, coeff, even_out, odd_out, sems):
    rows = field.shape[1]
    odd_y = is_odd("gy")
    copies = []
    for index, (out, at_top) in enumerate(((even_out, odd_y), (odd_out, jnp.logical_not(odd_y)))):
        for part, (source, place, depth) in enumerate(((field, 0, REACH), (coeff, REACH, 8))):
            start = pl.multiple_of(jnp.where(at_top, 0, rows - depth), 8)
            copies.append(
                pltpu.make_async_copy(
                    source.at[:, pl.ds(start, depth), :],
                    out.at[:, pl.ds(place, depth), :],
                    sems.at[index, part],
                )
            )
    for copy in copies:
        copy.start()
    for copy in copies:
        copy.wait()


def edge_rows(field, coeff):
    layers, _, cols = field.shape
    out = jax.ShapeDtypeStruct((layers, REACH + 8, cols), jnp.float32)
    return pl.pallas_call(
        edge_kernel,
        out_shape=(out, out),
        in_specs=[pl.BlockSpec(memory_space=pltpu.HBM)] * 2,
        out_specs=(VMEM_SPEC,) * 2,
        scratch_shapes=[pltpu.SemaphoreType.DMA((2, 2))],
        compiler_params=pltpu.CompilerParams(vmem_limit_bytes=EDGE_BYTES),
        name="edge_rows",
    )(field, coeff)


def zero_rim(pad, depth, rows):
    zeros = jnp.zeros((depth, LANES), jnp.float32)
    for layer in range(2):
        for tile in range(pad.shape[1]):
            pad[layer, tile, 0:depth, :] = zeros
            pad[layer, tile, depth + rows :, :] = zeros


def fill_own(pad, depth, field):
    rows, cols = field.shape[1:]
    for layer in range(2):
        for tile in range(cols // LANES):
            lanes = slice(tile * LANES, (tile + 1) * LANES)
            pad[layer, tile, depth : depth + rows, :] = field[layer, :, lanes]


def move_across(tiles, step_c, lane):
    count = len(tiles)
    back = jnp.bitwise_and(LANES - step_c, LANES - 1)
    from_left = lane < jnp.where(step_c < 0, -step_c, 0)
    from_right = lane >= jnp.where(step_c < 0, LANES, LANES - step_c)
    turned = [0.0] + [pltpu.roll(tile, back, 1) for tile in tiles] + [0.0]
    return [
        jnp.where(from_left, turned[i], jnp.where(from_right, turned[i + 2], turned[i + 1]))
        for i in range(count)
    ]


def from_the_right(tiles, lane, last):
    ahead = [pltpu.roll(tile, LANES - 1, 1) for tile in tiles]
    return [
        jnp.where(lane == LANES - 1, after, tile)
        for tile, after in zip(ahead, [*ahead[1:], last], strict=True)
    ]


def near_end(row, depth, rows):
    return row < SMAX or row + depth > rows - SMAX


def apply_chunk(
    layer, row, pad, coeff_pad, across, across_out, shifts, weight, grid_shape, tile_shape
):
    rows, cols = tile_shape
    tiles = cols // LANES
    other = 1 - layer
    lane = lane_of((OWN_CHUNK, LANES))
    row_at = lax.broadcasted_iota(jnp.int32, (OWN_CHUNK, LANES), 0)
    first_row = lax.axis_index("gy") * rows + row
    first_col = lax.axis_index("gx") * cols
    cut = [slice(tile * LANES, (tile + 1) * LANES) for tile in range(tiles)]

    def at(ref, tile, start):
        return ref[layer, tile, pl.ds(start, OWN_CHUNK), :]

    own = [at(pad, tile, REACH + row) for tile in range(tiles)]
    own_c = [at(coeff_pad, tile, 8 + row) for tile in range(tiles)]
    if across is None:
        right_c = from_the_right(own_c, lane, 0.0)
        both = [a + b for a, b in zip(own_c, right_c, strict=True)]
        for value, lanes in zip(both, cut, strict=True):
            across_out[layer, pl.ds(row, OWN_CHUNK), lanes] = value
    else:
        both = [across[layer, pl.ds(row, OWN_CHUNK), lanes] for lanes in cut]
    right = from_the_right(own, lane, own[-1])
    flow = [c * (a - b) for c, a, b in zip(both, own, right, strict=True)]
    turned = [pltpu.roll(value, 1, 1) for value in flow]
    result = []
    for tile in range(tiles):
        value, coeff = own[tile], own_c[tile]
        above, below = at(pad, tile, REACH - 1 + row), at(pad, tile, REACH + 1 + row)
        above_c, below_c = at(coeff_pad, tile, 7 + row), at(coeff_pad, tile, 9 + row)
        total = (coeff + above_c) * (value - above) + (coeff + below_c) * (value - below)
        inflow = jnp.where(lane == 0, turned[tile - 1] if tile else 0.0, turned[tile])
        result.append(weight * (total + flow[tile] - inflow))
    for direction in range(shifts.shape[2]):
        shift_r, shift_c = shifts[layer, 0, direction], shifts[layer, 1, direction]
        start_r = REACH + row + shifts[other, 0, direction] - shift_r
        source = [pad[other, tile, pl.ds(start_r, OWN_CHUNK), :] for tile in range(tiles)]
        moved = move_across(source, shifts[other, 1, direction] - shift_c, lane)
        masks = [[] for _ in range(tiles)]
        masks[0].append(lane >= shift_c - first_col)
        masks[-1].append(lane < grid_shape[1] + shift_c - first_col - (tiles - 1) * LANES)
        if near_end(row, OWN_CHUNK, rows):
            image_row = row_at + (first_row - shift_r)
            inside = (image_row >= 0) & (image_row < grid_shape[0])
            for mask in masks:
                mask.append(inside)
        for tile in range(tiles):
            value = own[tile] + moved[tile]
            if masks[tile]:
                value = jnp.where(functools.reduce(jnp.logical_and, masks[tile]), value, 0.0)
            result[tile] = result[tile] + value
    return result


def fold(parts):
    total = sum(parts[1:], parts[0])
    pieces = [total[8 * i : 8 * i + 8] for i in range(total.shape[0] // 8)]
    return sum(pieces[1:], pieces[0])


def dot_of(first, second):
    return fold([a * b for a, b in zip(first, second, strict=True)])


def weight_of(table, entry, layer):
    return 0.5 * table[entry[layer]]


def packed_ends(coeff):
    ends = []
    rows, cols = coeff.shape[1:]
    lane = lane_of((8, LANES))
    for high, edge in enumerate((slice(0, LANES), slice(cols - LANES, cols))):
        packed = jnp.zeros((8, LANES), jnp.float32)
        for layer in range(2):
            for group in range(rows // 8):
                at = layer * (rows // 8) + group
                turn = (at + high) % LANES
                value = coeff[layer, 8 * group : 8 * group + 8, edge]
                value = pltpu.roll(value, turn, 1) if turn else value
                packed = jnp.where(lane == at, value, packed)
        ends.append(packed)
    return ends


def own_kernel(
    grid_shape, field, coeff, across, shifts, table, entry, out, even_side, odd_side, across_out,
    coeff_pad, pad,
):
    rows, cols = field.shape[1:]
    zero_rim(pad, REACH, rows)
    fill_own(pad, REACH, field)
    low, high = packed_edges(lambda layer, edge: field[layer, :, edge], cols)
    store_packed(even_side, odd_side, 0, low, high)
    if across is None:
        zero_rim(coeff_pad, 8, rows)
        fill_own(coeff_pad, 8, coeff)
        store_packed(even_side, odd_side, rows, *packed_ends(coeff))
    for layer in range(2):
        weight = weight_of(table, entry, layer)
        for row in range(0, rows, OWN_CHUNK):
            result = apply_chunk(
                layer, row, pad, coeff_pad, across, across_out, shifts, weight, grid_shape, (rows, cols)
            )
            for tile, value in enumerate(result):
                out[layer, row : row + OWN_CHUNK, tile * LANES : (tile + 1) * LANES] = value


def products_of(own, result, base, fit):
    if base is None:
        pairs = ((own, own), (own, result), (result, result))
    else:
        rest = [a - fit * b for a, b in zip(base, own, strict=True)]
        slope = [a - fit * b for a, b in zip(own, result, strict=True)]
        pairs = (
            (rest, rest), (rest, own), (slope, rest), (result, rest), (slope, own), (result, own),
        )
    return tuple(dot_of(*pair) for pair in pairs)


def fit_of(sums):
    gamma, delta, omega = (jnp.sum(sums[index], keepdims=True) for index in range(3))
    fit = jnp.where(omega > 0.0, delta / jnp.where(omega > 0.0, omega, 1.0), 0.0)
    return gamma, delta, omega, jnp.clip(fit, -1.0, 1.0)


def rows_kernel(
    grid_shape, field, coeff, even_rows, odd_rows, even_edge, odd_edge, even_cols, odd_cols, even_ends,
    odd_ends, base, sums, shifts, table, entry, out, products, side_pad, pad,
):
    rows, cols = field.shape[1:]
    tiles = cols // LANES
    odd_y = is_odd("gy")
    first_row = lax.axis_index("gy") * rows
    first_col = lax.axis_index("gx") * cols
    zeros = jnp.zeros((REACH, LANES), jnp.float32)
    for layer in range(2):
        for tile in range(tiles):
            lanes = slice(tile * LANES, (tile + 1) * LANES)
            even = even_rows[layer, 0:REACH, lanes]
            other = odd_rows[layer, 0:REACH, lanes]
            pad[layer, 0, tile, 0:REACH, :] = jnp.where(odd_y, even, other)
            pad[layer, 0, tile, REACH:, :] = zeros
            pad[layer, 1, tile, 0:REACH, :] = zeros
            pad[layer, 1, tile, REACH:, :] = jnp.where(odd_y, other, even)
    lane = lane_of((CHUNK, LANES))
    row_at = lax.broadcasted_iota(jnp.int32, (CHUNK, LANES), 0)
    for layer in range(2):
        other_layer = 1 - layer

        def step(i, carry, layer=layer, other_layer=other_layer):
            part = pl.multiple_of(i * CHUNK, CHUNK)
            totals = [[jnp.zeros((CHUNK, LANES), jnp.float32)] * tiles for _ in range(2)]
            for direction in range(shifts.shape[2]):
                shift_r, shift_c = shifts[layer, 0, direction], shifts[layer, 1, direction]
                step_r = shifts[other_layer, 0, direction] - shift_r
                side = jnp.where(step_r < 0, 0, 1)
                start_r = part + step_r + jnp.where(step_r < 0, REACH, 0)
                row = part + jnp.where(step_r < 0, 0, rows - REACH)
                source = [
                    pad[other_layer, side, tile, pl.ds(start_r, CHUNK), :] for tile in range(tiles)
                ]
                moved = move_across(source, shifts[other_layer, 1, direction] - shift_c, lane)
                image_row = row_at + (first_row + row - shift_r)
                inside = (image_row >= 0) & (image_row < grid_shape[0])
                upper = inside & (jnp.full((CHUNK, LANES), side, jnp.int32) == 0)
                lower = inside & (jnp.full((CHUNK, LANES), side, jnp.int32) == 1)
                for tile in range(tiles):
                    value = moved[tile]
                    if tile == 0:
                        value = jnp.where(lane >= shift_c - first_col, value, 0.0)
                    if tile == tiles - 1:
                        last = grid_shape[1] + shift_c - first_col - tile * LANES
                        value = jnp.where(lane < last, value, 0.0)
                    totals[0][tile] = totals[0][tile] + jnp.where(upper, value, 0.0)
                    totals[1][tile] = totals[1][tile] + jnp.where(lower, value, 0.0)
            for side, base in enumerate((0, rows - REACH)):
                for tile in range(tiles):
                    lanes = slice(tile * LANES, (tile + 1) * LANES)
                    out[layer, pl.ds(base + part, CHUNK), lanes] += totals[side][tile]
            return carry

        lax.fori_loop(0, REACH // CHUNK, step, 0, unroll=True)
        weight = weight_of(table, entry, layer)
        at = lax.broadcasted_iota(jnp.int32, (8, cols), 0)
        even = even_edge[layer, REACH : REACH + 8, :]
        other = odd_edge[layer, REACH : REACH + 8, :]
        even_v = [even_rows[layer, start : start + 8, :] for start in (0, REACH - 8)]
        other_v = [odd_rows[layer, start : start + 8, :] for start in (0, REACH - 8)]
        for start, edge_c, edge_v, spot, source in (
            (0, jnp.where(odd_y, even, other), jnp.where(odd_y, even_v[1], other_v[1]), 0, 1),
            (
                rows - 8, jnp.where(odd_y, other, even), jnp.where(odd_y, other_v[0], even_v[0]),
                7, 7,
            ),
        ):
            edge_c = pltpu.roll(edge_c, source, 0)
            edge_v = pltpu.roll(edge_v, source, 0)
            value = field[layer, start : start + 8, :]
            own_c = coeff[layer, start : start + 8, :]
            extra = weight * (edge_c * value - (own_c + edge_c) * edge_v)
            out[layer, start : start + 8, :] += jnp.where(at == spot, extra, 0.0)
    fit = None if base is None else fit_of(sums)[3]
    carry = (jnp.zeros((8, LANES), jnp.float32),) * products.shape[0]
    inner = [slice(tile * LANES, (tile + 1) * LANES) for tile in range(1, tiles - 1)]
    for layer in range(2):

        def add(i, carry, layer=layer):
            chunk = pl.ds(pl.multiple_of(i * CHUNK, CHUNK), CHUNK)
            start, own, result = (
                None if ref is None else [ref[layer, chunk, lanes] for lanes in inner]
                for ref in (base, field, out)
            )
            more = products_of(own, result, start, fit)
            return tuple(a + b for a, b in zip(carry, more, strict=True))

        carry = lax.fori_loop(0, rows // CHUNK, add, carry, unroll=UNROLL)
    fill_sides(side_pad, even_cols, odd_cols, 0, REACH, rows)
    carry = finish(
        range(REACH // CHUNK, (rows - REACH) // CHUNK), carry, grid_shape, base, fit, field, coeff,
        even_ends, odd_ends, shifts, table, entry, out, side_pad,
    )
    for index, value in enumerate(carry):
        products[index] = value


def finish_chunk(grid_shape, layer, row, field, coeff, out, pad, ends, shifts, weight):
    rows, cols = field.shape[1:]
    tiles = cols // LANES
    first_row = lax.axis_index("gy") * rows + row
    first_col = lax.axis_index("gx") * cols
    lane = lane_of((CHUNK, LANES))
    row_at = lax.broadcasted_iota(jnp.int32, (CHUNK, LANES), 0)
    cut = (slice(0, LANES), slice(cols - LANES, cols))
    own = [field[layer, pl.ds(row, CHUNK), lanes] for lanes in cut]
    result = []
    for side, spot in ((0, 0), (1, LANES - 1)):
        at = layer * (rows // 8) + row // 8
        edge_c = jnp.concatenate(
            [
                pltpu.roll(ends[side], (spot - at - i) % LANES, 1)
                for i in range(CHUNK // 8)
            ]
        )
        edge_v = pad[layer, side, pl.ds(REACH + row, CHUNK), :]
        edge_v = pltpu.roll(edge_v, LANES - 1 if side else 1, 1)
        own_c = coeff[layer, pl.ds(row, CHUNK), cut[side]]
        extra = weight * ((own_c + edge_c) * (own[side] - edge_v))
        extra = jnp.where(lane == spot, extra, 0.0)
        result.append(out[layer, pl.ds(row, CHUNK), cut[side]] + extra)
    for direction in range(shifts.shape[2]):
        shift_r, shift_c = shifts[layer, 0, direction], shifts[layer, 1, direction]
        start_r = REACH + row + shifts[1 - layer, 0, direction] - shift_r
        step_c = shifts[1 - layer, 1, direction] - shift_c
        side = jnp.where(step_c < 0, 0, 1)
        back = jnp.bitwise_and(LANES - step_c, LANES - 1)
        moved = pltpu.roll(pad[1 - layer, side, pl.ds(start_r, CHUNK), :], back, 1)
        if near_end(row, CHUNK, rows):
            image_row = row_at + (first_row - shift_r)
            moved = jnp.where((image_row >= 0) & (image_row < grid_shape[0]), moved, 0.0)
        low, low_end = shift_c - first_col, jnp.where(step_c < 0, -step_c, 0)
        high = jnp.where(step_c < 0, LANES, LANES - step_c)
        high_end = grid_shape[1] + shift_c - first_col - (tiles - 1) * LANES
        result[0] = result[0] + jnp.where((lane >= low) & (lane < low_end), moved, 0.0)
        result[1] = result[1] + jnp.where((lane >= high) & (lane < high_end), moved, 0.0)
    for side in range(2):
        out[layer, pl.ds(row, CHUNK), cut[side]] = result[side]
    return own, result


def fill_sides(pad, even_ref, odd_ref, start, place, depth):
    odd_x = is_odd("gx")
    even, other = even_ref[start : start + depth, :], odd_ref[start : start + depth, :]
    for side, packed in ((0, jnp.where(odd_x, even, other)), (1, jnp.where(odd_x, other, even))):
        pad[0, side, place : place + depth, :] = packed
        pad[1, side, place : place + depth, :] = pltpu.roll(packed, HALF, 1)


def finish(
    chunks, carry, grid_shape, base, fit, field, coeff, even_ends, odd_ends, shifts, table, entry, out,
    pad,
):
    rows, cols = field.shape[1:]
    odd_x = is_odd("gx")
    even, other = even_ends[rows : rows + 8, :], odd_ends[rows : rows + 8, :]
    ends = (jnp.where(odd_x, even, other), jnp.where(odd_x, other, even))
    cut = (slice(0, LANES), slice(cols - LANES, cols))
    for layer in range(2):
        weight = weight_of(table, entry, layer)
        for row in (chunk * CHUNK for chunk in chunks):
            own, result = finish_chunk(
                grid_shape, layer, row, field, coeff, out, pad, ends, shifts, weight
            )
            start = None if base is None else [base[layer, row : row + CHUNK, x] for x in cut]
            more = products_of(own, result, start, fit)
            carry = tuple(a + b for a, b in zip(carry, more, strict=True))
    return carry


def finish_ends(grid_shape, even_corners, odd_corners, products, pad, field, *rest):
    rows = field.shape[1]
    fill_sides(pad, even_corners, odd_corners, 0, 0, REACH)
    fill_sides(pad, even_corners, odd_corners, REACH, REACH + rows, REACH)
    depth = REACH // CHUNK
    chunks = [*range(depth), *range(rows // CHUNK - depth, rows // CHUNK)]
    carry = tuple(products[index] for index in range(products.shape[0]))
    base, fit, *others = rest
    return finish(chunks, carry, grid_shape, base, fit, field, *others, pad)


def first_kernel(
    grid_shape, before, pad_before, field, coeff, even_ends, odd_ends, even_corners, odd_corners,
    products, shifts, table, entry, out, pad, sums, even_out, odd_out,
):
    del before, pad_before
    rows = field.shape[1]
    carry = finish_ends(
        grid_shape, even_corners, odd_corners, products, pad, field, None, None, coeff, even_ends,
        odd_ends, shifts, table, entry, out,
    )
    for index, value in enumerate(carry):
        sums[index] = value
    odd_y = is_odd("gy")
    low, high = out[:, 0:REACH, :], out[:, rows - REACH :, :]
    even_out[...] = jnp.where(odd_y, low, high)
    odd_out[...] = jnp.where(odd_y, high, low)


def second_kernel(
    grid_shape, before, pad_before, base, field, coeff, even_ends, odd_ends, even_corners, odd_corners,
    products, sums, shifts, table, entry, out, pad, parts,
):
    del before, pad_before
    gamma, delta, omega, fit = fit_of(sums)
    carry = finish_ends(
        grid_shape, even_corners, odd_corners, products, pad, field, base, fit, coeff, even_ends,
        odd_ends, shifts, table, entry, out,
    )
    rest2, rest_w, slope_rest, n_rest, slope_w, n_w = (
        jnp.sum(value, keepdims=True) for value in carry
    )
    lane = lane_of((8, LANES))
    row = jnp.zeros((8, LANES), jnp.float32)
    for at, value in (
        (0, rest2), (1, slope_rest), (8, 2.0 * rest_w), (9, n_rest + slope_w),
        (16, omega), (17, n_w), (24, fit), (25, fit), (32, gamma), (33, delta),
    ):
        row = jnp.where(lane == at, value, row)
    for start in range(0, parts.shape[0], 8):
        parts[start : start + 8, :] = row


def pick(row, lane, at):
    return jnp.sum(jnp.where(lane == at, row, 0.0), keepdims=True)


def last_kernel(
    parts, base, w_vec, n_vec, solution_out, residual_out, solution_part, residual_part, sems
):
    gathered = parts[...]
    count = gathered.shape[0]
    lane = lane_of((8, LANES))
    total = sum(gathered[8 * i : 8 * i + 8] for i in range(count // 8))
    gamma, delta = pick(total, lane, 32), pick(total, lane, 33)
    alpha = gamma / delta
    gap = alpha - pltpu.roll(gathered, LANES - 24, 1)
    moved = gathered - gap * pltpu.roll(gathered, LANES - 8, 1)
    moved = moved + gap * gap * pltpu.roll(gathered, LANES - 16, 1)
    total = sum(moved[8 * i : 8 * i + 8] for i in range(count // 8))
    gamma_next, delta_next = pick(total, lane, 0), pick(total, lane, 1)
    beta = gamma_next / gamma
    alpha_next = gamma_next / (delta_next - beta * gamma_next / alpha)
    layers, rows = base.shape[:2]
    depth = rows // PIECES
    copies = []
    for layer in range(layers):
        for piece in range(PIECES):
            part = pl.ds(piece * depth, depth)
            start, w_start = base[layer, part, :], w_vec[layer, part, :]
            residual = start - alpha * w_start
            w_next = w_start - alpha * n_vec[layer, part, :]
            solution_part[layer, part, :] = alpha * start + alpha_next * (residual + beta * start)
            residual_part[layer, part, :] = residual - alpha_next * (w_next + beta * w_start)
            for which, (source, target) in enumerate(
                ((solution_part, solution_out), (residual_part, residual_out))
            ):
                copy = pltpu.make_async_copy(
                    source.at[layer, part, :],
                    target.at[layer, part, :],
                    sems.at[which, layer, piece],
                )
                copy.start()
                copies.append(copy)
    for copy in copies:
        copy.wait()


def on_tensor_core(kernel, name, operands, scalars, out_shape, scratch, microseconds, in_place=0):
    return pl.pallas_call(
        kernel,
        out_shape=out_shape,
        in_specs=[VMEM_SPEC] * len(operands) + [SMEM_SPEC] * len(scalars),
        out_specs=(VMEM_SPEC,) * len(out_shape),
        scratch_shapes=[pltpu.VMEM(shape, jnp.float32) for shape in scratch],
        input_output_aliases={index: index for index in range(in_place)},
        compiler_params=pltpu.CompilerParams(vmem_limit_bytes=VMEM_BYTES),
        cost_estimate=pl.CostEstimate(
            flops=0, bytes_accessed=3_000_000 * microseconds, transcendentals=0
        ),
        name=name,
    )(*operands, *scalars)


def on_device(right_side, coefficient, strength_table, layer_entry, shifts):
    layers, rows, cols = right_side.shape
    count_y, count_x = lax.axis_size("gy"), lax.axis_size("gx")
    devices = count_x * count_y
    tiles = cols // LANES
    grid_shape = (rows * count_y, cols * count_x)
    full = jax.ShapeDtypeStruct((layers, rows, cols), jnp.float32)
    edge = jax.ShapeDtypeStruct((layers, REACH, cols), jnp.float32)
    scalars = (jnp.transpose(shifts, (1, 2, 0)), strength_table, layer_entry)
    own_pads = [(2, tiles, rows + 2 * REACH, LANES)]
    coeff_room = jax.ShapeDtypeStruct((2, tiles, rows + 16, LANES), jnp.float32)
    row_pads = [(2, 2, tiles, 2 * REACH, LANES)]
    side_pad = jax.ShapeDtypeStruct((2, 2, rows + 2 * REACH, LANES), jnp.float32)

    def side_of(count):
        return jax.ShapeDtypeStruct((count, LANES), jnp.float32)

    def sums_of(count):
        return jax.ShapeDtypeStruct((count, 8, LANES), jnp.float32)

    def bind(kernel):
        def bound(*refs):
            kernel(grid_shape, *refs)

        return bound

    def rows_first(before, packed, field, coeff, even, odd, even_cols, odd_cols, *refs):
        del before, packed
        rows_kernel(
            grid_shape, field, coeff, even, odd, even, odd, even_cols, odd_cols, even_cols, odd_cols,
            None, None, *refs,
        )

    def rows_second(before, packed, *refs):
        del before, packed
        rows_kernel(grid_shape, *refs)

    def own_first(field, coeff, *refs):
        own_kernel(grid_shape, field, coeff, None, *refs)

    def own_second(field, coeff_pad, across, shifts, table, entry, out, even, odd, pad):
        own_kernel(
            grid_shape, field, None, across, shifts, table, entry, out, even, odd, None, coeff_pad, pad
        )

    rows0 = swap(*edge_rows(right_side, coefficient), "gy")
    w_own, *columns, across, coeff_pad = on_tensor_core(
        own_first, "own_first", (right_side, coefficient), scalars,
        (full, side_of(rows + 8), side_of(rows + 8), full, coeff_room), own_pads, 6,
    )
    cols0 = swap(*columns, "gx")
    packed = pack_corners(*rows0)
    corners0 = swap(*packed, "gx")
    w_rows, products, sides = on_tensor_core(
        rows_first, "rows_first", (w_own, packed[0], right_side, coefficient, *rows0, *cols0), scalars,
        (full, sums_of(3), side_pad), row_pads, 3, 1,
    )
    w_vec, _, sums, even, odd = on_tensor_core(
        bind(first_kernel), "first_apply",
        (w_rows, sides, right_side, coefficient, *cols0, *corners0, products), scalars,
        (full, side_pad, sums_of(3), edge, edge), [], 3, 2,
    )
    rows1 = swap(even, odd, "gy")
    n_own, *columns = on_tensor_core(
        own_second, "own_second", (w_vec, coeff_pad, across), scalars,
        (full, side_of(rows), side_of(rows)), own_pads, 6,
    )
    cols1 = swap(*columns, "gx")
    packed = pack_corners(*rows1)
    corners1 = swap(*packed, "gx")
    n_rows, products, sides = on_tensor_core(
        rows_second, "rows_second",
        (n_own, packed[0], w_vec, coefficient, *rows1, *rows0, *cols1, *cols0, right_side, sums),
        scalars, (full, sums_of(6), side_pad), row_pads, 3, 1,
    )
    n_vec, _, parts = on_tensor_core(
        bind(second_kernel), "second_apply",
        (n_rows, sides, right_side, w_vec, coefficient, *cols0, *corners1, products, sums), scalars,
        (full, side_pad, jax.ShapeDtypeStruct((devices, LANES), jnp.float32)), [], 3, 2,
    )
    gathered = lax.all_to_all(parts, ("gx", "gy"), 0, 0, tiled=True)
    return pl.pallas_call(
        last_kernel,
        out_shape=(full, full),
        in_specs=[VMEM_SPEC] * 4,
        out_specs=(pl.BlockSpec(memory_space=pltpu.HBM),) * 2,
        scratch_shapes=[
            pltpu.VMEM((layers, rows, cols), jnp.float32),
            pltpu.VMEM((layers, rows, cols), jnp.float32),
            pltpu.SemaphoreType.DMA((2, layers, PIECES)),
        ],
        compiler_params=pltpu.CompilerParams(vmem_limit_bytes=VMEM_BYTES),
        name="last_update",
    )(gathered, right_side, w_vec, n_vec)


def solution(mesh):
    placed = (P(None, "gy", "gx"), P(None, "gy", "gx"), P(), P(), P())
    return jax.shard_map(
        on_device,
        mesh=mesh,
        in_specs=placed,
        out_specs=(P(None, "gy", "gx"), P(None, "gy", "gx")),
        check_vma=False,
    )
```

```python
import functools

import jax
import jax.numpy as jnp
from jax import lax
from jax.experimental import pallas as pl
from jax.experimental.pallas import tpu as pltpu
from jax.sharding import PartitionSpec as P

SMAX = 32
REACH = 2 * SMAX
LANES = 128
HALF = 64
CHUNK = 32
OWN_CHUNK = 64
UNROLL = 8
PIECES = 2
VMEM_BYTES = 32 * 1024 * 1024
EDGE_BYTES = 53 * 1024 * 1024
VMEM_SPEC = pl.BlockSpec(memory_space=pltpu.VMEM)
SMEM_SPEC = pl.BlockSpec(memory_space=pltpu.SMEM)


def pairs_from(start, count):
    low = range(start, count - 1, 2)
    return [(i, i + 1) for i in low] + [(i + 1, i) for i in low]


FIRST = {"gy": 1, "gx": 0}


def is_odd(axis):
    return lax.rem(lax.axis_index(axis) + FIRST[axis], 2) == 1


def swap(even, odd, axis):
    count = lax.axis_size(axis)
    return (
        lax.ppermute(even, axis, pairs_from(FIRST[axis], count)),
        lax.ppermute(odd, axis, pairs_from(1 - FIRST[axis], count)),
    )


def lane_of(shape):
    return lax.broadcasted_iota(jnp.int32, shape, 1)


def pack_columns(first, second, high):
    low_lanes = lane_of(first.shape) < HALF
    turned = pltpu.roll(second, HALF, 1)
    if high:
        return jnp.where(low_lanes, turned, first)
    return jnp.where(low_lanes, first, turned)


def packed_edges(load, cols):
    edges = (slice(0, LANES), slice(cols - LANES, cols))
    return [pack_columns(load(0, edge), load(1, edge), high) for high, edge in enumerate(edges)]


def store_packed(even_ref, odd_ref, start, low, high):
    odd = is_odd("gx")
    rows = low.shape[0]
    even_ref[start : start + rows, :] = jnp.where(odd, low, high)
    odd_ref[start : start + rows, :] = jnp.where(odd, high, low)


def pack_corners_kernel(even_rows, odd_rows, even_out, odd_out):
    cols = even_rows.shape[2]
    odd_y = is_odd("gy")
    for start, above in ((0, True), (REACH, False)):

        def halo(layer, edge, above=above):
            even = even_rows[layer, 0:REACH, edge]
            other = odd_rows[layer, 0:REACH, edge]
            return jnp.where(odd_y == above, even, other)

        store_packed(even_out, odd_out, start, *packed_edges(halo, cols))


def pack(kernel, operands, rows, name):
    out = jax.ShapeDtypeStruct((rows, LANES), jnp.float32)
    return pl.pallas_call(
        kernel,
        out_shape=(out, out),
        in_specs=[VMEM_SPEC] * len(operands),
        out_specs=(VMEM_SPEC,) * 2,
        compiler_params=pltpu.CompilerParams(vmem_limit_bytes=VMEM_BYTES),
        name=name,
    )(*operands)


def pack_corners(even_rows, odd_rows):
    return pack(pack_corners_kernel, (even_rows, odd_rows), 2 * REACH, "pack_corners")


def edge_kernel(field, coeff, even_out, odd_out, sems):
    rows = field.shape[1]
    odd_y = is_odd("gy")
    copies = []
    for index, (out, at_top) in enumerate(((even_out, odd_y), (odd_out, jnp.logical_not(odd_y)))):
        for part, (source, place, depth) in enumerate(((field, 0, REACH), (coeff, REACH, 8))):
            start = pl.multiple_of(jnp.where(at_top, 0, rows - depth), 8)
            copies.append(
                pltpu.make_async_copy(
                    source.at[:, pl.ds(start, depth), :],
                    out.at[:, pl.ds(place, depth), :],
                    sems.at[index, part],
                )
            )
    for copy in copies:
        copy.start()
    for copy in copies:
        copy.wait()


def edge_rows(field, coeff):
    layers, _, cols = field.shape
    out = jax.ShapeDtypeStruct((layers, REACH + 8, cols), jnp.float32)
    return pl.pallas_call(
        edge_kernel,
        out_shape=(out, out),
        in_specs=[pl.BlockSpec(memory_space=pltpu.HBM)] * 2,
        out_specs=(VMEM_SPEC,) * 2,
        scratch_shapes=[pltpu.SemaphoreType.DMA((2, 2))],
        compiler_params=pltpu.CompilerParams(vmem_limit_bytes=EDGE_BYTES),
        name="edge_rows",
    )(field, coeff)


def zero_rim(pad, depth, rows):
    zeros = jnp.zeros((depth, LANES), jnp.float32)
    for layer in range(2):
        for tile in range(pad.shape[1]):
            pad[layer, tile, 0:depth, :] = zeros
            pad[layer, tile, depth + rows :, :] = zeros


def fill_own(pad, depth, field):
    rows, cols = field.shape[1:]
    for layer in range(2):
        for tile in range(cols // LANES):
            lanes = slice(tile * LANES, (tile + 1) * LANES)
            pad[layer, tile, depth : depth + rows, :] = field[layer, :, lanes]


def move_across(tiles, step_c, lane):
    count = len(tiles)
    back = jnp.bitwise_and(LANES - step_c, LANES - 1)
    from_left = lane < jnp.where(step_c < 0, -step_c, 0)
    from_right = lane >= jnp.where(step_c < 0, LANES, LANES - step_c)
    turned = [0.0] + [pltpu.roll(tile, back, 1) for tile in tiles] + [0.0]
    return [
        jnp.where(from_left, turned[i], jnp.where(from_right, turned[i + 2], turned[i + 1]))
        for i in range(count)
    ]


def from_the_right(tiles, lane, last):
    ahead = [pltpu.roll(tile, LANES - 1, 1) for tile in tiles]
    return [
        jnp.where(lane == LANES - 1, after, tile)
        for tile, after in zip(ahead, [*ahead[1:], last], strict=True)
    ]


def near_end(row, depth, rows):
    return row < SMAX or row + depth > rows - SMAX


def apply_chunk(
    layer, row, pad, coeff_pad, across, across_out, shifts, weight, grid_shape, tile_shape
):
    rows, cols = tile_shape
    tiles = cols // LANES
    other = 1 - layer
    lane = lane_of((OWN_CHUNK, LANES))
    row_at = lax.broadcasted_iota(jnp.int32, (OWN_CHUNK, LANES), 0)
    first_row = lax.axis_index("gy") * rows + row
    first_col = lax.axis_index("gx") * cols
    cut = [slice(tile * LANES, (tile + 1) * LANES) for tile in range(tiles)]

    def at(ref, tile, start):
        return ref[layer, tile, pl.ds(start, OWN_CHUNK), :]

    own = [at(pad, tile, REACH + row) for tile in range(tiles)]
    own_c = [at(coeff_pad, tile, 8 + row) for tile in range(tiles)]
    if across is None:
        right_c = from_the_right(own_c, lane, 0.0)
        both = [a + b for a, b in zip(own_c, right_c, strict=True)]
        for value, lanes in zip(both, cut, strict=True):
            across_out[layer, pl.ds(row, OWN_CHUNK), lanes] = value
    else:
        both = [across[layer, pl.ds(row, OWN_CHUNK), lanes] for lanes in cut]
    right = from_the_right(own, lane, own[-1])
    flow = [c * (a - b) for c, a, b in zip(both, own, right, strict=True)]
    turned = [pltpu.roll(value, 1, 1) for value in flow]
    result = []
    for tile in range(tiles):
        value, coeff = own[tile], own_c[tile]
        above, below = at(pad, tile, REACH - 1 + row), at(pad, tile, REACH + 1 + row)
        above_c, below_c = at(coeff_pad, tile, 7 + row), at(coeff_pad, tile, 9 + row)
        total = (coeff + above_c) * (value - above) + (coeff + below_c) * (value - below)
        inflow = jnp.where(lane == 0, turned[tile - 1] if tile else 0.0, turned[tile])
        result.append(weight * (total + flow[tile] - inflow))
    for direction in range(shifts.shape[2]):
        shift_r, shift_c = shifts[layer, 0, direction], shifts[layer, 1, direction]
        start_r = REACH + row + shifts[other, 0, direction] - shift_r
        source = [pad[other, tile, pl.ds(start_r, OWN_CHUNK), :] for tile in range(tiles)]
        moved = move_across(source, shifts[other, 1, direction] - shift_c, lane)
        masks = [[] for _ in range(tiles)]
        masks[0].append(lane >= shift_c - first_col)
        masks[-1].append(lane < grid_shape[1] + shift_c - first_col - (tiles - 1) * LANES)
        if near_end(row, OWN_CHUNK, rows):
            image_row = row_at + (first_row - shift_r)
            inside = (image_row >= 0) & (image_row < grid_shape[0])
            for mask in masks:
                mask.append(inside)
        for tile in range(tiles):
            value = own[tile] + moved[tile]
            if masks[tile]:
                value = jnp.where(functools.reduce(jnp.logical_and, masks[tile]), value, 0.0)
            result[tile] = result[tile] + value
    return result


def fold(parts):
    total = sum(parts[1:], parts[0])
    pieces = [total[8 * i : 8 * i + 8] for i in range(total.shape[0] // 8)]
    return sum(pieces[1:], pieces[0])


def dot_of(first, second):
    return fold([a * b for a, b in zip(first, second, strict=True)])


def weight_of(table, entry, layer):
    return 0.5 * table[entry[layer]]


def packed_ends(coeff):
    ends = []
    rows, cols = coeff.shape[1:]
    lane = lane_of((8, LANES))
    for high, edge in enumerate((slice(0, LANES), slice(cols - LANES, cols))):
        packed = jnp.zeros((8, LANES), jnp.float32)
        for layer in range(2):
            for group in range(rows // 8):
                at = layer * (rows // 8) + group
                turn = (at + high) % LANES
                value = coeff[layer, 8 * group : 8 * group + 8, edge]
                value = pltpu.roll(value, turn, 1) if turn else value
                packed = jnp.where(lane == at, value, packed)
        ends.append(packed)
    return ends


def own_kernel(
    grid_shape, field, coeff, across, shifts, table, entry, out, even_side, odd_side, across_out,
    coeff_pad, pad,
):
    rows, cols = field.shape[1:]
    zero_rim(pad, REACH, rows)
    fill_own(pad, REACH, field)
    low, high = packed_edges(lambda layer, edge: field[layer, :, edge], cols)
    store_packed(even_side, odd_side, 0, low, high)
    if across is None:
        zero_rim(coeff_pad, 8, rows)
        fill_own(coeff_pad, 8, coeff)
        store_packed(even_side, odd_side, rows, *packed_ends(coeff))
    for layer in range(2):
        weight = weight_of(table, entry, layer)
        for row in range(0, rows, OWN_CHUNK):
            result = apply_chunk(
                layer, row, pad, coeff_pad, across, across_out, shifts, weight, grid_shape, (rows, cols)
            )
            for tile, value in enumerate(result):
                out[layer, row : row + OWN_CHUNK, tile * LANES : (tile + 1) * LANES] = value


def products_of(own, result, base, fit):
    if base is None:
        pairs = ((own, own), (own, result), (result, result))
    else:
        rest = [a - fit * b for a, b in zip(base, own, strict=True)]
        slope = [a - fit * b for a, b in zip(own, result, strict=True)]
        pairs = (
            (rest, rest), (rest, own), (slope, rest), (result, rest), (slope, own), (result, own),
        )
    return tuple(dot_of(*pair) for pair in pairs)


def fit_of(sums):
    gamma, delta, omega = (jnp.sum(sums[index], keepdims=True) for index in range(3))
    fit = jnp.where(omega > 0.0, delta / jnp.where(omega > 0.0, omega, 1.0), 0.0)
    return gamma, delta, omega, jnp.clip(fit, -1.0, 1.0)


def rows_kernel(
    grid_shape, field, coeff, even_rows, odd_rows, even_edge, odd_edge, even_cols, odd_cols, even_ends,
    odd_ends, base, sums, shifts, table, entry, out, products, side_pad, pad,
):
    rows, cols = field.shape[1:]
    tiles = cols // LANES
    odd_y = is_odd("gy")
    first_row = lax.axis_index("gy") * rows
    first_col = lax.axis_index("gx") * cols
    zeros = jnp.zeros((REACH, LANES), jnp.float32)
    for layer in range(2):
        for tile in range(tiles):
            lanes = slice(tile * LANES, (tile + 1) * LANES)
            even = even_rows[layer, 0:REACH, lanes]
            other = odd_rows[layer, 0:REACH, lanes]
            pad[layer, 0, tile, 0:REACH, :] = jnp.where(odd_y, even, other)
            pad[layer, 0, tile, REACH:, :] = zeros
            pad[layer, 1, tile, 0:REACH, :] = zeros
            pad[layer, 1, tile, REACH:, :] = jnp.where(odd_y, other, even)
    lane = lane_of((CHUNK, LANES))
    row_at = lax.broadcasted_iota(jnp.int32, (CHUNK, LANES), 0)
    for layer in range(2):
        other_layer = 1 - layer

        def step(i, carry, layer=layer, other_layer=other_layer):
            part = pl.multiple_of(i * CHUNK, CHUNK)
            totals = [[jnp.zeros((CHUNK, LANES), jnp.float32)] * tiles for _ in range(2)]
            for direction in range(shifts.shape[2]):
                shift_r, shift_c = shifts[layer, 0, direction], shifts[layer, 1, direction]
                step_r = shifts[other_layer, 0, direction] - shift_r
                side = jnp.where(step_r < 0, 0, 1)
                start_r = part + step_r + jnp.where(step_r < 0, REACH, 0)
                row = part + jnp.where(step_r < 0, 0, rows - REACH)
                source = [
                    pad[other_layer, side, tile, pl.ds(start_r, CHUNK), :] for tile in range(tiles)
                ]
                moved = move_across(source, shifts[other_layer, 1, direction] - shift_c, lane)
                image_row = row_at + (first_row + row - shift_r)
                inside = (image_row >= 0) & (image_row < grid_shape[0])
                upper = inside & (jnp.full((CHUNK, LANES), side, jnp.int32) == 0)
                lower = inside & (jnp.full((CHUNK, LANES), side, jnp.int32) == 1)
                for tile in range(tiles):
                    value = moved[tile]
                    if tile == 0:
                        value = jnp.where(lane >= shift_c - first_col, value, 0.0)
                    if tile == tiles - 1:
                        last = grid_shape[1] + shift_c - first_col - tile * LANES
                        value = jnp.where(lane < last, value, 0.0)
                    totals[0][tile] = totals[0][tile] + jnp.where(upper, value, 0.0)
                    totals[1][tile] = totals[1][tile] + jnp.where(lower, value, 0.0)
            for side, base in enumerate((0, rows - REACH)):
                for tile in range(tiles):
                    lanes = slice(tile * LANES, (tile + 1) * LANES)
                    out[layer, pl.ds(base + part, CHUNK), lanes] += totals[side][tile]
            return carry

        lax.fori_loop(0, REACH // CHUNK, step, 0, unroll=True)
        weight = weight_of(table, entry, layer)
        at = lax.broadcasted_iota(jnp.int32, (8, cols), 0)
        even = even_edge[layer, REACH : REACH + 8, :]
        other = odd_edge[layer, REACH : REACH + 8, :]
        even_v = [even_rows[layer, start : start + 8, :] for start in (0, REACH - 8)]
        other_v = [odd_rows[layer, start : start + 8, :] for start in (0, REACH - 8)]
        for start, edge_c, edge_v, spot, source in (
            (0, jnp.where(odd_y, even, other), jnp.where(odd_y, even_v[1], other_v[1]), 0, 1),
            (
                rows - 8, jnp.where(odd_y, other, even), jnp.where(odd_y, other_v[0], even_v[0]),
                7, 7,
            ),
        ):
            edge_c = pltpu.roll(edge_c, source, 0)
            edge_v = pltpu.roll(edge_v, source, 0)
            value = field[layer, start : start + 8, :]
            own_c = coeff[layer, start : start + 8, :]
            extra = weight * (edge_c * value - (own_c + edge_c) * edge_v)
            out[layer, start : start + 8, :] += jnp.where(at == spot, extra, 0.0)
    fit = None if base is None else fit_of(sums)[3]
    carry = (jnp.zeros((8, LANES), jnp.float32),) * products.shape[0]
    inner = [slice(tile * LANES, (tile + 1) * LANES) for tile in range(1, tiles - 1)]
    for layer in range(2):

        def add(i, carry, layer=layer):
            chunk = pl.ds(pl.multiple_of(i * CHUNK, CHUNK), CHUNK)
            start, own, result = (
                None if ref is None else [ref[layer, chunk, lanes] for lanes in inner]
                for ref in (base, field, out)
            )
            more = products_of(own, result, start, fit)
            return tuple(a + b for a, b in zip(carry, more, strict=True))

        carry = lax.fori_loop(0, rows // CHUNK, add, carry, unroll=UNROLL)
    fill_sides(side_pad, even_cols, odd_cols, 0, REACH, rows)
    carry = finish(
        range(REACH // CHUNK, (rows - REACH) // CHUNK), carry, grid_shape, base, fit, field, coeff,
        even_ends, odd_ends, shifts, table, entry, out, side_pad,
    )
    for index, value in enumerate(carry):
        products[index] = value


def finish_chunk(grid_shape, layer, row, field, coeff, out, pad, ends, shifts, weight):
    rows, cols = field.shape[1:]
    tiles = cols // LANES
    first_row = lax.axis_index("gy") * rows + row
    first_col = lax.axis_index("gx") * cols
    lane = lane_of((CHUNK, LANES))
    row_at = lax.broadcasted_iota(jnp.int32, (CHUNK, LANES), 0)
    cut = (slice(0, LANES), slice(cols - LANES, cols))
    own = [field[layer, pl.ds(row, CHUNK), lanes] for lanes in cut]
    result = []
    for side, spot in ((0, 0), (1, LANES - 1)):
        at = layer * (rows // 8) + row // 8
        edge_c = jnp.concatenate(
            [
                pltpu.roll(ends[side], (spot - at - i) % LANES, 1)
                for i in range(CHUNK // 8)
            ]
        )
        edge_v = pad[layer, side, pl.ds(REACH + row, CHUNK), :]
        edge_v = pltpu.roll(edge_v, LANES - 1 if side else 1, 1)
        own_c = coeff[layer, pl.ds(row, CHUNK), cut[side]]
        extra = weight * ((own_c + edge_c) * (own[side] - edge_v))
        extra = jnp.where(lane == spot, extra, 0.0)
        result.append(out[layer, pl.ds(row, CHUNK), cut[side]] + extra)
    for direction in range(shifts.shape[2]):
        shift_r, shift_c = shifts[layer, 0, direction], shifts[layer, 1, direction]
        start_r = REACH + row + shifts[1 - layer, 0, direction] - shift_r
        step_c = shifts[1 - layer, 1, direction] - shift_c
        side = jnp.where(step_c < 0, 0, 1)
        back = jnp.bitwise_and(LANES - step_c, LANES - 1)
        moved = pltpu.roll(pad[1 - layer, side, pl.ds(start_r, CHUNK), :], back, 1)
        if near_end(row, CHUNK, rows):
            image_row = row_at + (first_row - shift_r)
            moved = jnp.where((image_row >= 0) & (image_row < grid_shape[0]), moved, 0.0)
        low, low_end = shift_c - first_col, jnp.where(step_c < 0, -step_c, 0)
        high = jnp.where(step_c < 0, LANES, LANES - step_c)
        high_end = grid_shape[1] + shift_c - first_col - (tiles - 1) * LANES
        result[0] = result[0] + jnp.where((lane >= low) & (lane < low_end), moved, 0.0)
        result[1] = result[1] + jnp.where((lane >= high) & (lane < high_end), moved, 0.0)
    for side in range(2):
        out[layer, pl.ds(row, CHUNK), cut[side]] = result[side]
    return own, result


def fill_sides(pad, even_ref, odd_ref, start, place, depth):
    odd_x = is_odd("gx")
    even, other = even_ref[start : start + depth, :], odd_ref[start : start + depth, :]
    for side, packed in ((0, jnp.where(odd_x, even, other)), (1, jnp.where(odd_x, other, even))):
        pad[0, side, place : place + depth, :] = packed
        pad[1, side, place : place + depth, :] = pltpu.roll(packed, HALF, 1)


def finish(
    chunks, carry, grid_shape, base, fit, field, coeff, even_ends, odd_ends, shifts, table, entry, out,
    pad,
):
    rows, cols = field.shape[1:]
    odd_x = is_odd("gx")
    even, other = even_ends[rows : rows + 8, :], odd_ends[rows : rows + 8, :]
    ends = (jnp.where(odd_x, even, other), jnp.where(odd_x, other, even))
    cut = (slice(0, LANES), slice(cols - LANES, cols))
    for layer in range(2):
        weight = weight_of(table, entry, layer)
        for row in (chunk * CHUNK for chunk in chunks):
            own, result = finish_chunk(
                grid_shape, layer, row, field, coeff, out, pad, ends, shifts, weight
            )
            start = None if base is None else [base[layer, row : row + CHUNK, x] for x in cut]
            more = products_of(own, result, start, fit)
            carry = tuple(a + b for a, b in zip(carry, more, strict=True))
    return carry


def finish_ends(grid_shape, even_corners, odd_corners, products, pad, field, *rest):
    rows = field.shape[1]
    fill_sides(pad, even_corners, odd_corners, 0, 0, REACH)
    fill_sides(pad, even_corners, odd_corners, REACH, REACH + rows, REACH)
    depth = REACH // CHUNK
    chunks = [*range(depth), *range(rows // CHUNK - depth, rows // CHUNK)]
    carry = tuple(products[index] for index in range(products.shape[0]))
    base, fit, *others = rest
    return finish(chunks, carry, grid_shape, base, fit, field, *others, pad)


def first_kernel(
    grid_shape, before, pad_before, field, coeff, even_ends, odd_ends, even_corners, odd_corners,
    products, shifts, table, entry, out, pad, sums, even_out, odd_out,
):
    del before, pad_before
    rows = field.shape[1]
    carry = finish_ends(
        grid_shape, even_corners, odd_corners, products, pad, field, None, None, coeff, even_ends,
        odd_ends, shifts, table, entry, out,
    )
    for index, value in enumerate(carry):
        sums[index] = value
    odd_y = is_odd("gy")
    low, high = out[:, 0:REACH, :], out[:, rows - REACH :, :]
    even_out[...] = jnp.where(odd_y, low, high)
    odd_out[...] = jnp.where(odd_y, high, low)


def second_kernel(
    grid_shape, before, pad_before, base, field, coeff, even_ends, odd_ends, even_corners, odd_corners,
    products, sums, shifts, table, entry, out, pad, parts,
):
    del before, pad_before
    gamma, delta, omega, fit = fit_of(sums)
    carry = finish_ends(
        grid_shape, even_corners, odd_corners, products, pad, field, base, fit, coeff, even_ends,
        odd_ends, shifts, table, entry, out,
    )
    rest2, rest_w, slope_rest, n_rest, slope_w, n_w = (
        jnp.sum(value, keepdims=True) for value in carry
    )
    lane = lane_of((8, LANES))
    row = jnp.zeros((8, LANES), jnp.float32)
    for at, value in (
        (0, rest2), (1, slope_rest), (8, 2.0 * rest_w), (9, n_rest + slope_w),
        (16, omega), (17, n_w), (24, fit), (25, fit), (32, gamma), (33, delta),
    ):
        row = jnp.where(lane == at, value, row)
    for start in range(0, parts.shape[0], 8):
        parts[start : start + 8, :] = row


def pick(row, lane, at):
    return jnp.sum(jnp.where(lane == at, row, 0.0), keepdims=True)


def last_kernel(
    parts, base, w_vec, n_vec, solution_out, residual_out, solution_part, residual_part, sems
):
    gathered = parts[...]
    count = gathered.shape[0]
    lane = lane_of((8, LANES))
    total = sum(gathered[8 * i : 8 * i + 8] for i in range(count // 8))
    gamma, delta = pick(total, lane, 32), pick(total, lane, 33)
    alpha = gamma / delta
    gap = alpha - pltpu.roll(gathered, LANES - 24, 1)
    moved = gathered - gap * pltpu.roll(gathered, LANES - 8, 1)
    moved = moved + gap * gap * pltpu.roll(gathered, LANES - 16, 1)
    total = sum(moved[8 * i : 8 * i + 8] for i in range(count // 8))
    gamma_next, delta_next = pick(total, lane, 0), pick(total, lane, 1)
    beta = gamma_next / gamma
    alpha_next = gamma_next / (delta_next - beta * gamma_next / alpha)
    layers, rows = base.shape[:2]
    depth = rows // PIECES
    copies = []
    for layer in range(layers):
        for piece in range(PIECES):
            part = pl.ds(piece * depth, depth)
            start, w_start = base[layer, part, :], w_vec[layer, part, :]
            residual = start - alpha * w_start
            w_next = w_start - alpha * n_vec[layer, part, :]
            solution_part[layer, part, :] = alpha * start + alpha_next * (residual + beta * start)
            residual_part[layer, part, :] = residual - alpha_next * (w_next + beta * w_start)
            for which, (source, target) in enumerate(
                ((solution_part, solution_out), (residual_part, residual_out))
            ):
                copy = pltpu.make_async_copy(
                    source.at[layer, part, :],
                    target.at[layer, part, :],
                    sems.at[which, layer, piece],
                )
                copy.start()
                copies.append(copy)
    for copy in copies:
        copy.wait()


def on_tensor_core(kernel, name, operands, scalars, out_shape, scratch, microseconds, in_place=0):
    return pl.pallas_call(
        kernel,
        out_shape=out_shape,
        in_specs=[VMEM_SPEC] * len(operands) + [SMEM_SPEC] * len(scalars),
        out_specs=(VMEM_SPEC,) * len(out_shape),
        scratch_shapes=[pltpu.VMEM(shape, jnp.float32) for shape in scratch],
        input_output_aliases={index: index for index in range(in_place)},
        compiler_params=pltpu.CompilerParams(vmem_limit_bytes=VMEM_BYTES),
        cost_estimate=pl.CostEstimate(
            flops=0, bytes_accessed=3_000_000 * microseconds, transcendentals=0
        ),
        name=name,
    )(*operands, *scalars)


def on_device(right_side, coefficient, strength_table, layer_entry, shifts):
    layers, rows, cols = right_side.shape
    count_y, count_x = lax.axis_size("gy"), lax.axis_size("gx")
    devices = count_x * count_y
    tiles = cols // LANES
    grid_shape = (rows * count_y, cols * count_x)
    full = jax.ShapeDtypeStruct((layers, rows, cols), jnp.float32)
    edge = jax.ShapeDtypeStruct((layers, REACH, cols), jnp.float32)
    scalars = (jnp.transpose(shifts, (1, 2, 0)), strength_table, layer_entry)
    own_pads = [(2, tiles, rows + 2 * REACH, LANES)]
    coeff_room = jax.ShapeDtypeStruct((2, tiles, rows + 16, LANES), jnp.float32)
    row_pads = [(2, 2, tiles, 2 * REACH, LANES)]
    side_pad = jax.ShapeDtypeStruct((2, 2, rows + 2 * REACH, LANES), jnp.float32)

    def side_of(count):
        return jax.ShapeDtypeStruct((count, LANES), jnp.float32)

    def sums_of(count):
        return jax.ShapeDtypeStruct((count, 8, LANES), jnp.float32)

    def bind(kernel):
        def bound(*refs):
            kernel(grid_shape, *refs)

        return bound

    def rows_first(before, packed, field, coeff, even, odd, even_cols, odd_cols, *refs):
        del before, packed
        rows_kernel(
            grid_shape, field, coeff, even, odd, even, odd, even_cols, odd_cols, even_cols, odd_cols,
            None, None, *refs,
        )

    def rows_second(before, packed, *refs):
        del before, packed
        rows_kernel(grid_shape, *refs)

    def own_first(field, coeff, *refs):
        own_kernel(grid_shape, field, coeff, None, *refs)

    def own_second(field, coeff_pad, across, shifts, table, entry, out, even, odd, pad):
        own_kernel(
            grid_shape, field, None, across, shifts, table, entry, out, even, odd, None, coeff_pad, pad
        )

    rows0 = swap(*edge_rows(right_side, coefficient), "gy")
    w_own, *columns, across, coeff_pad = on_tensor_core(
        own_first, "own_first", (right_side, coefficient), scalars,
        (full, side_of(rows + 8), side_of(rows + 8), full, coeff_room), own_pads, 6,
    )
    cols0 = swap(*columns, "gx")
    packed = pack_corners(*rows0)
    corners0 = swap(*packed, "gx")
    w_rows, products, sides = on_tensor_core(
        rows_first, "rows_first", (w_own, packed[0], right_side, coefficient, *rows0, *cols0), scalars,
        (full, sums_of(3), side_pad), row_pads, 3, 1,
    )
    w_vec, _, sums, even, odd = on_tensor_core(
        bind(first_kernel), "first_apply",
        (w_rows, sides, right_side, coefficient, *cols0, *corners0, products), scalars,
        (full, side_pad, sums_of(3), edge, edge), [], 3, 2,
    )
    rows1 = swap(even, odd, "gy")
    n_own, *columns = on_tensor_core(
        own_second, "own_second", (w_vec, coeff_pad, across), scalars,
        (full, side_of(rows), side_of(rows)), own_pads, 6,
    )
    cols1 = swap(*columns, "gx")
    packed = pack_corners(*rows1)
    corners1 = swap(*packed, "gx")
    n_rows, products, sides = on_tensor_core(
        rows_second, "rows_second",
        (n_own, packed[0], w_vec, coefficient, *rows1, *rows0, *cols1, *cols0, right_side, sums),
        scalars, (full, sums_of(6), side_pad), row_pads, 3, 1,
    )
    n_vec, _, parts = on_tensor_core(
        bind(second_kernel), "second_apply",
        (n_rows, sides, right_side, w_vec, coefficient, *cols0, *corners1, products, sums), scalars,
        (full, side_pad, jax.ShapeDtypeStruct((devices, LANES), jnp.float32)), [], 3, 2,
    )
    gathered = lax.all_to_all(parts, ("gx", "gy"), 0, 0, tiled=True)
    return pl.pallas_call(
        last_kernel,
        out_shape=(full, full),
        in_specs=[VMEM_SPEC] * 4,
        out_specs=(pl.BlockSpec(memory_space=pltpu.HBM),) * 2,
        scratch_shapes=[
            pltpu.VMEM((layers, rows, cols), jnp.float32),
            pltpu.VMEM((layers, rows, cols), jnp.float32),
            pltpu.SemaphoreType.DMA((2, layers, PIECES)),
        ],
        compiler_params=pltpu.CompilerParams(vmem_limit_bytes=VMEM_BYTES),
        name="last_update",
    )(gathered, right_side, w_vec, n_vec)


def solution(mesh):
    placed = (P(None, "gy", "gx"), P(None, "gy", "gx"), P(), P(), P())
    return jax.shard_map(
        on_device,
        mesh=mesh,
        in_specs=placed,
        out_specs=(P(None, "gy", "gx"), P(None, "gy", "gx")),
        check_vma=False,
    )
```
